32 devices in a mesh: wide: 8 (over z, core), narrow: 4 (over y, x).
Axes of the slice: x: 2, y: 2, z: 4, core: 2. Of those that a mesh axis runs over, the one named last changes fastest.
Arguments:
- tokens: bfloat16 [24576, 1152], P(('wide', 'narrow')), may hold values from -6 to 6
- condition: float32 [12, 1152], replicated, may hold values from -6 to 6
- frame_clip: int32 [96], P('wide'), may hold values from 0 to 11, never falling along the last dimension, each value on 1 to 16 neighbouring positions
- mod_weight: bfloat16 [1152, 6, 1152], P('wide', None, 'narrow'), may hold values from -0.1875 to 0.1875
- mod_bias: bfloat16 [6, 1152], P(None, 'narrow'), may hold values from -3 to 3
- project_weight: bfloat16 [1152, 3, 1152], P('wide', None, 'narrow'), may hold values from -0.1875 to 0.1875
- project_bias: bfloat16 [2, 1152], P(None, 'narrow'), may hold values from -3 to 3
- merge_weight: bfloat16 [1152, 1152], P('narrow', 'wide'), may hold values from -1 to 1
- merge_bias: bfloat16 [1152], P('narrow'), may hold values from -3 to 3
- up_weight: bfloat16 [1152, 4608], P('wide', 'narrow'), may hold values from -0.1875 to 0.1875
- up_bias: bfloat16 [4608], P('narrow'), may hold values from -3 to 3
- down_weight: bfloat16 [4608, 1152], P('narrow', 'wide'), may hold values from -0.1875 to 0.1875
- down_bias: bfloat16 [1152], P('narrow'), may hold values from -3 to 3
- out_cotangent: bfloat16 [24576, 1152], P(('wide', 'narrow')), may hold values from -6 to 6
Outputs:
- output: bfloat16 [24576, 1152], P(('wide', 'narrow'))
- tokens_grad: float32 [24576, 1152], P(('wide', 'narrow'))
- condition_grad: float32 [12, 1152], replicated
- mod_weight_grad: float32 [1152, 6, 1152], P('wide', None, 'narrow')
- mod_bias_grad: float32 [6, 1152], P(None, 'narrow')
- project_weight_grad: float32 [1152, 3, 1152], P('wide', None, 'narrow')
- project_bias_grad: float32 [2, 1152], P(None, 'narrow')
- merge_weight_grad: float32 [1152, 1152], P('narrow', 'wide')
- merge_bias_grad: float32 [1152], P('narrow')
- up_weight_grad: float32 [1152, 4608], P('wide', 'narrow')
- up_bias_grad: float32 [4608], P('narrow')
- down_weight_grad: float32 [4608, 1152], P('narrow', 'wide')
- down_bias_grad: float32 [1152], P('narrow')
The draws below stay inside these ranges and needn't reach their ends.
Inputs may be any that keep to these rules, and one draw needn't show every extreme that they name: frame_clip[f] is the clip of frame f; the numbers never fall along the frames, each clip holds 1 to 16 frames.
All inputs are finite; a program needn't handle non-finite values.
Results may differ from the reference program's by a relative error of at most 0.019.
Values may be sent and summed in bfloat16 or wider, within the bound.
No kernel may reach another device: no remote copies, remote signals or barrier semaphores. Data moves between devices by JAX's collectives and lax.ppermute only.
A program may use at most 256 MiB of HBM per device.

```python
import math
import jax
import jax.numpy as jnp
import numpy as np
from jax import lax

D = 1152
HEADS = 16
FF = 4608
PATCHES = 256
FRAMES = 96
TOKENS = 24576
CLIPS = 12
LONGEST = 16


def level_of(own_key, extent, cuts, least, largest):
    gain, own = 1.0, jax.random.fold_in(own_key, 6)
    for dim, blocks in cuts:
        heights = jnp.exp(jax.random.uniform(jax.random.fold_in(own, dim), (blocks,), jnp.float32, least / len(cuts), largest / len(cuts)))
        gain = gain * jnp.repeat(heights, extent[dim] // blocks).reshape([-1 if axis == dim else 1 for axis in range(len(extent))])
    return gain


def length_profile(count, total, reach, slope):
    loads = [(1 << 20) // math.isqrt(grade ** slope) + 1 for grade in range(2, count + 1)]
    rest, given = total - reach - (count - 1), [1] * (count - 1)
    while rest > 0:
        free = [i for i in range(count - 1) if given[i] < reach]
        mass, left = sum([loads[i] for i in free]), rest
        for i in free:
            extra = min(reach - given[i], max(1, left * loads[i] // mass), rest)
            given[i] = given[i] + extra
            rest = rest - extra
    return np.array([reach] + given)


def ragged(stream_key, count, total, limit, slope):
    if count == 2:
        one = jax.random.randint(stream_key, (), max(1, total - limit), min(limit, total - 1) + 1)
        return jnp.stack([one, total - one])
    tallies = jnp.asarray(length_profile(count, total, limit, slope), jnp.int32)
    pairs = (count - 1) // 2
    giver, taker = tallies[1:1 + 2 * pairs:2], tallies[2:2 + 2 * pairs:2]
    slack = jnp.minimum(giver - 1, limit - taker)
    passed = jax.random.randint(jax.random.fold_in(stream_key, 1), (pairs,), 0, 1 << 20) % (slack + 1)
    tallies = tallies.at[1:1 + 2 * pairs:2].set(giver - passed).at[2:2 + 2 * pairs:2].set(taker + passed)
    return tallies[jax.random.permutation(jax.random.fold_in(stream_key, 2), count)]


def scatter_about(key, dims, scale, bound, split=(), held_as=jnp.bfloat16):
    drawn = jax.random.normal(key, dims, jnp.float32) * scale
    if len(split) > 0:
        drawn = level_of(key, dims, split, -0.22, 0.18) * drawn
    return jnp.clip(drawn, min=-bound, max=bound).astype(held_as)


def setup_inputs(seed: int = 0) -> dict:
    streams_of = jax.random.split(jax.random.key(seed), 15)
    tokens = scatter_about(streams_of[0], (TOKENS, D), 1.0, 6.0, ((0, 32),))
    condition = scatter_about(streams_of[1], (CLIPS, D), 1.0, 6.0, (), jnp.float32)
    frame_clip = jnp.searchsorted(jnp.cumsum(ragged(streams_of[2], CLIPS, FRAMES, LONGEST, 0)), jnp.arange(FRAMES), side="right").astype(jnp.int32)
    mod_weight = scatter_about(streams_of[3], (D, 6, D), D ** -0.5, 0.1875, ((0, 8), (2, 4)))
    mod_bias = scatter_about(streams_of[4], (6, D), 0.5, 3.0, ((1, 4),))
    project_weight = scatter_about(streams_of[5], (D, 3, D), D ** -0.5, 0.1875, ((0, 8), (2, 4)))
    project_bias = scatter_about(streams_of[6], (2, D), 0.5, 3.0, ((1, 4),))
    merge_weight = scatter_about(streams_of[7], (D, D), (D // 32) ** -0.5, 1.0, ((0, 4), (1, 8)))
    merge_bias = scatter_about(streams_of[8], (D,), 0.5, 3.0, ((0, 4),))
    up_weight = scatter_about(streams_of[9], (D, FF), D ** -0.5, 0.1875, ((0, 8), (1, 4)))
    up_bias = scatter_about(streams_of[10], (FF,), 0.5, 3.0, ((0, 4),))
    down_weight = scatter_about(streams_of[11], (FF, D), (FF // 4) ** -0.5, 0.1875, ((0, 4), (1, 8)))
    down_bias = scatter_about(streams_of[12], (D,), 0.5, 3.0, ((0, 4),))
    out_cotangent = scatter_about(streams_of[13], (TOKENS, D), 1.0, 6.0, ((0, 32),))
    return {"tokens": tokens, "condition": condition, "frame_clip": frame_clip, "mod_weight": mod_weight, "mod_bias": mod_bias, "project_weight": project_weight, "project_bias": project_bias, "merge_weight": merge_weight, "merge_bias": merge_bias, "up_weight": up_weight, "up_bias": up_bias, "down_weight": down_weight, "down_bias": down_bias, "out_cotangent": out_cotangent}


@jax.custom_vjp
def low(v):
    return lax.optimization_barrier(v.astype(jnp.bfloat16)).astype(jnp.float32)

@jax.custom_vjp
def low_back(v):
    return v

def low_keep(v):
    return (low(v), None)

def low_pass(kept, grad):
    return (grad,)

def back_keep(v):
    return (v, None)

def back_low(kept, grad):
    return (low(grad),)
low.defvjp(low_keep, low_pass)
low_back.defvjp(back_keep, back_low)
epsilon = 1e-06
highest = lax.Precision.HIGHEST

def normalize(values_in):
    center = lax.optimization_barrier(jnp.mean(values_in, axis=-1, keepdims=True))
    spread = lax.optimization_barrier(jnp.mean(values_in * values_in, axis=-1, keepdims=True)) - center * center
    return (values_in - center) * lax.rsqrt(spread + epsilon)

def attend_frames(triple):
    query, keys, values = triple
    scale = query.shape[-1] ** (-0.5)
    scores = low_back(scale * jnp.einsum('fshe,fthe->fhst', query, keys, precision=highest))
    logsum = jax.nn.logsumexp(scores, axis=-1, keepdims=True)
    weights = low(jnp.exp(scores - logsum))
    return jnp.einsum('fhst,fthe->fshe', weights, values, precision=highest)

def forward(tokens, condition, frame_clip, mod_weight, mod_bias, project_weight, project_bias, merge_weight, merge_bias, up_weight, up_bias, down_weight, down_bias):
    active = low(jax.nn.silu(condition))
    modes = jnp.einsum('cd,dki->cki', active, mod_weight, precision=highest) + mod_bias[None]
    frame_mod = modes[frame_clip]

    def mod_at(column):
        return frame_mod[:, None, column, :]
    layout = tokens.reshape(FRAMES, PATCHES, D)
    hidden_a = low(normalize(layout) * (1.0 + mod_at(1)) + mod_at(0))
    project = jnp.einsum('fpd,dki->fpki', hidden_a, project_weight, precision=highest)
    query = low_back(low(project[:, :, 0] + project_bias[0]))
    keys = low_back(low(project[:, :, 1]))
    values = low_back(low(project[:, :, 2] + project_bias[1]))
    bundle = math.gcd(FRAMES, 16)
    shaped = (FRAMES // bundle, bundle, PATCHES, HEADS, D // HEADS)
    attended = lax.map(jax.checkpoint(attend_frames), (query.reshape(shaped), keys.reshape(shaped), values.reshape(shaped)))
    attended = low_back(low(attended.reshape(FRAMES, PATCHES, D)))
    branch_a = low_back(jnp.einsum('fpi,id->fpd', attended, merge_weight, precision=highest)) + merge_bias
    middle = layout + mod_at(2) * branch_a
    hidden_b = low(normalize(middle) * (1.0 + mod_at(4)) + mod_at(3))
    upper = low_back(jnp.einsum('fpd,dh->fph', hidden_b, up_weight, precision=highest) + up_bias)
    gelu_out = low(jax.nn.gelu(upper, approximate=True))
    branch_b = low_back(jnp.einsum('fph,hd->fpd', gelu_out, down_weight, precision=highest)) + down_bias
    return (middle + mod_at(5) * branch_b).reshape(TOKENS, D)

def reference(tokens, condition, frame_clip, mod_weight, mod_bias, project_weight, project_bias, merge_weight, merge_bias, up_weight, up_bias, down_weight, down_bias, out_cotangent):
    floats = [array.astype(jnp.float32) for array in (tokens, condition, mod_weight, mod_bias, project_weight, project_bias, merge_weight, merge_bias, up_weight, up_bias, down_weight, down_bias)]

    def wrapped(tokens_f, condition_f, mod_w, mod_b, project_w, project_b, merge_w, merge_b, up_w, up_b, down_w, down_b):
        return forward(tokens_f, condition_f, frame_clip, mod_w, mod_b, project_w, project_b, merge_w, merge_b, up_w, up_b, down_w, down_b)
    output, pullback = jax.vjp(wrapped, *floats)
    grads = pullback(out_cotangent.astype(jnp.float32))
    return (output.astype(jnp.bfloat16), grads[0], grads[1], grads[2], grads[3], grads[4], grads[5], grads[6], grads[7], grads[8], grads[9], grads[10], grads[11])
```

```python
import functools
import math

import jax
import jax.numpy as jnp
from jax import lax
from jax.experimental import pallas as pl
from jax.experimental.pallas import tpu as pltpu
from jax.sharding import PartitionSpec as P

HEAD = 72
PATCHES = 256
EPSILON = 1e-06
MIB = 1 << 20
F32 = jnp.float32
BF16 = jnp.bfloat16


def bits_of(size):
    return [1 << k for k in range(size.bit_length() - 1)]


def swap(block, axis, bit):
    count = lax.axis_size(axis)
    return lax.ppermute(block, axis, [(i, i ^ bit) for i in range(count)])


def my_bit(axis, bit):
    return (lax.axis_index(axis) // bit) % 2


def normalize(values):
    center = jnp.mean(values, axis=-1, keepdims=True)
    spread = jnp.mean(values * values, axis=-1, keepdims=True) - center * center
    inverse = lax.rsqrt(spread + EPSILON)
    return inverse, (values - center) * inverse


def norm_back(incoming, normed, inverse):
    first = jnp.mean(incoming, axis=-1, keepdims=True)
    second = jnp.mean(incoming * normed, axis=-1, keepdims=True)
    return inverse * (incoming - first - normed * second)


def gelu_both(upper):
    c0 = math.sqrt(2.0 / math.pi)
    square = upper * upper
    inner = c0 * upper * (1.0 + 0.044715 * square)
    tanh = jnp.tanh(inner)
    half = 0.5 * (1.0 + tanh)
    slope = half + 0.5 * upper * (1.0 - tanh * tanh) * (c0 * (1.0 + 0.134145 * square))
    return upper * half, slope


def dot(a, b, ca, cb):
    return lax.dot_general(a, b, (((ca,), (cb,)), ((), ())), preferred_element_type=F32)


def attend_kernel(heads, qkv_ref, out_ref):
    part = heads * HEAD
    scale = HEAD ** (-0.5)
    results = []
    for h in range(heads):
        q = qkv_ref[0, :, h * HEAD : (h + 1) * HEAD]
        k = qkv_ref[0, :, part + h * HEAD : part + (h + 1) * HEAD]
        v = qkv_ref[0, :, 2 * part + h * HEAD : 2 * part + (h + 1) * HEAD]
        s = dot(q, k, 1, 1)
        top = jnp.max(s, axis=1, keepdims=True)
        p = jnp.exp((s - top) * scale)
        total = jnp.sum(p, axis=1, keepdims=True)
        results.append(dot(p.astype(BF16), v, 1, 0) / total)
    out_ref[0] = jnp.concatenate(results, axis=1).astype(BF16)


def attend(qkv, heads):
    groups, rows, cols = qkv.shape
    part = heads * HEAD
    return pl.pallas_call(
        functools.partial(attend_kernel, heads),
        grid=(groups, rows // PATCHES),
        in_specs=[pl.BlockSpec((1, PATCHES, cols), lambda n, f: (n, f, 0))],
        out_specs=pl.BlockSpec((1, PATCHES, part), lambda n, f: (n, f, 0)),
        out_shape=jax.ShapeDtypeStruct((groups, rows, part), BF16),
        compiler_params=pltpu.CompilerParams(vmem_limit_bytes=32 * MIB),
        cost_estimate=pl.CostEstimate(
            flops=groups * rows * heads * PATCHES * 128 * 4,
            bytes_accessed=2 * groups * rows * (cols + part),
            transcendentals=groups * rows * heads * PATCHES,
        ),
        name="attend",
    )(qkv)


def attend_back_kernel(heads, qkv_ref, grad_ref, out_ref):
    part = heads * HEAD
    scale = HEAD ** (-0.5)
    dqs, dks, dvs = [], [], []
    for h in range(heads):
        q = qkv_ref[0, :, h * HEAD : (h + 1) * HEAD]
        k = qkv_ref[0, :, part + h * HEAD : part + (h + 1) * HEAD]
        v = qkv_ref[0, :, 2 * part + h * HEAD : 2 * part + (h + 1) * HEAD]
        g = grad_ref[0, :, h * HEAD : (h + 1) * HEAD]
        s = dot(q, k, 1, 1)
        top = jnp.max(s, axis=1, keepdims=True)
        p = jnp.exp((s - top) * scale)
        total = jnp.sum(p, axis=1, keepdims=True)
        p = p * (1.0 / total)
        dvs.append(dot(p.astype(BF16), g, 0, 0))
        dp = dot(g, v, 1, 1)
        mixed = p * dp
        ds = (mixed - p * jnp.sum(mixed, axis=1, keepdims=True)).astype(BF16)
        dqs.append(dot(ds, k, 1, 0) * scale)
        dks.append(dot(ds, q, 0, 0) * scale)
    out_ref[0] = jnp.concatenate(dqs + dks + dvs, axis=1).astype(BF16)


def attend_back(qkv, grad, heads):
    groups, rows, cols = qkv.shape
    part = heads * HEAD
    return pl.pallas_call(
        functools.partial(attend_back_kernel, heads),
        grid=(groups, rows // PATCHES),
        in_specs=[
            pl.BlockSpec((1, PATCHES, cols), lambda n, f: (n, f, 0)),
            pl.BlockSpec((1, PATCHES, part), lambda n, f: (n, f, 0)),
        ],
        out_specs=pl.BlockSpec((1, PATCHES, cols), lambda n, f: (n, f, 0)),
        out_shape=jax.ShapeDtypeStruct((groups, rows, cols), BF16),
        compiler_params=pltpu.CompilerParams(vmem_limit_bytes=32 * MIB),
        cost_estimate=pl.CostEstimate(
            flops=groups * rows * heads * PATCHES * 128 * 10,
            bytes_accessed=2 * groups * rows * (2 * cols + part),
            transcendentals=groups * rows * heads * PATCHES,
        ),
        name="attend_back",
    )(qkv, grad)


def widen(block, axis, bit, dim):
    other = swap(block, axis, bit)
    upper = my_bit(axis, bit) == 1
    return jnp.concatenate(
        [jnp.where(upper, other, block), jnp.where(upper, block, other)], axis=dim
    )


def dims_of():
    return [("narrow", bit) for bit in reversed(bits_of(lax.axis_size("narrow")))] + [
        ("wide", bit) for bit in reversed(bits_of(lax.axis_size("wide")))
    ]


def gather_chunk(shard):
    rows, cols = shard.shape
    dims = dims_of()
    place = {key: i for i, key in enumerate(dims)}
    cut = max(16, rows // 2 // 16 * 16)
    narrow = [key for key in dims if key[0] == "narrow"]
    wide = [key for key in dims if key[0] == "wide"]
    block = shard.reshape([1] * len(dims) + [rows, cols])
    for key in wide[:-1]:
        block = widen(block, *key, place[key])
    first, second = block[..., :cut, :], block[..., cut:, :]
    for key, other in zip(narrow, reversed(narrow)):
        first = widen(first, *key, place[key])
        second = widen(second, *other, place[other])
    first = widen(first, *wide[-1], place[wide[-1]])
    second = widen(second, *wide[-1], place[wide[-1]])
    whole = jnp.concatenate([first, second], axis=-2)
    narrow_count, wide_count = lax.axis_size("narrow"), lax.axis_size("wide")
    return whole.reshape(narrow_count, wide_count * rows, cols)


def halve(block, axis, bit, dim):
    mine = my_bit(axis, bit)
    kept = lax.dynamic_slice_in_dim(block, mine, 1, dim)
    sent = lax.dynamic_slice_in_dim(block, 1 - mine, 1, dim)
    return (kept.astype(F32) + swap(sent, axis, bit).astype(F32)).astype(block.dtype)


def scatter_chunk(grad):
    narrow_count, wide_count = lax.axis_size("narrow"), lax.axis_size("wide")
    rows, cols = grad.shape[1] // wide_count, grad.shape[2]
    dims = dims_of()
    place = {key: i for i, key in enumerate(dims)}
    cut = max(16, rows // 2 // 16 * 16)
    narrow = [key for key in dims if key[0] == "narrow"]
    wide = [key for key in dims if key[0] == "wide"]
    block = grad.reshape([2] * len(dims) + [rows, cols])
    block = halve(block, *wide[-1], place[wide[-1]])
    first, second = block[..., :cut, :], block[..., cut:, :]
    for key, other in zip(narrow, reversed(narrow)):
        first = halve(first, *key, place[key])
        second = halve(second, *other, place[other])
    block = jnp.concatenate([first, second], axis=-2)
    for key in reversed(wide[:-1]):
        block = halve(block, *key, place[key])
    return block.reshape(rows, cols).astype(F32)


def sum_over(block, axis):
    for bit in bits_of(lax.axis_size(axis)):
        block = block + swap(block, axis, bit)
    return block


def collect(block, axis):
    block = block[None]
    for bit in bits_of(lax.axis_size(axis)):
        block = widen(block, axis, bit, 0)
    return block


def share(block, count):
    for bit in bits_of(count):
        groups, rows, cols = block.shape
        pair = block.reshape(2, groups // 2, rows, cols)
        mine = my_bit("narrow", bit)
        kept = lax.dynamic_index_in_dim(pair, mine, 0, False)
        got = swap(lax.dynamic_index_in_dim(pair, 1 - mine, 0, False), "narrow", bit)
        block = jnp.concatenate(
            [jnp.where(mine == 1, got, kept), jnp.where(mine == 1, kept, got)], axis=1
        )
    return block


def unshare(block, count):
    for bit in reversed(bits_of(count)):
        groups, rows, cols = block.shape
        pair = block.reshape(groups, 2, rows // 2, cols)
        mine = my_bit("narrow", bit)
        kept = lax.dynamic_index_in_dim(pair, mine, 1, False)
        got = swap(lax.dynamic_index_in_dim(pair, 1 - mine, 1, False), "narrow", bit)
        block = jnp.concatenate(
            [jnp.where(mine == 1, got, kept), jnp.where(mine == 1, kept, got)], axis=0
        )
    return block


def shards(
    tokens,
    condition,
    frame_clip,
    mod_weight,
    mod_bias,
    project_weight,
    project_bias,
    merge_weight,
    merge_bias,
    up_weight,
    up_bias,
    down_weight,
    down_bias,
    out_cotangent,
):
    rows, width = tokens.shape
    wide_count, narrow_count = lax.axis_size("wide"), lax.axis_size("narrow")
    wide_me, narrow_me = lax.axis_index("wide"), lax.axis_index("narrow")
    depth = width // wide_count
    part = width // narrow_count
    units = up_weight.shape[1]
    heads = part // HEAD
    clips = condition.shape[0]
    span = math.gcd(rows, PATCHES)
    spans = rows // span
    sharing = PATCHES // span

    attn_shard = jnp.concatenate(
        [project_weight.reshape(depth, 3 * part), merge_weight.T], axis=1
    )
    attn_w = gather_chunk(attn_shard)
    up_w = gather_chunk(up_weight)
    down_w = gather_chunk(down_weight.T)
    project_w = attn_w[:, :, : 3 * part]
    merge_w = attn_w[:, :, 3 * part :]

    active = jax.nn.silu(condition).astype(BF16)
    active_mine = lax.dynamic_slice_in_dim(active, wide_me * depth, depth, 1)
    mode_part = jnp.einsum("cd,dki->cki", active_mine, mod_weight, preferred_element_type=F32)
    mode_part = sum_over(mode_part, "wide") + mod_bias.astype(F32)[None]
    unit_rows = units // part
    small = jnp.concatenate(
        [
            mode_part.reshape(clips * 6, part),
            project_bias.astype(F32),
            merge_bias.astype(F32)[None],
            down_bias.astype(F32)[None],
            up_bias.astype(F32).reshape(unit_rows, part),
        ],
        axis=0,
    )
    small = collect(small, "narrow")
    modes = small[:, : clips * 6].reshape(narrow_count, clips, 6, part)
    at = clips * 6
    bias_q = small[:, at]
    bias_v = small[:, at + 1]
    merge_bias_full = small[:, at + 2].reshape(width)
    down_bias_full = small[:, at + 3].reshape(width)
    up_bias_full = small[:, at + 4 :].reshape(narrow_count, units)

    span_frame = (narrow_me * rows + jnp.arange(spans, dtype=jnp.int32) * span) // PATCHES
    span_clip = jnp.sum(
        jnp.where(
            span_frame[:, None] == jnp.arange(frame_clip.shape[0], dtype=jnp.int32)[None],
            frame_clip[None],
            0,
        ),
        axis=1,
    )
    span_modes = jnp.concatenate(
        [lax.dynamic_slice_in_dim(modes, span_clip[s], 1, 1) for s in range(spans)], axis=1
    )
    span_modes = span_modes.transpose(1, 2, 0, 3).reshape(spans, 6, 1, width)
    shift_a, scale_a, gate_a, shift_b, scale_b, gate_b = [span_modes[:, i] for i in range(6)]

    inputs = tokens.astype(F32).reshape(spans, span, width)
    inverse_a, normed_a = normalize(inputs)
    hidden_a = (normed_a * (1.0 + scale_a) + shift_a).astype(BF16).reshape(rows, width)
    qkv_bias = jnp.concatenate([bias_q, jnp.zeros_like(bias_q), bias_v], axis=1)
    qkv = jnp.einsum("td,ndc->ntc", hidden_a, project_w, preferred_element_type=F32)
    qkv = (qkv + qkv_bias[:, None]).astype(BF16)
    qkv_frames = share(qkv, sharing)
    attended = unshare(attend(qkv_frames, heads), sharing)
    merged = jnp.einsum("nti,ndi->td", attended, merge_w, preferred_element_type=F32)
    branch_a = (merged + merge_bias_full).reshape(spans, span, width)
    middle = inputs + gate_a * branch_a
    inverse_b, normed_b = normalize(middle)
    hidden_b = (normed_b * (1.0 + scale_b) + shift_b).astype(BF16).reshape(rows, width)
    upper = jnp.einsum("td,ndf->ntf", hidden_b, up_w, preferred_element_type=F32)
    gelu_out, slope = gelu_both(upper + up_bias_full[:, None])
    gelu_out, slope = gelu_out.astype(BF16), slope.astype(BF16)
    core = jnp.einsum("ntf,ndf->td", gelu_out, down_w, preferred_element_type=F32)
    branch_b = (core + down_bias_full).reshape(spans, span, width)
    output = (middle + gate_b * branch_b).astype(BF16).reshape(rows, width)

    grad_out = out_cotangent.astype(F32).reshape(spans, span, width)
    gated_out = gate_b * grad_out
    down_bias_grad = jnp.sum(gated_out, axis=(0, 1))
    core_grad = gated_out.astype(BF16).reshape(rows, width)
    down_part = jnp.einsum("td,ntf->ndf", core_grad, gelu_out, preferred_element_type=F32)
    down_grad = scatter_chunk(down_part.astype(BF16))
    gelu_grad = jnp.einsum("td,ndf->ntf", core_grad, down_w, preferred_element_type=F32)
    upper_grad = (gelu_grad * slope.astype(F32)).astype(BF16)
    up_bias_grad = jnp.sum(upper_grad.astype(F32), axis=1)
    up_part = jnp.einsum("td,ntf->ndf", hidden_b, upper_grad, preferred_element_type=F32)
    up_grad = scatter_chunk(up_part.astype(BF16))
    hidden_b_grad = jnp.einsum("ntf,ndf->td", upper_grad, up_w, preferred_element_type=F32)
    hidden_b_grad = hidden_b_grad.reshape(spans, span, width)
    middle_grad = grad_out + norm_back(hidden_b_grad * (1.0 + scale_b), normed_b, inverse_b)

    gated_middle = gate_a * middle_grad
    merge_bias_grad = jnp.sum(gated_middle, axis=(0, 1))
    merged_grad = gated_middle.astype(BF16).reshape(rows, width)
    attended_grad = jnp.einsum("td,ndi->nti", merged_grad, merge_w, preferred_element_type=F32)
    attended_grad = share(attended_grad.astype(BF16), sharing)
    merge_part = jnp.einsum("td,nti->ndi", merged_grad, attended, preferred_element_type=F32)
    qkv_grad = unshare(attend_back(qkv_frames, attended_grad, heads), sharing)
    qkv_sums = jnp.sum(qkv_grad.astype(F32), axis=1)
    project_part = jnp.einsum("td,ntc->ndc", hidden_a, qkv_grad, preferred_element_type=F32)
    attn_part = jnp.concatenate([project_part.astype(BF16), merge_part.astype(BF16)], axis=2)
    attn_grad = scatter_chunk(attn_part)
    hidden_a_grad = jnp.einsum("ntc,ndc->td", qkv_grad, project_w, preferred_element_type=F32)
    hidden_a_grad = hidden_a_grad.reshape(spans, span, width)
    tokens_grad = middle_grad + norm_back(hidden_a_grad * (1.0 + scale_a), normed_a, inverse_a)

    span_grad = jnp.stack(
        [
            jnp.sum(hidden_a_grad, axis=1),
            jnp.sum(hidden_a_grad * normed_a, axis=1),
            jnp.sum(middle_grad * branch_a, axis=1),
            jnp.sum(hidden_b_grad, axis=1),
            jnp.sum(hidden_b_grad * normed_b, axis=1),
            jnp.sum(grad_out * branch_b, axis=1),
        ],
        axis=1,
    )
    hits = span_clip[None, :] == jnp.arange(clips, dtype=jnp.int32)[:, None]
    clip_grad = jnp.sum(jnp.where(hits[:, :, None, None], span_grad[None], 0.0), axis=1)
    clip_grad = clip_grad.reshape(clips * 6, narrow_count, part).transpose(1, 0, 2)
    packed = jnp.concatenate(
        [
            clip_grad,
            qkv_sums[:, None, :part],
            qkv_sums[:, None, 2 * part :],
            merge_bias_grad.reshape(narrow_count, 1, part),
            down_bias_grad.reshape(narrow_count, 1, part),
            up_bias_grad.reshape(narrow_count, unit_rows, part),
        ],
        axis=1,
    )
    depth_rows = packed.shape[1]
    packed = packed.reshape([2] * len(bits_of(narrow_count)) + [depth_rows, part])
    for place, bit in enumerate(reversed(bits_of(narrow_count))):
        packed = halve(packed, "narrow", bit, place)
    packed = sum_over(packed.reshape(depth_rows, part), "wide")
    clip_slice = packed[: clips * 6].reshape(clips, 6, part)
    mod_bias_grad = jnp.sum(clip_slice, axis=0)
    mod_weight_grad = jnp.einsum(
        "cd,cki->dki", active_mine.astype(F32), clip_slice, precision=lax.Precision.HIGHEST
    )
    active_grad = jnp.einsum(
        "cki,dki->cd", clip_slice, mod_weight.astype(F32), precision=lax.Precision.HIGHEST
    )
    active_grad = collect(sum_over(active_grad, "narrow"), "wide")
    active_grad = active_grad.transpose(1, 0, 2).reshape(clips, width)
    unused, silu_pullback = jax.vjp(jax.nn.silu, condition)
    condition_grad = silu_pullback(active_grad)[0]

    return (
        output,
        tokens_grad.reshape(rows, width),
        condition_grad,
        mod_weight_grad,
        mod_bias_grad,
        attn_grad[:, : 3 * part].reshape(depth, 3, part),
        packed[at : at + 2],
        attn_grad[:, 3 * part :].T,
        packed[at + 2],
        up_grad,
        packed[at + 4 :].reshape(units),
        down_grad.T,
        packed[at + 3],
    )


def solution(mesh):
    both = P(("wide", "narrow"), None)
    ins = (
        both,
        P(),
        P("wide"),
        P("wide", None, "narrow"),
        P(None, "narrow"),
        P("wide", None, "narrow"),
        P(None, "narrow"),
        P("narrow", "wide"),
        P("narrow"),
        P("wide", "narrow"),
        P("narrow"),
        P("narrow", "wide"),
        P("narrow"),
        both,
    )
    outs = (
        both,
        both,
        P(),
        P("wide", None, "narrow"),
        P(None, "narrow"),
        P("wide", None, "narrow"),
        P(None, "narrow"),
        P("narrow", "wide"),
        P("narrow"),
        P("wide", "narrow"),
        P("narrow"),
        P("narrow", "wide"),
        P("narrow"),
    )
    return jax.shard_map(shards, mesh=mesh, in_specs=ins, out_specs=outs, check_vma=False)
```

```python
import functools
import math

import jax
import jax.numpy as jnp
from jax import lax
from jax.experimental import pallas as pl
from jax.experimental.pallas import tpu as pltpu
from jax.sharding import PartitionSpec as P

HEAD = 72
PATCHES = 256
EPSILON = 1e-06
MIB = 1 << 20
F32 = jnp.float32
BF16 = jnp.bfloat16


def bits_of(size):
    return [1 << k for k in range(size.bit_length() - 1)]


def swap(block, axis, bit):
    count = lax.axis_size(axis)
    return lax.ppermute(block, axis, [(i, i ^ bit) for i in range(count)])


def my_bit(axis, bit):
    return (lax.axis_index(axis) // bit) % 2


def tied(*values):
    return lax.optimization_barrier(values)


def dot(a, b, ca, cb):
    return lax.dot_general(a, b, (((ca,), (cb,)), ((), ())), preferred_element_type=F32)


def row_mean(values):
    return jnp.mean(values, axis=1, keepdims=True)


def normalize(values):
    center = row_mean(values)
    inverse = lax.rsqrt(row_mean(values * values) - center * center + EPSILON)
    return inverse, (values - center) * inverse


def norm_back(incoming, normed, inverse):
    return inverse * (incoming - row_mean(incoming) - normed * row_mean(incoming * normed))


def gelu_both(upper):
    c0 = math.sqrt(2.0 / math.pi)
    square = upper * upper
    tanh = jnp.tanh(upper * (c0 + (c0 * 0.044715) * square))
    half = 0.5 + 0.5 * tanh
    bend = (half * (1.0 - half)) * (2.0 * c0 + (2.0 * c0 * 0.134145) * square)
    return upper * half, half + upper * bend


def params(limit=56):
    return pltpu.CompilerParams(vmem_limit_bytes=limit * MIB)


def cost():
    return pl.CostEstimate(flops=1000000000, bytes_accessed=1, transcendentals=0)


def whole(array):
    return pl.BlockSpec(array.shape, lambda i, *_: (0,) * array.ndim)


def along(array):
    return pl.BlockSpec((1,) + array.shape[1:], lambda i, *_: (i,) + (0,) * (array.ndim - 1))


def shape_of(shape, dtype):
    return jax.ShapeDtypeStruct(shape, dtype)


def attend_kernel(heads, qkv_ref, out_ref):
    part = heads * HEAD
    scale = HEAD ** (-0.5)
    results = []
    for n in range(qkv_ref.shape[0]):
        for h in range(heads):
            at = h * HEAD
            q = qkv_ref[n, :, at : at + HEAD]
            k = qkv_ref[n, :, part + at : part + at + HEAD]
            v = qkv_ref[n, :, 2 * part + at : 2 * part + at + HEAD]
            s = dot(k, q, 1, 1)
            p = jnp.exp((s - jnp.max(s, axis=0, keepdims=True)) * scale)
            total = jnp.sum(p, axis=0, keepdims=True)
            results.append(dot(v, p.astype(BF16), 0, 0) / total)
    out_ref[...] = jnp.concatenate(results, axis=0).T.astype(BF16)


def attend(qkv, heads):
    groups, rows, cols = qkv.shape
    width = groups * heads * HEAD
    out = shape_of((rows, width), BF16)
    return pl.pallas_call(
        functools.partial(attend_kernel, heads),
        grid=(rows // PATCHES,),
        in_specs=[pl.BlockSpec((groups, PATCHES, cols), lambda f: (0, f, 0))],
        out_specs=pl.BlockSpec((PATCHES, width), lambda f: (f, 0)),
        out_shape=out,
        compiler_params=params(),
        cost_estimate=cost(),
        name="attend",
    )(qkv)


def attend_back_kernel(heads, qkv_ref, grad_ref, out_ref):
    part = heads * HEAD
    scale = HEAD ** (-0.5)
    for n in range(qkv_ref.shape[0]):
        dqs, dks, dvs = [], [], []
        for h in range(heads):
            at = h * HEAD
            q = qkv_ref[n, :, at : at + HEAD]
            k = qkv_ref[n, :, part + at : part + at + HEAD]
            v = qkv_ref[n, :, 2 * part + at : 2 * part + at + HEAD]
            g = grad_ref[:, n * part + at : n * part + at + HEAD]
            s = dot(k, q, 1, 1)
            p = jnp.exp((s - jnp.max(s, axis=0, keepdims=True)) * scale)
            p = p * (1.0 / jnp.sum(p, axis=0, keepdims=True))
            dvs.append(dot(p.astype(BF16), g, 1, 0))
            dp = dot(v, g, 1, 1)
            dp = dp - jnp.sum(p * dp, axis=0, keepdims=True)
            ds = (p * dp).astype(BF16)
            dks.append(dot(ds, q, 1, 0) * scale)
            dqs.append(dot(k, ds, 0, 0) * scale)
        dq = jnp.concatenate(dqs, axis=0).T
        pad = [jnp.zeros((PATCHES, out_ref.shape[2] - 3 * part), F32)]
        out_ref[n] = jnp.concatenate([dq] + dks + dvs + pad, axis=1).astype(BF16)


def attend_back(qkv, grad, heads, frame):
    groups, rows, cols = qkv.shape
    width = groups * heads * HEAD
    out = shape_of((groups, PATCHES, -(-cols // 128) * 128), BF16)
    return pl.pallas_call(
        functools.partial(attend_back_kernel, heads),
        grid=(1,),
        in_specs=[
            pl.BlockSpec((groups, PATCHES, cols), lambda i: (0, frame, 0)),
            pl.BlockSpec((PATCHES, width), lambda i: (frame, 0)),
        ],
        out_specs=pl.BlockSpec(out.shape, lambda i: (0, 0, 0)),
        out_shape=out,
        compiler_params=params(),
        cost_estimate=cost(),
        name="attend_back",
    )(qkv, grad)


class Sent:
    def __init__(self, *values):
        self.pending = list(values)

    def take(self, got):
        self.got = got
        self.pending = []


def land(sents, *ties):
    sents = [sent for sent in sents if sent.pending]
    pending = [value for sent in sents for value in sent.pending]
    values = list(tied(*pending, *ties))
    for sent in sents:
        count = len(sent.pending)
        sent.take(values[:count])
        values = values[count:]
    return values


class Gather:
    def __init__(self, shard, low, high):
        self.low = low
        self.depth = high - low
        self.cut = max(16, self.depth // 2 // 16 * 16)
        wide = [("wide", bit) for bit in reversed(bits_of(lax.axis_size("wide")))]
        narrow = [("narrow", bit) for bit in reversed(bits_of(lax.axis_size("narrow")))]
        self.core = wide[-1]
        self.front = wide[:-1]
        self.orders = [narrow, narrow[::-1]]
        self.parts = [shard[low:high][None]]
        self.stage = 0
        self.stages = len(self.front) + len(narrow)
        self.pending = []
        self.cored = []

    def start(self):
        if self.stage < len(self.front):
            keys = [self.front[self.stage]]
        else:
            keys = [order[self.stage - len(self.front)] for order in self.orders]
        self.pending = [swap(part, *key) for part, key in zip(self.parts, keys)]
        return self

    def take(self, got):
        self.pending = []
        self.stage += 1
        if self.stage == self.stages:
            self.near, self.far = self.parts, list(got)
        else:
            blocks = [jnp.concatenate([part, new], axis=0) for part, new in zip(self.parts, got)]
            if self.stage == len(self.front):
                block = blocks[0]
                blocks = [block[:, : self.cut], block[:, self.cut :]]
            self.parts = blocks

    def across(self):
        blocks = self.parts if self.stage < self.stages else self.far
        sent = Sent(*[swap(block, *self.core) for block in blocks])
        self.cored.append(sent)
        return sent

    def finish(self):
        near_core, far_core = self.cored[0].got, self.cored[1].got
        self.arrays = []
        for part in range(2):
            self.arrays += [self.near[part], self.far[part], near_core[part], far_core[part]]

    def ranges(self):
        return [(0, self.cut), (self.cut, self.depth - self.cut)]

    def entries(self, n, shift):
        found = []
        for w in range(lax.axis_size("wide")):
            for part, (offset, size) in enumerate(self.ranges()):
                keys = self.front + self.orders[part]
                flips = [(n if axis == "narrow" else w) & bit for axis, bit in keys]
                index = sum(1 << j for j, flip in enumerate(flips[:-1]) if flip)
                which = 4 * part + 2 * bool(w & self.core[1]) + bool(flips[-1])
                found.append((shift + which, index, w, self.low + offset, size))
        return found

    def assembled(self):
        pieces = []
        for part in range(2):
            near, far, near_core, far_core = self.arrays[4 * part : 4 * part + 4]
            block = jnp.stack([jnp.stack([near, far]), jnp.stack([near_core, far_core])])
            keys = [self.core] + (self.front + self.orders[part])[::-1]
            block = block.reshape([2] * len(keys) + list(block.shape[-2:]))
            wanted = [("narrow", bit) for bit in reversed(bits_of(lax.axis_size("narrow")))]
            wanted += self.front + [self.core]
            block = block.transpose([keys.index(key) for key in wanted] + [len(keys), len(keys) + 1])
            for dim, key in enumerate(wanted):
                if key[0] == "wide":
                    block = jnp.where(my_bit(*key) == 1, jnp.flip(block, dim), block)
            pieces.append(block)
        block = jnp.concatenate(pieces, axis=-2)
        return block.reshape(
            lax.axis_size("narrow"), lax.axis_size("wide"), self.depth, block.shape[-1]
        )


class Weight:
    def __init__(self, *gathers):
        groups, blocks = lax.axis_size("narrow"), lax.axis_size("wide")
        self.depth = sum(g.depth for g in gathers)
        self.cols = gathers[0].arrays[0].shape[-1]
        sizes = [size for g in gathers for pair in g.ranges() for size in pair]
        if any(size % 16 for size in sizes):
            block = jnp.concatenate([g.assembled() for g in gathers], axis=2)
            self.arrays = [block.reshape(groups, blocks * self.depth, self.cols)]
            self.plan = [[(0, n, None, 0, 0)] for n in range(groups)]
        else:
            self.arrays, self.plan = [], [[] for n in range(groups)]
            for g in gathers:
                for n in range(groups):
                    self.plan[n] += g.entries(n, len(self.arrays))
                self.arrays += g.arrays


def stream(step, weight, me, refs, buffer, sems):
    plan = weight.plan

    def issue(n):
        for which, index, w, offset, size in plan[n]:
            if w is None:
                target = buffer.at[n % 2]
            else:
                row = pl.multiple_of((me ^ w) * weight.depth + offset, 16)
                target = buffer.at[n % 2, pl.ds(row, size)]
            pltpu.make_async_copy(refs[which].at[index], target, sems.at[n % 2]).start()

    for n in range(len(plan)):

        @pl.when(step == n)
        def _():
            if n == 0:
                issue(0)
            if n + 1 < len(plan):
                issue(n + 1)

    slot = step % 2
    pltpu.make_async_copy(buffer.at[slot], buffer.at[slot], sems.at[slot]).wait()
    return buffer.at[slot]


def weight_call(body, weight, ins, in_specs, outs, out_specs, scratch, name):
    count, groups = len(weight.arrays), len(weight.plan)
    width = lax.axis_size("wide") * weight.depth

    def kernel(me_ref, *refs):
        step = pl.program_id(0)
        in_refs = refs[: len(ins)]
        weight_refs = refs[len(ins) : len(ins) + count]
        out_refs = refs[len(ins) + count : len(ins) + count + len(outs)]
        buffer, sems = refs[len(ins) + count + len(outs) :][:2]
        scratch_refs = refs[len(ins) + count + len(outs) + 2 :]
        w = stream(step, weight, me_ref[0], weight_refs, buffer, sems)
        body(step, in_refs, w, out_refs, scratch_refs)

    me = lax.axis_index("wide").astype(jnp.int32)[None]
    return pl.pallas_call(
        kernel,
        grid_spec=pltpu.PrefetchScalarGridSpec(
            num_scalar_prefetch=1,
            grid=(groups,),
            in_specs=list(in_specs) + [pl.BlockSpec(memory_space=pl.ANY)] * count,
            out_specs=list(out_specs),
            scratch_shapes=[
                pltpu.VMEM((2, width, weight.cols), BF16),
                pltpu.SemaphoreType.DMA((2,)),
            ]
            + list(scratch),
        ),
        out_shape=list(outs),
        compiler_params=params(),
        cost_estimate=cost(),
        name=name,
    )(me, *ins, *weight.arrays)


def project_call(weight, tokens, modes, bias, part):
    rows, width = tokens.shape
    spans, span = modes.shape[0], rows // modes.shape[0]
    groups = len(weight.plan)
    outs = [
        shape_of((rows, width), BF16),
        shape_of((groups, rows, 3 * part), BF16),
        shape_of((width, groups * part), BF16),
    ]

    def body(step, ins, w, out, scratch):
        tokens_ref, modes_ref, bias_ref = ins
        hidden_ref, qkv_ref, merge_ref = out

        @pl.when(step == 0)
        def _():
            for s in range(spans):
                at = slice(s * span, (s + 1) * span)
                unused, normed = normalize(tokens_ref[at, :].astype(F32))
                hidden = normed * (1.0 + modes_ref[s, 1:2]) + modes_ref[s, 0:1]
                hidden_ref[at, :] = hidden.astype(BF16)

        qkv_ref[0] = (dot(hidden_ref[...], w[:, : 3 * part], 1, 0) + bias_ref[0]).astype(BF16)
        for n in range(groups):

            @pl.when(step == n)
            def _():
                merge_ref[:, n * part : (n + 1) * part] = w[:, 3 * part :]

    return weight_call(
        body,
        weight,
        [tokens, modes, bias],
        [whole(tokens), whole(modes), along(bias)],
        outs,
        [whole(outs[0]), along(outs[1]), whole(outs[2])],
        [],
        "project",
    )


def merge_kernel(attended_ref, weight_ref, tokens_ref, modes_ref, bias_ref, branch_ref, hidden_ref):
    branch = dot(attended_ref[...], weight_ref[...], 1, 1) + bias_ref[...]
    branch_ref[...] = branch
    middle = tokens_ref[...].astype(F32) + modes_ref[0, 2:3] * branch
    unused, normed = normalize(middle)
    hidden_ref[...] = (normed * (1.0 + modes_ref[0, 4:5]) + modes_ref[0, 3:4]).astype(BF16)


def merge_call(attended, weight, tokens, modes, bias):
    rows, width = tokens.shape
    spans, span = modes.shape[0], rows // modes.shape[0]
    block = pl.BlockSpec((span, width), lambda i: (i, 0))
    outs = [shape_of((rows, width), F32), shape_of((rows, width), BF16)]
    return pl.pallas_call(
        merge_kernel,
        grid=(spans,),
        in_specs=[block, whole(weight), block, along(modes), whole(bias)],
        out_specs=[block, block],
        out_shape=outs,
        compiler_params=params(),
        cost_estimate=cost(),
        name="merge",
    )(attended, weight, tokens, modes, bias)


def up_call(weight, hidden, bias):
    rows, width = hidden.shape
    groups, units = len(weight.plan), weight.cols
    outs = [shape_of((groups, rows, units), BF16)] * 2

    def body(step, ins, w, out, scratch):
        hidden_ref, bias_ref = ins
        gelu, slope = gelu_both(dot(hidden_ref[...], w[...], 1, 0) + bias_ref[0])
        out[0][0] = gelu.astype(BF16)
        out[1][0] = slope.astype(BF16)

    return weight_call(
        body,
        weight,
        [hidden, bias],
        [whole(hidden), along(bias)],
        outs,
        [along(outs[0]), along(outs[1])],
        [],
        "up",
    )


def down_call(weight, gelu, tokens, branch, modes, bias, grad):
    rows, width = tokens.shape
    spans, span = modes.shape[0], rows // modes.shape[0]
    groups, units = len(weight.plan), weight.cols
    outs = [shape_of((rows, width), BF16), shape_of((spans, 1, width), F32)]

    def body(step, ins, w, out, scratch):
        gelu_ref, tokens_ref, branch_ref, modes_ref, bias_ref, grad_ref = ins
        total = scratch[0]
        @pl.when(step == 0)
        def _():
            total[...] = dot(gelu_ref[0], w[...], 1, 1)

        @pl.when((step > 0) & (step < groups - 1))
        def _():
            total[...] += dot(gelu_ref[0], w[...], 1, 1)

        @pl.when(step == groups - 1)
        def _():
            for s in range(spans):
                at = slice(s * span, (s + 1) * span)
                summed = total[at, :] + dot(gelu_ref[0, at, :], w[...], 1, 1)
                other = summed + bias_ref[...]
                middle = tokens_ref[at, :].astype(F32) + modes_ref[s, 2:3] * branch_ref[at, :]
                out[0][at, :] = (middle + modes_ref[s, 5:6] * other).astype(BF16)
                out[1][s] = jnp.sum(grad_ref[at, :].astype(F32) * other, axis=0, keepdims=True)

    return weight_call(
        body,
        weight,
        [gelu, tokens, branch, modes, bias, grad],
        [along(gelu)] + [whole(a) for a in (tokens, branch, modes, bias, grad)],
        outs,
        [whole(outs[0]), whole(outs[1])],
        [pltpu.VMEM((rows, width), F32)],
        "down",
    )


def gelu_back_call(weight, grad, slope):
    rows, width = grad.shape
    groups, units = len(weight.plan), weight.cols
    outs = [shape_of((groups, rows, units), BF16), shape_of((groups, 1, units), F32)]

    def body(step, ins, w, out, scratch):
        grad_ref, slope_ref = ins
        upper = (dot(grad_ref[...], w[...], 1, 0) * slope_ref[0].astype(F32)).astype(BF16)
        out[0][0] = upper
        out[1][0] = jnp.sum(upper.astype(F32), axis=0, keepdims=True)

    return weight_call(
        body,
        weight,
        [grad, slope],
        [whole(grad), along(slope)],
        outs,
        [along(outs[0]), along(outs[1])],
        [],
        "gelu_back",
    )


def up_back_call(weight, upper, tokens, branch, modes, grad):
    rows, width = tokens.shape
    spans, span = modes.shape[0], rows // modes.shape[0]
    groups, units = len(weight.plan), weight.cols
    outs = [
        shape_of((rows, width), F32),
        shape_of((rows, width), BF16),
        shape_of((spans, 3, width), F32),
        shape_of((1, width), F32),
    ]

    def body(step, ins, w, out, scratch):
        upper_ref, tokens_ref, branch_ref, modes_ref, grad_ref = ins
        middle_ref, merged_ref, sums_ref, bias_ref = out
        total = scratch[0]
        @pl.when(step == 0)
        def _():
            total[...] = dot(upper_ref[0], w[...], 1, 1)

        @pl.when((step > 0) & (step < groups - 1))
        def _():
            total[...] += dot(upper_ref[0], w[...], 1, 1)

        @pl.when(step == groups - 1)
        def _():
            for s in range(spans):
                at = slice(s * span, (s + 1) * span)
                summed = total[at, :] + dot(upper_ref[0, at, :], w[...], 1, 1)
                branch = branch_ref[at, :]
                gate = modes_ref[s, 2:3]
                inverse, normed = normalize(tokens_ref[at, :].astype(F32) + gate * branch)
                hidden = summed
                back = norm_back(hidden * (1.0 + modes_ref[s, 4:5]), normed, inverse)
                middle = grad_ref[at, :].astype(F32) + back
                gated = gate * middle
                middle_ref[at, :] = middle
                merged_ref[at, :] = gated.astype(BF16)
                sums_ref[s, 0:1] = jnp.sum(middle * branch, axis=0, keepdims=True)
                sums_ref[s, 1:2] = jnp.sum(hidden, axis=0, keepdims=True)
                sums_ref[s, 2:3] = jnp.sum(hidden * normed, axis=0, keepdims=True)
                here = jnp.sum(gated, axis=0, keepdims=True)
                bias_ref[...] = here if s == 0 else bias_ref[...] + here

    return weight_call(
        body,
        weight,
        [upper, tokens, branch, modes, grad],
        [along(upper)] + [whole(a) for a in (tokens, branch, modes, grad)],
        outs,
        [whole(a) for a in outs],
        [pltpu.VMEM((rows, width), F32)],
        "up_back",
    )


def project_back_call(weight, qkv_grads, tokens, middle, modes, cols):
    rows, width = tokens.shape
    spans, span = modes.shape[0], rows // modes.shape[0]
    groups, pieces = len(weight.plan), len(qkv_grads)
    outs = [
        shape_of((rows, width), F32),
        shape_of((spans, 2, width), F32),
        shape_of((groups, 1, cols), F32),
    ]

    def body(step, ins, w, out, scratch):
        tokens_ref, middle_ref, modes_ref = ins[pieces:]
        tokens_grad_ref, sums_ref, bias_ref = out
        total = scratch[0]
        grad = jnp.concatenate([ref[0, :, :cols] for ref in ins[:pieces]], axis=0)
        bias_ref[0] = jnp.sum(grad.astype(F32), axis=0, keepdims=True)

        @pl.when(step == 0)
        def _():
            total[...] = dot(grad, w[:, :cols], 1, 1)

        @pl.when((step > 0) & (step < groups - 1))
        def _():
            total[...] += dot(grad, w[:, :cols], 1, 1)

        @pl.when(step == groups - 1)
        def _():
            for s in range(spans):
                at = slice(s * span, (s + 1) * span)
                inverse, normed = normalize(tokens_ref[at, :].astype(F32))
                hidden = total[at, :] + dot(grad[at], w[:, :cols], 1, 1)
                back = norm_back(hidden * (1.0 + modes_ref[s, 1:2]), normed, inverse)
                tokens_grad_ref[at, :] = middle_ref[at, :] + back
                sums_ref[s, 0:1] = jnp.sum(hidden, axis=0, keepdims=True)
                sums_ref[s, 1:2] = jnp.sum(hidden * normed, axis=0, keepdims=True)

    return weight_call(
        body,
        weight,
        [*qkv_grads, tokens, middle, modes],
        [along(a) for a in qkv_grads] + [whole(a) for a in (tokens, middle, modes)],
        outs,
        [whole(outs[0]), whole(outs[1]), along(outs[2])],
        [pltpu.VMEM((rows, width), F32)],
        "project_back",
    )


def put_turned(depth, side, block, own_ref, other_ref):
    turned_block = block.T
    for z in range(own_ref.shape[0]):
        even = turned_block[2 * z * depth : (2 * z + 1) * depth]
        odd = turned_block[(2 * z + 1) * depth : (2 * z + 2) * depth]
        own_ref[z] = jnp.where(side == 1, odd, even)
        other_ref[z] = jnp.where(side == 1, even, odd)


def turn_kernel(depth, me_ref, block_ref, own_ref, other_ref):
    put_turned(depth, me_ref[0] & 1, block_ref[...], own_ref, other_ref)


def turn(block):
    rows, width = block.shape
    blocks = lax.axis_size("wide")
    out = shape_of((blocks // 2, width // blocks, rows), BF16)
    me = lax.axis_index("wide").astype(jnp.int32)[None]
    own, other = pl.pallas_call(
        functools.partial(turn_kernel, width // blocks),
        grid_spec=pltpu.PrefetchScalarGridSpec(
            num_scalar_prefetch=1, grid=(1,), in_specs=[whole(block)], out_specs=[whole(out)] * 2
        ),
        out_shape=[out, out],
        compiler_params=params(24),
        cost_estimate=cost(),
        name="turn",
    )(me, block)
    return own, other


def weight_grad_call(lefts, grads, merged, attended, cols, low, high):
    zs, depth, rows = lefts[0].shape
    groups, size = grads[0].shape[0], high - low
    width = 2 * zs * depth
    cut = max(16, size // 2 // 16 * 16)
    part = width // groups if merged else 0
    half = groups // 2
    outs = []
    for height in (cut, cut, size - cut, size - cut):
        outs.append(shape_of((half, zs, height, cols + part), BF16))
    ins = [*lefts, *merged, *grads, *attended]
    count = len(lefts)

    def kernel(*refs):
        step = pl.program_id(0)
        in_refs, out_refs, scratch = refs[: len(ins)], refs[len(ins) : len(ins) + 4], refs[len(ins) + 4 :]
        grad_refs = in_refs[count + len(merged) : count + len(merged) + len(grads)]
        attended_refs = in_refs[count + len(merged) + len(grads) :]

        @pl.when(step == 0)
        def _():
            for i in range(count + len(merged)):
                target, at = scratch[i // count], (i % count) * rows
                for z in range(zs):
                    target[z * size : (z + 1) * size, at : at + rows] = in_refs[i][z, low:high]
            if merged:
                both = jnp.concatenate([ref[...] for ref in attended_refs], axis=0)
                scratch[2][...] = dot(scratch[1][...], both, 1, 0).astype(BF16)

        both = jnp.concatenate([ref[0, :, :cols] for ref in grad_refs], axis=0)
        result = dot(scratch[0][...], both, 1, 0).astype(BF16)
        for n in range(groups):

            @pl.when(step == n)
            def _():
                value = result
                if merged:
                    value = jnp.concatenate([value, scratch[2][:, n * part : (n + 1) * part]], axis=1)
                first = out_refs[0] if n < half else out_refs[1]
                second = out_refs[2] if n % 2 == 0 else out_refs[3]
                for z in range(zs):
                    first[0, z] = value[z * size : z * size + cut]
                    second[0, z] = value[z * size + cut : (z + 1) * size]

    scratch = [pltpu.VMEM((zs * size, count * rows), BF16)]
    if merged:
        scratch += [pltpu.VMEM((zs * size, count * rows), BF16), pltpu.VMEM((zs * size, width), BF16)]
    rest = (0, 0, 0)
    out_specs = [
        pl.BlockSpec((1,) + outs[0].shape[1:], lambda i: (jnp.minimum(i, half - 1),) + rest),
        pl.BlockSpec((1,) + outs[1].shape[1:], lambda i: (jnp.maximum(i - half, 0),) + rest),
        pl.BlockSpec((1,) + outs[2].shape[1:], lambda i: (i // 2,) + rest),
        pl.BlockSpec((1,) + outs[3].shape[1:], lambda i: (i // 2,) + rest),
    ]
    return pl.pallas_call(
        kernel,
        grid=(groups,),
        in_specs=[whole(a) for a in (*lefts, *merged)]
        + [along(a) for a in grads]
        + [whole(a) for a in attended],
        out_specs=out_specs,
        scratch_shapes=scratch,
        out_shape=outs,
        compiler_params=params(),
        cost_estimate=cost(),
        name="weight_grad",
    )(*ins)


def plus(a, b):
    return (a.astype(F32) + b.astype(F32)).astype(BF16)


class Scatter:
    def __init__(self, first_kept, first_sent, second_kept, second_sent):
        narrow = list(reversed(bits_of(lax.axis_size("narrow"))))
        self.orders = [narrow, narrow[::-1]]
        self.left = [list(narrow), list(narrow)]
        self.front = list(bits_of(lax.axis_size("wide")))[1:]
        self.stage = 0
        self.stages = len(narrow) + len(self.front)
        self.kept, self.pending = [], []
        sides = ((first_kept, first_sent), (second_kept, second_sent))
        for part, (kept, sent) in enumerate(sides):
            bit = self.orders[part][0]
            self.left[part].remove(bit)
            self.kept.append(kept.reshape([2] * (len(narrow) - 1) + list(kept.shape[1:])))
            self.pending.append(swap(sent.reshape(self.kept[-1].shape), "narrow", bit))

    def take(self, got):
        kept, narrow = self.kept, len(self.orders[0])
        self.stage += 1
        if self.stage < narrow:
            self.kept, self.pending = [], []
            for part, order in enumerate(self.orders):
                bit = order[self.stage]
                dim = self.left[part].index(bit)
                self.left[part].remove(bit)
                stay, go = [
                    plus(
                        lax.index_in_dim(kept[part], side, dim, False),
                        lax.index_in_dim(got[part], side, dim, False),
                    )
                    for side in (0, 1)
                ]
                self.kept.append(stay)
                self.pending.append(swap(go, "narrow", bit))
        elif self.stage < self.stages:
            bit = self.front[self.stage - narrow]
            mine = my_bit("wide", bit)
            dim = len(self.front) - 1 - (self.stage - narrow)
            sides = []
            for side in (mine, 1 - mine):
                blocks = []
                for a, b in zip(kept, got):
                    if self.stage == narrow:
                        shape = [2] * len(self.front) + list(a.shape[1:])
                        a, b = a.reshape(shape), b.reshape(shape)
                    blocks.append(
                        plus(
                            lax.dynamic_index_in_dim(a, side, dim, False),
                            lax.dynamic_index_in_dim(b, side, dim, False),
                        )
                    )
                sides.append(jnp.concatenate(blocks, axis=-2) if len(blocks) > 1 else blocks[0])
            self.kept = [sides[0]]
            self.pending = [swap(sides[1], "wide", bit)]
        else:
            self.result = kept[0].astype(F32) + got[0].astype(F32)
            self.pending = []


def spread(block, axis, bits):
    blocks = [block]
    for index in range(1, 1 << len(bits)):
        mask = sum(bit for j, bit in enumerate(bits) if index >> j & 1)
        blocks.append(swap(block, axis, mask))
    return blocks


def tree_sum(blocks):
    while len(blocks) > 1:
        blocks = [blocks[i] + blocks[i + 1] for i in range(0, len(blocks), 2)]
    return blocks[0]


def unpack_call(span_clip, narrow_me, clips, blocks, grad):
    spans = span_clip.shape[0]
    rows, width = grad.shape
    span = rows // spans
    groups = sum(block.shape[0] for block in blocks)
    height, part = blocks[0].shape[1:]
    at = 6 * clips
    units = (height - at - 4) * part
    wide = lax.axis_size("wide")
    outs = [
        shape_of((spans, 6, width), F32),
        shape_of((2, 1, width), F32),
        shape_of((groups, 1, 3 * part), F32),
        shape_of((groups, 1, units), F32),
        shape_of((rows, width), BF16),
        shape_of((1, width), F32),
        shape_of((wide // 2, width // wide, rows), BF16),
        shape_of((wide // 2, width // wide, rows), BF16),
    ]

    def kernel(clip_ref, me_ref, *refs):
        block_refs, grad_ref = refs[: len(blocks)], refs[len(blocks)]
        modes_ref, bias_ref, qkv_ref, up_ref, core_ref, sum_ref, own_ref, other_ref = refs[len(blocks) + 1 :]
        places = [(ref, i) for ref, block in zip(block_refs, blocks) for i in range(block.shape[0])]
        for rel, (ref, i) in enumerate(places):
            owner = me_ref[0] ^ rel
            found = []
            for s in range(spans):
                for k in range(6):
                    found.append(ref[i, pl.ds(k * clips + clip_ref[s], 1), :])
            for n in range(groups):

                @pl.when(owner == n)
                def _():
                    lanes = slice(n * part, (n + 1) * part)
                    for s in range(spans):
                        for k in range(6):
                            modes_ref[s, k : k + 1, lanes] = found[6 * s + k]
                    for k in range(2):
                        bias_ref[k, :, lanes] = ref[i, at + 2 + k : at + 3 + k, :]

            qkv_ref[rel] = jnp.concatenate(
                [ref[i, at : at + 1, :], jnp.zeros((1, part), F32), ref[i, at + 1 : at + 2, :]], axis=1
            )
            for j in range(units // part):
                up_ref[rel, :, j * part : (j + 1) * part] = ref[i, at + 4 + j : at + 5 + j, :]
        for s in range(spans):
            lines = slice(s * span, (s + 1) * span)
            gated = modes_ref[s, 5:6] * grad_ref[lines, :].astype(F32)
            core_ref[lines, :] = gated.astype(BF16)
            here = jnp.sum(gated, axis=0, keepdims=True)
            sum_ref[...] = here if s == 0 else sum_ref[...] + here
        put_turned(width // wide, me_ref[1] & 1, core_ref[...], own_ref, other_ref)

    me = jnp.stack([narrow_me, lax.axis_index("wide")]).astype(jnp.int32)
    return pl.pallas_call(
        kernel,
        grid_spec=pltpu.PrefetchScalarGridSpec(
            num_scalar_prefetch=2,
            grid=(1,),
            in_specs=[whole(a) for a in (*blocks, grad)],
            out_specs=[whole(a) for a in outs],
        ),
        out_shape=outs,
        compiler_params=params(32),
        cost_estimate=cost(),
        name="unpack",
    )(span_clip, me, *blocks, grad)


def pack_call(span_clip, narrow_me, clips, sums_a, sums_b, sums_g, merge_bias, down_bias, qkv_sums, up_bias):
    spans, unused, width = sums_a.shape
    groups = qkv_sums.shape[0]
    part, units = width // groups, up_bias.shape[2]
    at = 6 * clips
    height = at + 4 + units // part
    outs = [shape_of((groups // 2, height, part), F32)] * 2
    ins = [sums_a, sums_b, sums_g, merge_bias, down_bias, qkv_sums, up_bias]

    def kernel(clip_ref, me_ref, a_ref, b_ref, g_ref, merge_ref, down_ref, qkv_ref, up_ref, *refs):
        total = refs[2]
        out_refs = [refs[rel // (groups // 2)].at[rel % (groups // 2)] for rel in range(groups)]
        total[...] = jnp.zeros_like(total)
        for s in range(spans):
            rows = [a_ref[s, 0:1], a_ref[s, 1:2]] + [b_ref[s, i : i + 1] for i in range(3)]
            rows.append(g_ref[s, 0:1])
            for k in range(6):
                row = pl.ds(k * clips + clip_ref[s], 1)
                total[row, :] += rows[k]
        total[at : at + 1, :] = merge_ref[...]
        total[at + 1 : at + 2, :] = down_ref[...]
        for rel in range(groups):
            owner = me_ref[0] ^ rel
            for n in range(groups):

                @pl.when(owner == n)
                def _():
                    own = total[:, n * part : (n + 1) * part]
                    out_refs[rel][:at, :] = own[:at]
                    out_refs[rel][at + 2 : at + 4, :] = own[at : at + 2]

            out_refs[rel][at : at + 1, :] = qkv_ref[rel, :, :part]
            out_refs[rel][at + 1 : at + 2, :] = qkv_ref[rel, :, 2 * part :]
            for j in range(units // part):
                out_refs[rel][at + 4 + j : at + 5 + j, :] = up_ref[rel, :, j * part : (j + 1) * part]

    return pl.pallas_call(
        kernel,
        grid_spec=pltpu.PrefetchScalarGridSpec(
            num_scalar_prefetch=2,
            grid=(1,),
            in_specs=[whole(a) for a in ins],
            out_specs=[whole(a) for a in outs],
            scratch_shapes=[pltpu.VMEM((at + 8, width), F32)],
        ),
        out_shape=outs,
        compiler_params=params(16),
        name="pack",
    )(span_clip, narrow_me.astype(jnp.int32)[None], *ins)


def sum_over(block, axis):
    for bit in bits_of(lax.axis_size(axis)):
        block = block + swap(block, axis, bit)
    return block


def collect(block, axis):
    block = block[None]
    for bit in bits_of(lax.axis_size(axis)):
        block = jnp.concatenate([block, swap(block, axis, bit)], axis=0)
    return block


def turned(block, axis):
    count = lax.axis_size(axis)
    bits = bits_of(count)
    rest = block.shape[1:]
    block = block.reshape([2] * len(bits) + list(rest))
    for dim, bit in enumerate(reversed(bits)):
        block = jnp.where(my_bit(axis, bit) == 1, jnp.flip(block, dim), block)
    return block.reshape((count,) + rest)


def share(block, count):
    for bit in bits_of(count):
        groups, rows, cols = block.shape
        pair = block.reshape(groups // 2, 2, rows, cols)
        kept, got = pair[:, 0], swap(pair[:, 1], "narrow", bit)
        mine = my_bit("narrow", bit) == 1
        block = jnp.concatenate([jnp.where(mine, got, kept), jnp.where(mine, kept, got)], axis=1)
    return block


def unshare(block, count):
    for bit in reversed(bits_of(count)):
        groups, rows, cols = block.shape
        pair = block.reshape(groups, 2, rows // 2, cols)
        mine = my_bit("narrow", bit)
        kept = lax.dynamic_index_in_dim(pair, mine, 1, True)
        got = swap(lax.dynamic_index_in_dim(pair, 1 - mine, 1, True), "narrow", bit)
        block = jnp.concatenate([kept, got], axis=1).reshape(2 * groups, rows // 2, cols)
    return block


def shards(
    tokens,
    condition,
    frame_clip,
    mod_weight,
    mod_bias,
    project_weight,
    project_bias,
    merge_weight,
    merge_bias,
    up_weight,
    up_bias,
    down_weight,
    down_bias,
    out_cotangent,
):
    rows, width = tokens.shape
    wide_count, narrow_count = lax.axis_size("wide"), lax.axis_size("narrow")
    wide_me, narrow_me = lax.axis_index("wide"), lax.axis_index("narrow")
    depth = width // wide_count
    part = width // narrow_count
    units = up_weight.shape[1]
    heads = part // HEAD
    clips = condition.shape[0]
    span = math.gcd(rows, PATCHES)
    spans = rows // span
    sharing = PATCHES // span

    def twin(*blocks):
        return Sent(*[swap(block, "wide", 1) for block in blocks])

    def hop(block, axis, bit):
        return Sent(swap(block, axis, bit))

    attn = Gather(
        jnp.concatenate([project_weight.reshape(depth, 3 * part), merge_weight.T], axis=1), 0, depth
    )
    up, down = Gather(up_weight, 0, depth), Gather(down_weight.T, 0, depth)
    attn.start()
    z_bits = bits_of(wide_count)[1:]
    narrow_bits = bits_of(narrow_count)
    active = jax.nn.silu(condition).astype(BF16)
    active_mine = lax.dynamic_slice_in_dim(active, wide_me * depth, depth, 1)
    mode_part = jnp.einsum("cd,dki->kci", active_mine, mod_weight, preferred_element_type=F32)
    mode_part = mode_part + swap(mode_part, "wide", 1)
    for bit in z_bits:
        sent = hop(mode_part, "wide", bit)
        if bit == z_bits[0]:
            (mode_part,) = land([sent, attn], mode_part)
        else:
            mode_part, *attn.parts = land([sent], mode_part, *attn.parts)
        mode_part = mode_part + sent.got[0]
    unit_rows = units // part
    at = 6 * clips
    small = jnp.concatenate(
        [
            (mode_part + mod_bias.astype(F32)[:, None]).reshape(at, part),
            project_bias.astype(F32),
            merge_bias.astype(F32)[None],
            down_bias.astype(F32)[None],
            up_bias.astype(F32).reshape(unit_rows, part),
        ],
        axis=0,
    )
    span_frame = (narrow_me * rows + jnp.arange(spans, dtype=jnp.int32) * span) // PATCHES
    span_clip = jnp.sum(
        jnp.where(
            span_frame[:, None] == jnp.arange(frame_clip.shape[0], dtype=jnp.int32)[None],
            frame_clip[None],
            0,
        ),
        axis=1,
    )
    attn.start()
    sent = Sent(*spread(small, "narrow", narrow_bits)[1:])
    small, span_clip, *up.parts = land([sent, attn], small, span_clip, *up.parts)
    while attn.stage < len(attn.front):
        attn.start()
        land([attn])
    attn.start()
    up.start()
    modes, out_bias, qkv_bias, up_bias_all, core_grad, down_bias_grad, core_own, core_other = unpack_call(
        span_clip, narrow_me, clips, [block[None] for block in (small, *sent.got)], out_cotangent
    )
    (modes,) = land([attn, up], modes)
    while attn.stage < attn.stages - 1:
        attn.start()
        up.start()
        land([attn, up])
    attn.start()
    if up.stage < len(up.front):
        up.start()
    attn_near = attn.across()
    modes, *down.parts = land([attn, up, attn_near], modes, *down.parts)
    while up.stage < len(up.front):
        up.start()
        land([up])
    attn_far = attn.across()
    up.start()
    down.start()
    (modes,) = land([attn_far], modes)
    attn.finish()

    attn_w = Weight(attn)
    hidden_a, qkv, merge_w = project_call(attn_w, tokens, modes, qkv_bias, part)
    qkv, hidden_a = land([up, down], qkv, hidden_a)
    while up.stage < up.stages - 1:
        up.start()
        (qkv,) = land([up], qkv)
    up.start()
    down.start()
    up_near = up.across()
    qkv_frames = share(qkv, sharing)
    attended = attend(qkv_frames, heads)
    if sharing > 1:
        attended = attended.reshape(rows * sharing, narrow_count // sharing, part)
        attended = unshare(attended.transpose(1, 0, 2), sharing)
        attended = attended.transpose(1, 0, 2).reshape(rows, width)
    attended, hidden_a = land([down, up_near], attended, hidden_a)
    while down.stage < len(down.front):
        down.start()
        (attended,) = land([down], attended)
    down.start()
    hidden_own, hidden_other = turn(hidden_a)
    hidden_twin = twin(hidden_other)
    branch_a, hidden_b = merge_call(attended, merge_w, tokens, modes, out_bias[0])
    hidden_b, attended = land([up, down, hidden_twin], hidden_b, attended)
    while down.stage < down.stages - 1:
        down.start()
        (hidden_b,) = land([down], hidden_b)
    up_far = up.across()
    down.start()
    (hidden_b,) = land([up_far], hidden_b)
    up.finish()
    down_near = down.across()
    up_w = Weight(up)
    gelu, slope = up_call(up_w, hidden_b, up_bias_all)

    gelu, slope, hidden_b = land([down, down_near], gelu, slope, hidden_b)
    down_far = down.across()
    sent_parts = weight_grad_call([core_other], [gelu], [], [], units, 0, depth)
    slope, core_own, *sent_parts = land([down_far], slope, core_own, *sent_parts)
    down.finish()
    down_cross = twin(*sent_parts)
    kept_parts = weight_grad_call([core_own], [gelu], [], [], units, 0, depth)
    slope, hidden_b, *kept_parts = land([], slope, hidden_b, *kept_parts)
    hidden_b_own, hidden_b_other = turn(hidden_b)
    hidden_b_twin = twin(hidden_b_other)
    down_w = Weight(down)
    upper_grad, up_bias_grad = gelu_back_call(down_w, core_grad, slope)
    upper_grad, attended, *kept_parts = land(
        [down_cross, hidden_b_twin], upper_grad, attended, *kept_parts
    )
    upper_twin = twin(upper_grad)
    attended_twin = twin(attended)
    down_scatter = Scatter(*[plus(a, b) for a, b in zip(kept_parts, down_cross.got)])
    middle_grad, merged_grad, sums_b, merge_bias_grad = up_back_call(
        up_w, upper_grad, tokens, branch_a, modes, out_cotangent
    )
    merged_grad, upper_grad = land([upper_twin, attended_twin], merged_grad, upper_grad)
    merged_own, merged_other = turn(merged_grad)
    merged_twin = twin(merged_other)
    up_parts = weight_grad_call(
        [hidden_b_own, hidden_b_twin.got[0]], [upper_grad, upper_twin.got[0]], [], [], units, 0, depth
    )
    merged_grad, *up_parts = land([down_scatter, merged_twin], merged_grad, *up_parts)
    up_scatter = Scatter(*up_parts)

    attended_grad = jnp.dot(merged_grad, merge_w, preferred_element_type=F32).astype(BF16)
    if sharing > 1:
        attended_grad = attended_grad.reshape(rows, narrow_count, part).transpose(1, 0, 2)
        attended_grad = share(attended_grad, sharing).transpose(1, 0, 2)
        attended_grad = attended_grad.reshape(rows * sharing, width // sharing)
    qkv_grads, qkv_twins = [], []
    frames = rows * sharing // PATCHES
    for frame in range(frames):
        qkv_grad = attend_back(qkv_frames, attended_grad, heads, frame)
        scatters = [down_scatter] if frame == frames - 1 else []
        qkv_grad, attended_grad = land(scatters, qkv_grad, attended_grad)
        qkv_grads.append(qkv_grad)
        if sharing == 1:
            qkv_twins.append(twin(qkv_grad))
    if sharing > 1:
        qkv_grads = [unshare(jnp.concatenate(qkv_grads, axis=1), sharing)]
        qkv_twins = [twin(qkv_grads[0])]
    tokens_grad, sums_a, qkv_sums = project_back_call(
        attn_w, qkv_grads, tokens, middle_grad, modes, 3 * part
    )
    sums_a, *qkv_grads = land([up_scatter, down_scatter, *qkv_twins], sums_a, *qkv_grads)
    attn_parts = weight_grad_call(
        [hidden_own, hidden_twin.got[0]],
        qkv_grads + [sent.got[0] for sent in qkv_twins],
        [merged_own, merged_twin.got[0]],
        [attended, attended_twin.got[0]],
        3 * part,
        0,
        depth,
    )
    gelu, *attn_parts = land([up_scatter, down_scatter], gelu, *attn_parts)
    attn_scatter = Scatter(*attn_parts)
    output, sums_g = down_call(
        down_w, gelu, tokens, branch_a, modes, out_bias[1], out_cotangent
    )
    (sums_g,) = land([up_scatter], sums_g)

    lower, upper = pack_call(
        span_clip, narrow_me, clips, sums_a, sums_b, sums_g, merge_bias_grad, down_bias_grad,
        qkv_sums, up_bias_grad,
    )
    sent = hop(upper, "narrow", narrow_bits[-1])
    (lower,) = land([sent, up_scatter], lower)
    packed = lower + sent.got[0]
    for bit in reversed(narrow_bits[:-1]):
        packed = packed[:bit] + swap(packed[bit:], "narrow", bit)
    packed = packed[0]
    sent = hop(packed, "wide", 1)
    (packed,) = land([sent, attn_scatter], packed)
    packed = packed + sent.got[0]
    for bit in z_bits:
        sent = hop(packed, "wide", bit)
        (packed,) = land([sent], packed)
        packed = packed + sent.got[0]
    clip_slice = packed[:at].reshape(6, clips, part)
    active_grad = jnp.einsum(
        "kci,dki->cd", clip_slice, mod_weight.astype(F32), precision=lax.Precision.HIGHEST
    )
    for bit in narrow_bits:
        sent = hop(active_grad, "narrow", bit)
        (active_grad,) = land([sent] + ([attn_scatter] if bit == narrow_bits[-1] else []), active_grad)
        active_grad = active_grad + sent.got[0]
    active_grad = active_grad[None]
    for bit in bits_of(wide_count):
        sent = hop(active_grad, "wide", bit)
        (active_grad,) = land([sent], active_grad)
        active_grad = jnp.concatenate([active_grad, sent.got[0]], axis=0)
    active_grad = turned(active_grad, "wide").transpose(1, 0, 2).reshape(clips, width)
    unused, silu_pullback = jax.vjp(jax.nn.silu, condition)
    condition_grad = silu_pullback(active_grad)[0]
    mod_bias_grad = jnp.sum(clip_slice, axis=1)
    mod_weight_grad = jnp.einsum(
        "cd,kci->dki", active_mine.astype(F32), clip_slice, precision=lax.Precision.HIGHEST
    )

    for scatter in (down_scatter, up_scatter, attn_scatter):
        while scatter.stage < scatter.stages:
            land([scatter])
    attn_grad = attn_scatter.result
    return (
        output,
        tokens_grad,
        condition_grad,
        mod_weight_grad,
        mod_bias_grad,
        attn_grad[:, : 3 * part].reshape(depth, 3, part),
        packed[at : at + 2],
        attn_grad[:, 3 * part :].T,
        packed[at + 2],
        up_scatter.result,
        packed[at + 4 :].reshape(units),
        down_scatter.result.T,
        packed[at + 3],
    )


def solution(mesh):
    both = P(("wide", "narrow"), None)
    ins = (
        both,
        P(),
        P("wide"),
        P("wide", None, "narrow"),
        P(None, "narrow"),
        P("wide", None, "narrow"),
        P(None, "narrow"),
        P("narrow", "wide"),
        P("narrow"),
        P("wide", "narrow"),
        P("narrow"),
        P("narrow", "wide"),
        P("narrow"),
        both,
    )
    outs = (
        both,
        both,
        P(),
        P("wide", None, "narrow"),
        P(None, "narrow"),
        P("wide", None, "narrow"),
        P(None, "narrow"),
        P("narrow", "wide"),
        P("narrow"),
        P("wide", "narrow"),
        P("narrow"),
        P("narrow", "wide"),
        P("narrow"),
    )
    return jax.shard_map(shards, mesh=mesh, in_specs=ins, out_specs=outs, check_vma=False)
```

```python
import functools
import math

import jax
import jax.numpy as jnp
from jax import lax
from jax.experimental import pallas as pl
from jax.experimental.pallas import tpu as pltpu
from jax.sharding import PartitionSpec as P

HEAD = 72
PATCHES = 256
EPSILON = 1e-06
MIB = 1 << 20
F32 = jnp.float32
BF16 = jnp.bfloat16


def bits_of(size):
    return [1 << k for k in range(size.bit_length() - 1)]


def swap(block, axis, bit):
    count = lax.axis_size(axis)
    return lax.ppermute(block, axis, [(i, i ^ bit) for i in range(count)])


def my_bit(axis, bit):
    return (lax.axis_index(axis) // bit) % 2


def tied(*values):
    return lax.optimization_barrier(values)


def dot(a, b, ca, cb):
    return lax.dot_general(a, b, (((ca,), (cb,)), ((), ())), preferred_element_type=F32)


def row_mean(values):
    return jnp.mean(values, axis=1, keepdims=True)


def normalize(values):
    center = row_mean(values)
    inverse = lax.rsqrt(row_mean(values * values) - center * center + EPSILON)
    return inverse, (values - center) * inverse


def norm_back(incoming, normed, inverse):
    return inverse * (incoming - row_mean(incoming) - normed * row_mean(incoming * normed))


def gelu_both(upper):
    c0 = math.sqrt(2.0 / math.pi)
    square = upper * upper
    tanh = jnp.tanh(upper * (c0 + (c0 * 0.044715) * square))
    half = 0.5 + 0.5 * tanh
    bend = (half * (1.0 - half)) * (2.0 * c0 + (2.0 * c0 * 0.134145) * square)
    return upper * half, half + upper * bend


def params(limit=56):
    return pltpu.CompilerParams(vmem_limit_bytes=limit * MIB)


def cost():
    return pl.CostEstimate(flops=1000000000, bytes_accessed=1, transcendentals=0)


def whole(array):
    return pl.BlockSpec(array.shape, lambda i, *_: (0,) * array.ndim)


def along(array):
    return pl.BlockSpec((1,) + array.shape[1:], lambda i, *_: (i,) + (0,) * (array.ndim - 1))


def shape_of(shape, dtype):
    return jax.ShapeDtypeStruct(shape, dtype)


def attend_kernel(heads, qkv_ref, out_ref):
    part = heads * HEAD
    scale = HEAD ** (-0.5)
    results = []
    for n in range(qkv_ref.shape[0]):
        qs, ks, vs = [
            [qkv_ref[n, :, i * part + h * HEAD : i * part + (h + 1) * HEAD] for h in range(heads)]
            for i in range(3)
        ]
        scores = [dot(k, q, 1, 1) for k, q in zip(ks, qs)]
        probs = []
        for s in scores:
            p = jnp.exp((s - jnp.max(s, axis=0, keepdims=True)) * scale)
            probs.append((p.astype(BF16), 1.0 / jnp.sum(p, axis=0, keepdims=True)))
        for (p, weight), v in zip(probs, vs):
            results.append(dot(v, p, 0, 0) * weight)
    out_ref[...] = jnp.concatenate(results, axis=0).T.astype(BF16)


def attend(qkv, heads):
    groups, rows, cols = qkv.shape
    width = groups * heads * HEAD
    out = shape_of((rows, width), BF16)
    return pl.pallas_call(
        functools.partial(attend_kernel, heads),
        grid=(rows // PATCHES,),
        in_specs=[pl.BlockSpec((groups, PATCHES, cols), lambda f: (0, f, 0))],
        out_specs=pl.BlockSpec((PATCHES, width), lambda f: (f, 0)),
        out_shape=out,
        compiler_params=params(),
        cost_estimate=cost(),
        name="attend",
    )(qkv)


def attend_back_kernel(heads, qkv_ref, grad_ref, *refs):
    out_ref = refs[-1]
    part = heads * HEAD
    scale = HEAD ** (-0.5)
    pad = out_ref.shape[2] - 3 * part
    grad = grad_ref[...]
    if len(refs) > 1:
        grad = dot(grad, refs[0][...], 1, 0).astype(BF16)
    for n in range(qkv_ref.shape[0]):
        qs, ks, vs = [
            [qkv_ref[n, :, i * part + h * HEAD : i * part + (h + 1) * HEAD] for h in range(heads)]
            for i in range(3)
        ]
        gs = [grad[:, n * part + h * HEAD : n * part + (h + 1) * HEAD] for h in range(heads)]
        scores = [dot(k, q, 1, 1) for k, q in zip(ks, qs)]
        slopes = [dot(v, g, 1, 1) for v, g in zip(vs, gs)]
        probs, score_grads = [], []
        for s, dp in zip(scores, slopes):
            p = jnp.exp((s - jnp.max(s, axis=0, keepdims=True)) * scale)
            p = p * (1.0 / jnp.sum(p, axis=0, keepdims=True))
            probs.append(p.astype(BF16))
            score_grads.append((p * (dp - jnp.sum(p * dp, axis=0, keepdims=True))).astype(BF16))
        dvs = [dot(p, g, 1, 0) for p, g in zip(probs, gs)]
        dks = [dot(ds, q, 1, 0) * scale for ds, q in zip(score_grads, qs)]
        dqs = [dot(k, ds, 0, 0) * scale for ds, k in zip(score_grads, ks)]
        dq = jnp.concatenate(dqs, axis=0).T
        zeros = [jnp.zeros((PATCHES, pad), F32)] if pad else []
        out_ref[n] = jnp.concatenate([dq] + dks + dvs + zeros, axis=1).astype(BF16)


def attend_back(qkv, grad, heads, weight=None):
    groups, rows, cols = qkv.shape
    width = groups * heads * HEAD
    out = shape_of((groups, rows, -(-cols // 128) * 128), BF16)
    more = [] if weight is None else [weight]
    return pl.pallas_call(
        functools.partial(attend_back_kernel, heads),
        grid=(rows // PATCHES,),
        in_specs=[
            pl.BlockSpec((groups, PATCHES, cols), lambda f: (0, f, 0)),
            pl.BlockSpec((PATCHES, width), lambda f: (f, 0)),
        ]
        + [whole(a) for a in more],
        out_specs=pl.BlockSpec((groups, PATCHES, out.shape[2]), lambda f: (0, f, 0)),
        out_shape=out,
        compiler_params=params(),
        cost_estimate=cost(),
        name="attend_back",
    )(qkv, grad, *more)


class Sent:
    def __init__(self, *values):
        self.pending = list(values)

    def take(self, got):
        self.got = got
        self.pending = []


def land(sents, *ties):
    sents = [sent for sent in sents if sent.pending]
    pending = [value for sent in sents for value in sent.pending]
    values = list(tied(*pending, *ties))
    for sent in sents:
        count = len(sent.pending)
        sent.take(values[:count])
        values = values[count:]
    return values


class Gather:
    def __init__(self, shard):
        self.depth, self.cols = shard.shape
        self.cut = max(16, self.depth // 2 // 16 * 16)
        wide = [("wide", bit) for bit in reversed(bits_of(lax.axis_size("wide")))]
        narrow = [("narrow", bit) for bit in reversed(bits_of(lax.axis_size("narrow")))]
        self.core = wide[-1]
        self.front = wide[:-1] + narrow[:-2]
        self.last = narrow[-2:]
        self.own = shard[None]
        self.stage = 0
        self.pending = []
        self.crossed = {}

    def in_front(self):
        return self.stage < len(self.front)

    def start(self):
        if self.in_front():
            self.pending = [swap(self.own, *self.front[self.stage])]
        elif self.stage == len(self.front):
            self.pending = [swap(self.own, *key) for key in self.last]
        else:
            self.pending = [
                swap(self.first[:, : self.cut], *self.last[1]),
                swap(self.second[:, self.cut :], *self.last[0]),
            ]
        return self

    def take(self, got):
        self.pending = []
        if self.in_front():
            self.own = jnp.concatenate([self.own, got[0]], axis=0)
        elif self.stage == len(self.front):
            self.first, self.second = got
        else:
            self.third, self.fourth = got
        self.stage += 1

    def cross(self, *names):
        sent = Sent(*[swap(getattr(self, name), *self.core) for name in names])
        for i, name in enumerate(names):
            self.crossed[name] = (sent, i)
        return sent

    def finish(self):
        names = ["own", "first", "second", "third", "fourth"]
        self.arrays = [getattr(self, name) for name in names]
        for name in names:
            sent, i = self.crossed[name]
            self.arrays.append(sent.got[i])
        return self

    def entries(self, n):
        found = []
        (unused, high), (unused, low) = self.last
        whole_rows, cut = (0, self.depth), self.cut
        for w in range(lax.axis_size("wide")):
            index = 0
            for j, (axis, bit) in enumerate(self.front):
                index += bool((n if axis == "narrow" else w) & bit) << j
            side = 5 * bool(w & self.core[1])
            if n & high and n & low:
                parts = [(3, 0, cut), (4, cut, self.depth - cut)]
            else:
                parts = [(1 if n & high else 2 if n & low else 0, 0, self.depth)]
            found += [(side + which, index, w, offset, size) for which, offset, size in parts]
        return found

    def assembled(self):
        sides = []
        for side in (0, 5):
            own, first, second, third, fourth = self.arrays[side : side + 5]
            across = jnp.concatenate([third, fourth], axis=1)
            sides.append(jnp.stack([jnp.stack([own, second]), jnp.stack([first, across])]))
        block = jnp.stack(sides)
        keys = [self.core, *self.last, *self.front[::-1]]
        block = block.reshape([2] * len(keys) + [self.depth, self.cols])
        narrow = [("narrow", bit) for bit in reversed(bits_of(lax.axis_size("narrow")))]
        wide = [("wide", bit) for bit in reversed(bits_of(lax.axis_size("wide")))]
        order = [keys.index(key) for key in narrow + wide]
        block = block.transpose(order + [len(keys), len(keys) + 1])
        for dim, key in enumerate(wide):
            dim += len(narrow)
            block = jnp.where(my_bit(*key) == 1, jnp.flip(block, dim), block)
        return block.reshape(lax.axis_size("narrow"), -1, self.cols)


class Weight:
    def __init__(self, gather):
        groups = lax.axis_size("narrow")
        self.depth, self.cols = gather.depth, gather.cols
        if gather.cut % 16 or gather.depth % 16:
            self.arrays = [gather.assembled()]
            self.plan = [[(0, n, None, 0, 0)] for n in range(groups)]
        else:
            self.arrays = gather.arrays
            self.plan = [gather.entries(n) for n in range(groups)]


class Whole:
    def __init__(self, shard):
        self.depth, self.cols = shard.shape
        groups = lax.axis_size("narrow")
        blocks = lax.all_gather(shard, ("narrow", "wide"), axis=0)
        self.blocks = blocks.reshape(groups, lax.axis_size("wide") * self.depth, self.cols)

    def finish(self):
        self.arrays = [self.blocks]
        self.plan = [[(0, n, None, 0, 0)] for n in range(lax.axis_size("narrow"))]
        return self


def stream(step, weight, me, refs, buffer, sems, before):
    plan = weight.plan

    def issue(n):
        for which, index, w, offset, size in plan[n]:
            if w is None:
                target = buffer.at[n % 2]
                if isinstance(weight, Whole):
                    index = me[1] ^ index
            else:
                row = pl.multiple_of((me[0] ^ w) * weight.depth + offset, 16)
                target = buffer.at[n % 2, pl.ds(row, size)]
            pltpu.make_async_copy(refs[which].at[index], target, sems.at[n % 2]).start()

    @pl.when(step == -before)
    def _():
        issue(0)
        pltpu.make_async_copy(buffer.at[0], buffer.at[0], sems.at[0]).wait()
        issue(1)

    for n in range(1, len(plan)):

        @pl.when(step == n)
        def _():
            pltpu.make_async_copy(buffer.at[n % 2], buffer.at[n % 2], sems.at[n % 2]).wait()
            if n + 1 < len(plan):
                issue(n + 1)

    return buffer.at[jnp.clip(step, 0, len(plan) - 1) % 2]


def group_at(array, before, groups):
    def index(i, *_):
        return (jnp.clip(i - before, 0, groups - 1),) + (0,) * (array.ndim - 1)

    return pl.BlockSpec((1,) + array.shape[1:], index)


def rows_at(array, first, spans):
    def index(i, *_):
        return (jnp.clip(i - first, 0, spans - 1),) + (0,) * (array.ndim - 1)

    return pl.BlockSpec((array.shape[0] // spans,) + array.shape[1:], index)


def weight_call(body, weight, ins, in_specs, outs, out_specs, scratch, name, before=0, after=0):
    count, groups = len(weight.arrays), len(weight.plan)
    width = lax.axis_size("wide") * weight.depth

    def kernel(me_ref, *refs):
        step = pl.program_id(0) - before
        in_refs = refs[: len(ins)]
        weight_refs = refs[len(ins) : len(ins) + count]
        out_refs = refs[len(ins) + count : len(ins) + count + len(outs)]
        buffer, sems = refs[len(ins) + count + len(outs) :][:2]
        scratch_refs = refs[len(ins) + count + len(outs) + 2 :]
        w = stream(step, weight, me_ref, weight_refs, buffer, sems, before)
        body(step, in_refs, w, out_refs, scratch_refs)

    me = jnp.stack([lax.axis_index("wide"), lax.axis_index("narrow")]).astype(jnp.int32)
    return pl.pallas_call(
        kernel,
        grid_spec=pltpu.PrefetchScalarGridSpec(
            num_scalar_prefetch=1,
            grid=(before + groups + after,),
            in_specs=list(in_specs) + [pl.BlockSpec(memory_space=pl.ANY)] * count,
            out_specs=list(out_specs),
            scratch_shapes=[
                pltpu.VMEM((2, width, weight.cols), BF16),
                pltpu.SemaphoreType.DMA((2,)),
            ]
            + list(scratch),
        ),
        out_shape=list(outs),
        compiler_params=params(),
        cost_estimate=cost(),
        name=name,
    )(me, *ins, *weight.arrays)


def project_call(weight, tokens, modes, bias, part):
    rows, width = tokens.shape
    spans, span = modes.shape[0], rows // modes.shape[0]
    groups = len(weight.plan)
    outs = [
        shape_of((rows, width), BF16),
        shape_of((groups, rows, 3 * part), BF16),
        shape_of((width, groups * part), BF16),
    ]

    before = spans - 1

    def body(step, ins, w, out, scratch):
        tokens_ref, modes_ref, bias_ref = ins
        hidden_ref, qkv_ref, merge_ref = out
        held = scratch[0]

        @pl.when(step <= 0)
        def _():
            at = pl.ds(pl.multiple_of((step + before) * span, span), span)
            unused, normed = normalize(tokens_ref[...].astype(F32))
            hidden = (normed * (1.0 + modes_ref[0, 1:2]) + modes_ref[0, 0:1]).astype(BF16)
            hidden_ref[...] = hidden
            held[at, :] = hidden
            qkv_ref[0, at, :] = (dot(hidden, w[:, : 3 * part], 1, 0) + bias_ref[0]).astype(BF16)

        @pl.when(step > 0)
        def _():
            qkv_ref[0] = (dot(held[...], w[:, : 3 * part], 1, 0) + bias_ref[0]).astype(BF16)

        for n in range(groups):

            @pl.when(step == n)
            def _():
                merge_ref[:, n * part : (n + 1) * part] = w[:, 3 * part :]

    return weight_call(
        body,
        weight,
        [tokens, modes, bias],
        [rows_at(tokens, 0, spans), rows_at(modes, 0, spans), group_at(bias, before, groups)],
        outs,
        [rows_at(outs[0], 0, spans), group_at(outs[1], before, groups), whole(outs[2])],
        [pltpu.VMEM((rows, width), BF16)],
        "project",
        before=before,
    )


def merge_kernel(attended_ref, weight_ref, tokens_ref, modes_ref, bias_ref, branch_ref, hidden_ref):
    branch = dot(attended_ref[...], weight_ref[...], 1, 1) + bias_ref[...]
    branch_ref[...] = branch
    middle = tokens_ref[...].astype(F32) + modes_ref[0, 2:3] * branch
    unused, normed = normalize(middle)
    hidden_ref[...] = (normed * (1.0 + modes_ref[0, 4:5]) + modes_ref[0, 3:4]).astype(BF16)


def merge_call(attended, weight, tokens, modes, bias):
    rows, width = tokens.shape
    spans, span = modes.shape[0], rows // modes.shape[0]
    block = pl.BlockSpec((span, width), lambda i: (i, 0))
    outs = [shape_of((rows, width), F32), shape_of((rows, width), BF16)]
    return pl.pallas_call(
        merge_kernel,
        grid=(spans,),
        in_specs=[block, whole(weight), block, along(modes), whole(bias)],
        out_specs=[block, block],
        out_shape=outs,
        compiler_params=params(),
        cost_estimate=cost(),
        name="merge",
    )(attended, weight, tokens, modes, bias)


def up_call(weight, hidden, bias, left):
    rows, width = hidden.shape
    groups, units = len(weight.plan), weight.cols
    zs, depth = left.shape[:2]
    outs = [shape_of((groups, rows, units), BF16)] * 2 + [shape_of((groups, zs, depth, units), BF16)]

    def body(step, ins, w, out, scratch):
        hidden_ref, bias_ref, left_ref = ins
        gelu, slope = gelu_both(dot(hidden_ref[...], w[...], 1, 0) + bias_ref[0])
        gelu = gelu.astype(BF16)
        out[0][0] = gelu
        out[1][0] = slope.astype(BF16)
        part = dot(left_ref[...].reshape(zs * depth, rows), gelu, 1, 0)
        out[2][0] = part.astype(BF16).reshape(zs, depth, units)

    return weight_call(
        body,
        weight,
        [hidden, bias, left],
        [whole(hidden), along(bias), whole(left)],
        outs,
        [along(out) for out in outs],
        [],
        "up",
    )


def down_call(weight, gelu, tokens, branch, modes, bias, grad):
    rows, width = tokens.shape
    spans, span = modes.shape[0], rows // modes.shape[0]
    groups, units = len(weight.plan), weight.cols
    outs = [shape_of((rows, width), BF16), shape_of((spans, 1, width), F32)]

    def body(step, ins, w, out, scratch):
        gelu_ref, tokens_ref, branch_ref, modes_ref, bias_ref, grad_ref = ins
        total = scratch[0]

        @pl.when(step == 0)
        def _():
            total[...] = dot(gelu_ref[0], w[...], 1, 1)

        @pl.when((step > 0) & (step < groups - 1))
        def _():
            total[...] += dot(gelu_ref[0], w[...], 1, 1)

        @pl.when(step >= groups - 1)
        def _():
            at = pl.ds(pl.multiple_of((step - groups + 1) * span, span), span)
            other = total[at, :] + dot(gelu_ref[0, at, :], w[...], 1, 1) + bias_ref[...]
            middle = tokens_ref[...].astype(F32) + modes_ref[0, 2:3] * branch_ref[...]
            out[0][...] = (middle + modes_ref[0, 5:6] * other).astype(BF16)
            out[1][0] = jnp.sum(grad_ref[...].astype(F32) * other, axis=0, keepdims=True)

    def by_span(array):
        return rows_at(array, groups - 1, spans)

    return weight_call(
        body,
        weight,
        [gelu, tokens, branch, modes, bias, grad],
        [group_at(gelu, 0, groups), by_span(tokens), by_span(branch), by_span(modes), whole(bias), by_span(grad)],
        outs,
        [by_span(outs[0]), by_span(outs[1])],
        [pltpu.VMEM((rows, width), F32)],
        "down",
        after=spans - 1,
    )


def gelu_back_call(weight, grad, slope, left):
    rows, width = grad.shape
    groups, units = len(weight.plan), weight.cols
    zs, depth = left.shape[:2]
    outs = [
        shape_of((groups, rows, units), BF16),
        shape_of((groups, 1, units), F32),
        shape_of((groups, zs, depth, units), BF16),
    ]

    def body(step, ins, w, out, scratch):
        grad_ref, slope_ref, left_ref = ins
        upper = (dot(grad_ref[...], w[...], 1, 0) * slope_ref[0].astype(F32)).astype(BF16)
        out[0][0] = upper
        out[1][0] = jnp.sum(upper.astype(F32), axis=0, keepdims=True)
        part = dot(left_ref[...].reshape(zs * depth, rows), upper, 1, 0)
        out[2][0] = part.astype(BF16).reshape(zs, depth, units)

    return weight_call(
        body,
        weight,
        [grad, slope, left],
        [whole(grad), along(slope), whole(left)],
        outs,
        [along(out) for out in outs],
        [],
        "gelu_back",
    )


def up_back_call(weight, upper, tokens, branch, modes, grad):
    rows, width = tokens.shape
    spans, span = modes.shape[0], rows // modes.shape[0]
    groups, units = len(weight.plan), weight.cols
    outs = [
        shape_of((rows, width), F32),
        shape_of((rows, width), BF16),
        shape_of((spans, 3, width), F32),
        shape_of((1, width), F32),
    ]

    def body(step, ins, w, out, scratch):
        upper_ref, tokens_ref, branch_ref, modes_ref, grad_ref = ins
        middle_ref, merged_ref, sums_ref, bias_ref = out
        total = scratch[0]

        @pl.when(step == 0)
        def _():
            total[...] = dot(upper_ref[0], w[...], 1, 1)
            bias_ref[...] = jnp.zeros_like(bias_ref)

        @pl.when((step > 0) & (step < groups - 1))
        def _():
            total[...] += dot(upper_ref[0], w[...], 1, 1)

        @pl.when(step >= groups - 1)
        def _():
            at = pl.ds(pl.multiple_of((step - groups + 1) * span, span), span)
            hidden = total[at, :] + dot(upper_ref[0, at, :], w[...], 1, 1)
            branch = branch_ref[...]
            gate = modes_ref[0, 2:3]
            inverse, normed = normalize(tokens_ref[...].astype(F32) + gate * branch)
            back = norm_back(hidden * (1.0 + modes_ref[0, 4:5]), normed, inverse)
            middle = grad_ref[...].astype(F32) + back
            gated = gate * middle
            middle_ref[...] = middle
            merged_ref[...] = gated.astype(BF16)
            sums_ref[0, 0:1] = jnp.sum(middle * branch, axis=0, keepdims=True)
            sums_ref[0, 1:2] = jnp.sum(hidden, axis=0, keepdims=True)
            sums_ref[0, 2:3] = jnp.sum(hidden * normed, axis=0, keepdims=True)
            bias_ref[...] += jnp.sum(gated, axis=0, keepdims=True)

    def by_span(array):
        return rows_at(array, groups - 1, spans)

    return weight_call(
        body,
        weight,
        [upper, tokens, branch, modes, grad],
        [group_at(upper, 0, groups)] + [by_span(a) for a in (tokens, branch, modes, grad)],
        outs,
        [by_span(a) for a in outs[:3]] + [whole(outs[3])],
        [pltpu.VMEM((rows, width), F32)],
        "up_back",
        after=spans - 1,
    )


def project_back_call(weight, qkv_grad, tokens, middle, modes, cols):
    rows, width = tokens.shape
    spans, span = modes.shape[0], rows // modes.shape[0]
    groups = len(weight.plan)
    outs = [
        shape_of((rows, width), F32),
        shape_of((spans, 2, width), F32),
        shape_of((groups, 1, cols), F32),
    ]

    def body(step, ins, w, out, scratch):
        grad_ref, tokens_ref, middle_ref, modes_ref = ins
        tokens_grad_ref, sums_ref, bias_ref = out
        total = scratch[0]

        @pl.when(step < groups)
        def _():
            bias_ref[0] = jnp.sum(grad_ref[0, :, :cols].astype(F32), axis=0, keepdims=True)

        @pl.when(step == 0)
        def _():
            total[...] = dot(grad_ref[0, :, :cols], w[:, :cols], 1, 1)

        @pl.when((step > 0) & (step < groups - 1))
        def _():
            total[...] += dot(grad_ref[0, :, :cols], w[:, :cols], 1, 1)

        @pl.when(step >= groups - 1)
        def _():
            at = pl.ds(pl.multiple_of((step - groups + 1) * span, span), span)
            inverse, normed = normalize(tokens_ref[...].astype(F32))
            hidden = total[at, :] + dot(grad_ref[0, at, :cols], w[:, :cols], 1, 1)
            back = norm_back(hidden * (1.0 + modes_ref[0, 1:2]), normed, inverse)
            tokens_grad_ref[...] = middle_ref[...] + back
            sums_ref[0, 0:1] = jnp.sum(hidden, axis=0, keepdims=True)
            sums_ref[0, 1:2] = jnp.sum(hidden * normed, axis=0, keepdims=True)

    def by_span(array):
        return rows_at(array, groups - 1, spans)

    return weight_call(
        body,
        weight,
        [qkv_grad, tokens, middle, modes],
        [group_at(qkv_grad, 0, groups)] + [by_span(a) for a in (tokens, middle, modes)],
        outs,
        [by_span(outs[0]), by_span(outs[1]), group_at(outs[2], 0, groups)],
        [pltpu.VMEM((rows, width), F32)],
        "project_back",
        after=spans - 1,
    )


def put_turned(depth, side, block, own_ref, other_ref):
    turned_block = block.T
    for z in range(own_ref.shape[0]):
        even = turned_block[2 * z * depth : (2 * z + 1) * depth]
        odd = turned_block[(2 * z + 1) * depth : (2 * z + 2) * depth]
        own_ref[z] = jnp.where(side == 1, odd, even)
        other_ref[z] = jnp.where(side == 1, even, odd)


def turn_kernel(depth, me_ref, block_ref, own_ref, other_ref):
    put_turned(depth, me_ref[0] & 1, block_ref[...], own_ref, other_ref)


def turn(block):
    rows, width = block.shape
    blocks = lax.axis_size("wide")
    out = shape_of((blocks // 2, width // blocks, rows), BF16)
    me = lax.axis_index("wide").astype(jnp.int32)[None]
    own, other = pl.pallas_call(
        functools.partial(turn_kernel, width // blocks),
        grid_spec=pltpu.PrefetchScalarGridSpec(
            num_scalar_prefetch=1, grid=(1,), in_specs=[whole(block)], out_specs=[whole(out)] * 2
        ),
        out_shape=[out, out],
        compiler_params=params(24),
        cost_estimate=cost(),
        name="turn",
    )(me, block)
    return own, other


def weight_grad_call(lefts, grads, merged, attended, cols, added=None):
    zs, size, rows = lefts[0].shape
    groups = grads[0].shape[0]
    width = 2 * zs * size
    cut = max(16, size // 2 // 16 * 16)
    part = width // groups if merged else 0
    half = groups // 2
    outs = []
    for height in (cut, cut, size - cut, size - cut):
        outs.append(shape_of((half, zs, height, cols + part), BF16))
    more = [] if added is None else [added]
    ins = [*lefts, *grads, *more, *merged, *attended]
    count = len(lefts)

    def product(left_refs, right_refs):
        terms = [
            dot(left[...].reshape(zs * size, rows), right, 1, 0)
            for left, right in zip(left_refs, right_refs)
        ]
        return sum(terms[1:], terms[0])

    def kernel(*refs):
        step = pl.program_id(0)
        left_refs, grad_refs, rest = refs[:count], refs[count : 2 * count], refs[2 * count : len(ins)]
        out_refs, scratch = refs[len(ins) : len(ins) + 4], refs[len(ins) + 4 :]
        result = product(left_refs, [ref[0, :, :cols] for ref in grad_refs])
        if more:
            result = result + rest[0][0].reshape(zs * size, cols).astype(F32)
        result = result.astype(BF16)
        if merged:

            @pl.when(step == 0)
            def _():
                pairs = rest[len(more) :]
                values = [ref[...] for ref in pairs[len(merged) :]]
                scratch[0][...] = product(pairs[: len(merged)], values).astype(BF16)

        for n in range(groups):

            @pl.when(step == n)
            def _():
                value = result
                if merged:
                    value = jnp.concatenate([value, scratch[0][:, n * part : (n + 1) * part]], axis=1)
                first = out_refs[0] if n < half else out_refs[1]
                second = out_refs[2] if n % 2 == 0 else out_refs[3]
                for z in range(zs):
                    first[0, z] = value[z * size : z * size + cut]
                    second[0, z] = value[z * size + cut : (z + 1) * size]

    rest = (0, 0, 0)
    out_specs = [
        pl.BlockSpec((1,) + out.shape[1:], index)
        for out, index in zip(
            outs,
            [
                lambda i: (jnp.minimum(i, half - 1),) + rest,
                lambda i: (jnp.maximum(i - half, 0),) + rest,
                lambda i: (i // 2,) + rest,
                lambda i: (i // 2,) + rest,
            ],
        )
    ]
    return pl.pallas_call(
        kernel,
        grid=(groups,),
        in_specs=[whole(a) for a in lefts]
        + [along(a) for a in (*grads, *more)]
        + [whole(a) for a in (*merged, *attended)],
        out_specs=out_specs,
        scratch_shapes=[pltpu.VMEM((zs * size, width), BF16)] if merged else [],
        out_shape=outs,
        compiler_params=params(),
        cost_estimate=cost(),
        name="weight_grad",
    )(*ins)


def plus(a, b):
    return (a.astype(F32) + b.astype(F32)).astype(BF16)


class Scatter:
    def __init__(self, first_kept, first_sent, second_kept, second_sent):
        narrow = list(reversed(bits_of(lax.axis_size("narrow"))))
        self.orders = [narrow, narrow[::-1]]
        self.left = [list(narrow), list(narrow)]
        self.front = list(bits_of(lax.axis_size("wide")))[1:]
        self.stage = 0
        self.stages = len(narrow) + len(self.front)
        self.kept, self.pending = [], []
        sides = ((first_kept, first_sent), (second_kept, second_sent))
        for part, (kept, sent) in enumerate(sides):
            bit = self.orders[part][0]
            self.left[part].remove(bit)
            self.kept.append(kept.reshape([2] * (len(narrow) - 1) + list(kept.shape[1:])))
            self.pending.append(swap(sent.reshape(self.kept[-1].shape), "narrow", bit))

    def take(self, got):
        self.got = list(got)
        self.go()

    def wait(self):
        sent = Sent(*self.pending)
        sent.take = lambda got: setattr(self, "got", list(got))
        self.pending = []
        return sent

    def go(self):
        kept, got, narrow = self.kept, self.got, len(self.orders[0])
        self.stage += 1
        if self.stage < narrow:
            self.kept, self.pending = [], []
            for part, order in enumerate(self.orders):
                bit = order[self.stage]
                dim = self.left[part].index(bit)
                self.left[part].remove(bit)
                stay, go = [
                    plus(
                        lax.index_in_dim(kept[part], side, dim, False),
                        lax.index_in_dim(got[part], side, dim, False),
                    )
                    for side in (0, 1)
                ]
                self.kept.append(stay)
                self.pending.append(swap(go, "narrow", bit))
        elif self.stage < self.stages:
            bit = self.front[self.stage - narrow]
            mine = my_bit("wide", bit)
            dim = len(self.front) - 1 - (self.stage - narrow)
            sides = []
            for side in (mine, 1 - mine):
                blocks = []
                for a, b in zip(kept, got):
                    if self.stage == narrow:
                        shape = [2] * len(self.front) + list(a.shape[1:])
                        a, b = a.reshape(shape), b.reshape(shape)
                    blocks.append(
                        plus(
                            lax.dynamic_index_in_dim(a, side, dim, False),
                            lax.dynamic_index_in_dim(b, side, dim, False),
                        )
                    )
                sides.append(jnp.concatenate(blocks, axis=-2) if len(blocks) > 1 else blocks[0])
            self.kept = [sides[0]]
            self.pending = [swap(sides[1], "wide", bit)]
        else:
            self.result = kept[0].astype(F32) + got[0].astype(F32)
            self.pending = []


def spread(block, axis, bits):
    blocks = [block]
    for index in range(1, 1 << len(bits)):
        mask = sum(bit for j, bit in enumerate(bits) if index >> j & 1)
        blocks.append(swap(block, axis, mask))
    return blocks


def tree_sum(blocks):
    while len(blocks) > 1:
        blocks = [blocks[i] + blocks[i + 1] for i in range(0, len(blocks), 2)]
    return blocks[0]


def unpack_call(span_clip, narrow_me, clips, blocks, grad):
    spans = span_clip.shape[0]
    rows, width = grad.shape
    span = rows // spans
    groups = len(blocks)
    height, part = blocks[0].shape
    at = 6 * clips
    units = (height - at - 4) * part
    wide = lax.axis_size("wide")
    outs = [
        shape_of((spans, 6, width), F32),
        shape_of((2, 1, width), F32),
        shape_of((groups, 1, 3 * part), F32),
        shape_of((groups, 1, units), F32),
        shape_of((rows, width), BF16),
        shape_of((1, width), F32),
        shape_of((wide // 2, width // wide, rows), BF16),
        shape_of((wide // 2, width // wide, rows), BF16),
    ]

    def kernel(clip_ref, me_ref, *refs):
        block_refs, grad_ref = refs[: len(blocks)], refs[len(blocks)]
        modes_ref, bias_ref, qkv_ref, up_ref, core_ref, sum_ref, own_ref, other_ref = refs[len(blocks) + 1 :]
        for rel, ref in enumerate(block_refs):
            owner = me_ref[0] ^ rel
            found = []
            for s in range(spans):
                for k in range(6):
                    found.append(ref[pl.ds(k * clips + clip_ref[s], 1), :])
            for n in range(groups):

                @pl.when(owner == n)
                def _():
                    lanes = slice(n * part, (n + 1) * part)
                    for s in range(spans):
                        for k in range(6):
                            modes_ref[s, k : k + 1, lanes] = found[6 * s + k]
                    for k in range(2):
                        bias_ref[k, :, lanes] = ref[at + 2 + k : at + 3 + k, :]

            qkv_ref[rel] = jnp.concatenate(
                [ref[at : at + 1, :], jnp.zeros((1, part), F32), ref[at + 1 : at + 2, :]], axis=1
            )
            for j in range(units // part):
                up_ref[rel, :, j * part : (j + 1) * part] = ref[at + 4 + j : at + 5 + j, :]
        for s in range(spans):
            lines = slice(s * span, (s + 1) * span)
            gated = modes_ref[s, 5:6] * grad_ref[lines, :].astype(F32)
            core_ref[lines, :] = gated.astype(BF16)
            here = jnp.sum(gated, axis=0, keepdims=True)
            sum_ref[...] = here if s == 0 else sum_ref[...] + here
        put_turned(width // wide, me_ref[1] & 1, core_ref[...], own_ref, other_ref)

    me = jnp.stack([narrow_me, lax.axis_index("wide")]).astype(jnp.int32)
    return pl.pallas_call(
        kernel,
        grid_spec=pltpu.PrefetchScalarGridSpec(
            num_scalar_prefetch=2,
            grid=(1,),
            in_specs=[whole(a) for a in (*blocks, grad)],
            out_specs=[whole(a) for a in outs],
        ),
        out_shape=outs,
        compiler_params=params(32),
        cost_estimate=cost(),
        name="unpack",
    )(span_clip, me, *blocks, grad)


def pack_call(span_clip, narrow_me, clips, sums_a, sums_b, sums_g, merge_bias, down_bias, qkv_sums, up_bias):
    spans, unused, width = sums_a.shape
    groups = qkv_sums.shape[0]
    part, units = width // groups, up_bias.shape[2]
    at = 6 * clips
    height = at + 4 + units // part
    outs = [shape_of((groups // 2, height, part), F32)] * 2
    ins = [sums_a, sums_b, sums_g, merge_bias, down_bias, qkv_sums, up_bias]

    def kernel(clip_ref, me_ref, a_ref, b_ref, g_ref, merge_ref, down_ref, qkv_ref, up_ref, *refs):
        total = refs[2]
        out_refs = [refs[rel // (groups // 2)].at[rel % (groups // 2)] for rel in range(groups)]
        total[...] = jnp.zeros_like(total)
        for s in range(spans):
            rows = [a_ref[s, 0:1], a_ref[s, 1:2]] + [b_ref[s, i : i + 1] for i in range(3)]
            rows.append(g_ref[s, 0:1])
            for k in range(6):
                row = pl.ds(k * clips + clip_ref[s], 1)
                total[row, :] += rows[k]
        total[at : at + 1, :] = merge_ref[...]
        total[at + 1 : at + 2, :] = down_ref[...]
        for rel in range(groups):
            owner = me_ref[0] ^ rel
            for n in range(groups):

                @pl.when(owner == n)
                def _():
                    own = total[:, n * part : (n + 1) * part]
                    out_refs[rel][:at, :] = own[:at]
                    out_refs[rel][at + 2 : at + 4, :] = own[at : at + 2]

            out_refs[rel][at : at + 1, :] = qkv_ref[rel, :, :part]
            out_refs[rel][at + 1 : at + 2, :] = qkv_ref[rel, :, 2 * part :]
            for j in range(units // part):
                out_refs[rel][at + 4 + j : at + 5 + j, :] = up_ref[rel, :, j * part : (j + 1) * part]

    return pl.pallas_call(
        kernel,
        grid_spec=pltpu.PrefetchScalarGridSpec(
            num_scalar_prefetch=2,
            grid=(1,),
            in_specs=[whole(a) for a in ins],
            out_specs=[whole(a) for a in outs],
            scratch_shapes=[pltpu.VMEM((at + 8, width), F32)],
        ),
        out_shape=outs,
        compiler_params=params(16),
        name="pack",
    )(span_clip, narrow_me.astype(jnp.int32)[None], *ins)


def sum_over(block, axis):
    for bit in bits_of(lax.axis_size(axis)):
        block = block + swap(block, axis, bit)
    return block


def collect(block, axis):
    block = block[None]
    for bit in bits_of(lax.axis_size(axis)):
        block = jnp.concatenate([block, swap(block, axis, bit)], axis=0)
    return block


def turned(block, axis):
    count = lax.axis_size(axis)
    bits = bits_of(count)
    rest = block.shape[1:]
    block = block.reshape([2] * len(bits) + list(rest))
    for dim, bit in enumerate(reversed(bits)):
        block = jnp.where(my_bit(axis, bit) == 1, jnp.flip(block, dim), block)
    return block.reshape((count,) + rest)


def share(block, count):
    for bit in bits_of(count):
        groups, rows, cols = block.shape
        pair = block.reshape(groups // 2, 2, rows, cols)
        kept, got = pair[:, 0], swap(pair[:, 1], "narrow", bit)
        mine = my_bit("narrow", bit) == 1
        block = jnp.concatenate([jnp.where(mine, got, kept), jnp.where(mine, kept, got)], axis=1)
    return block


def unshare(block, count):
    for bit in reversed(bits_of(count)):
        groups, rows, cols = block.shape
        pair = block.reshape(groups, 2, rows // 2, cols)
        mine = my_bit("narrow", bit)
        kept = lax.dynamic_index_in_dim(pair, mine, 1, True)
        got = swap(lax.dynamic_index_in_dim(pair, 1 - mine, 1, True), "narrow", bit)
        block = jnp.concatenate([kept, got], axis=1).reshape(2 * groups, rows // 2, cols)
    return block


def shards(
    tokens,
    condition,
    frame_clip,
    mod_weight,
    mod_bias,
    project_weight,
    project_bias,
    merge_weight,
    merge_bias,
    up_weight,
    up_bias,
    down_weight,
    down_bias,
    out_cotangent,
):
    rows, width = tokens.shape
    wide_count, narrow_count = lax.axis_size("wide"), lax.axis_size("narrow")
    wide_me, narrow_me = lax.axis_index("wide"), lax.axis_index("narrow")
    depth = width // wide_count
    part = width // narrow_count
    units = up_weight.shape[1]
    heads = part // HEAD
    clips = condition.shape[0]
    span = math.gcd(rows, PATCHES)
    spans = rows // span
    sharing = PATCHES // span

    def twin(*blocks):
        return Sent(*[swap(block, "wide", 1) for block in blocks])

    def hop(block, axis, bit):
        return Sent(swap(block, axis, bit))

    attn = Gather(
        jnp.concatenate([project_weight.reshape(depth, 3 * part), merge_weight.T], axis=1)
    )
    up, down_shard = Gather(up_weight), down_weight.T
    attn.start()
    z_bits = bits_of(wide_count)[1:]
    narrow_bits = bits_of(narrow_count)
    active = jax.nn.silu(condition).astype(BF16)
    active_mine = lax.dynamic_slice_in_dim(active, wide_me * depth, depth, 1)
    mode_part = jnp.einsum("cd,dki->kci", active_mine, mod_weight, preferred_element_type=F32)
    unit_rows = units // part
    at = 6 * clips
    mode_part = mode_part + swap(mode_part, "wide", 1)
    for bit in z_bits:
        sent = hop(mode_part, "wide", bit)
        if bit == z_bits[0]:
            (mode_part,) = land([sent, attn], mode_part)
        else:
            mode_part, attn.own = land([sent], mode_part, attn.own)
        mode_part = mode_part + sent.got[0]
    small = jnp.concatenate(
        [
            (mode_part + mod_bias.astype(F32)[:, None]).reshape(at, part),
            project_bias.astype(F32),
            merge_bias.astype(F32)[None],
            down_bias.astype(F32)[None],
            up_bias.astype(F32).reshape(unit_rows, part),
        ],
        axis=0,
    )
    span_frame = (narrow_me * rows + jnp.arange(spans, dtype=jnp.int32) * span) // PATCHES
    span_clip = jnp.sum(
        jnp.where(
            span_frame[:, None] == jnp.arange(frame_clip.shape[0], dtype=jnp.int32)[None],
            frame_clip[None],
            0,
        ),
        axis=1,
    )
    attn.start()
    sent = Sent(*spread(small, "narrow", narrow_bits)[1:])
    small, span_clip, up.own = land([sent, attn], small, span_clip, up.own)
    while attn.in_front():
        attn.start()
        land([attn])
    attn.start()
    up.start()
    modes, out_bias, qkv_bias, up_bias_all, core_grad, down_bias_grad, core_own, core_other = unpack_call(
        span_clip, narrow_me, clips, [small, *sent.got], out_cotangent
    )
    (modes,) = land([attn, up, attn.cross("own")], modes)
    while len(up.front) - up.stage > 1:
        up.start()
        land([up])
    attn.start()
    up.start()
    modes, down_shard = land([attn, up, attn.cross("first")], modes, down_shard)
    down = Whole(down_shard)
    attn_far = attn.cross("second", "third", "fourth")
    up.start()
    modes, up.own = land([attn_far], modes, up.own)
    attn.finish()

    attn_w = Weight(attn)
    up_own = up.cross("own")
    hidden_a, qkv, merge_w = project_call(attn_w, tokens, modes, qkv_bias, part)
    qkv, hidden_a = land([up, up_own], qkv, hidden_a)
    up.start()
    up_near = up.cross("first")
    qkv_frames = share(qkv, sharing)
    attended = attend(qkv_frames, heads)
    if sharing > 1:
        attended = attended.reshape(rows * sharing, narrow_count // sharing, part)
        attended = unshare(attended.transpose(1, 0, 2), sharing)
        attended = attended.transpose(1, 0, 2).reshape(rows, width)
    attended, hidden_a = land([up, up_near], attended, hidden_a)
    up_far = up.cross("second", "third", "fourth")
    branch_a, hidden_b = merge_call(attended, merge_w, tokens, modes, out_bias[0])
    hidden_b, attended, hidden_a = land([up_far], hidden_b, attended, hidden_a)
    up.finish()
    hidden_own, hidden_other = turn(hidden_a)
    hidden_twin = twin(hidden_other)
    up_w = Weight(up)
    gelu, slope, sent_part = up_call(up_w, hidden_b, up_bias_all, core_other)

    gelu, slope, hidden_b, sent_part = land([hidden_twin], gelu, slope, hidden_b, sent_part)
    down_cross = twin(sent_part)
    hidden_b_own, hidden_b_other = turn(hidden_b)
    down_w = down.finish()
    upper_grad, up_bias_grad, sent_part = gelu_back_call(down_w, core_grad, slope, hidden_b_other)
    upper_grad, sent_part, attended, gelu, core_own = land(
        [down_cross], upper_grad, sent_part, attended, gelu, core_own
    )
    up_cross = twin(sent_part)
    down_parts = weight_grad_call([core_own], [gelu], [], [], units, down_cross.got[0])
    upper_grad, attended, *down_parts = land([up_cross], upper_grad, attended, *down_parts)
    down_scatter = Scatter(*down_parts)
    attended_twin = twin(attended)
    middle_grad, merged_grad, sums_b, merge_bias_grad = up_back_call(
        up_w, upper_grad, tokens, branch_a, modes, out_cotangent
    )
    merged_grad, upper_grad = land([attended_twin], merged_grad, upper_grad)
    merged_own, merged_other = turn(merged_grad)
    merged_twin = twin(merged_other)
    (merged_grad,) = land([], merged_grad)

    if sharing > 1:
        attended_grad = jnp.dot(merged_grad, merge_w, preferred_element_type=F32).astype(BF16)
        attended_grad = attended_grad.reshape(rows, narrow_count, part).transpose(1, 0, 2)
        attended_grad = share(attended_grad, sharing).transpose(1, 0, 2)
        attended_grad = attended_grad.reshape(rows * sharing, width // sharing)
        qkv_grad = unshare(attend_back(qkv_frames, attended_grad, heads), sharing)
    else:
        qkv_grad = attend_back(qkv_frames, merged_grad, heads, merge_w)
    qkv_grad, upper_grad = land([down_scatter, merged_twin], qkv_grad, upper_grad)
    qkv_twin = twin(qkv_grad)
    up_parts = weight_grad_call(
        [hidden_b_own],
        [upper_grad],
        [merged_own, merged_twin.got[0]],
        [attended, attended_twin.got[0]],
        units,
        up_cross.got[0],
    )
    qkv_grad, *up_parts = land([down_scatter, qkv_twin], qkv_grad, *up_parts)
    up_scatter = Scatter(*up_parts)
    tokens_grad, sums_a, qkv_sums = project_back_call(
        attn_w, qkv_grad, tokens, middle_grad, modes, 3 * part
    )
    sums_a, qkv_grad = land([down_scatter], sums_a, qkv_grad)
    attn_parts = weight_grad_call(
        [hidden_own, hidden_twin.got[0]],
        [qkv_grad, qkv_twin.got[0]],
        [],
        [],
        3 * part,
    )
    gelu, *attn_parts = land([down_scatter], gelu, *attn_parts)
    attn_scatter = Scatter(*attn_parts)
    output, sums_g = down_call(
        down_w, gelu, tokens, branch_a, modes, out_bias[1], out_cotangent
    )
    sums_g, *up_scatter.kept = land([up_scatter.wait()], sums_g, *up_scatter.kept)

    lower, upper = pack_call(
        span_clip, narrow_me, clips, sums_a, sums_b, sums_g, merge_bias_grad, down_bias_grad,
        qkv_sums, up_bias_grad,
    )
    sent = hop(upper, "narrow", narrow_bits[-1])
    up_scatter.go()
    lower, *attn_scatter.kept = land([sent, attn_scatter.wait()], lower, *attn_scatter.kept)
    packed = lower + sent.got[0]
    for bit in reversed(narrow_bits[:-1]):
        sent = hop(packed[bit:], "narrow", bit)
        packed, *attn_scatter.kept = land([sent], packed, *attn_scatter.kept)
        packed = packed[:bit] + sent.got[0]
    packed = packed[0]
    attn_scatter.go()
    sent = hop(packed, "wide", 1)
    (packed,) = land([sent], packed)
    packed = packed + sent.got[0]
    for bit in z_bits:
        sent = hop(packed, "wide", bit)
        (packed,) = land([sent], packed)
        packed = packed + sent.got[0]
    clip_slice = packed[:at].reshape(6, clips, part)
    active_grad = jnp.einsum(
        "kci,dki->cd", clip_slice, mod_weight.astype(F32), precision=lax.Precision.HIGHEST
    )
    (active_grad,) = land([up_scatter], active_grad)
    for bit in narrow_bits:
        sent = hop(active_grad, "narrow", bit)
        (active_grad,) = land(
            [sent, attn_scatter] if bit == narrow_bits[0] else [sent], active_grad
        )
        active_grad = active_grad + sent.got[0]
    active_grad = active_grad[None]
    for bit in bits_of(wide_count):
        sent = hop(active_grad, "wide", bit)
        scatters = {1: [up_scatter], z_bits[0]: [attn_scatter]}
        (active_grad,) = land([sent, *scatters.get(bit, [])], active_grad)
        active_grad = jnp.concatenate([active_grad, sent.got[0]], axis=0)
    active_grad = turned(active_grad, "wide").transpose(1, 0, 2).reshape(clips, width)
    unused, silu_pullback = jax.vjp(jax.nn.silu, condition)
    condition_grad = silu_pullback(active_grad)[0]
    mod_bias_grad = jnp.sum(clip_slice, axis=1)
    mod_weight_grad = jnp.einsum(
        "cd,kci->dki", active_mine.astype(F32), clip_slice, precision=lax.Precision.HIGHEST
    )

    for scatter in (down_scatter, up_scatter, attn_scatter):
        while scatter.stage < scatter.stages:
            land([scatter])
    return (
        output,
        tokens_grad,
        condition_grad,
        mod_weight_grad,
        mod_bias_grad,
        attn_scatter.result.reshape(depth, 3, part),
        packed[at : at + 2],
        up_scatter.result[:, units:].T,
        packed[at + 2],
        up_scatter.result[:, :units],
        packed[at + 4 :].reshape(units),
        down_scatter.result.T,
        packed[at + 3],
    )


def solution(mesh):
    both = P(("wide", "narrow"), None)
    ins = (
        both,
        P(),
        P("wide"),
        P("wide", None, "narrow"),
        P(None, "narrow"),
        P("wide", None, "narrow"),
        P(None, "narrow"),
        P("narrow", "wide"),
        P("narrow"),
        P("wide", "narrow"),
        P("narrow"),
        P("narrow", "wide"),
        P("narrow"),
        both,
    )
    outs = (
        both,
        both,
        P(),
        P("wide", None, "narrow"),
        P(None, "narrow"),
        P("wide", None, "narrow"),
        P(None, "narrow"),
        P("narrow", "wide"),
        P("narrow"),
        P("wide", "narrow"),
        P("narrow"),
        P("narrow", "wide"),
        P("narrow"),
    )
    return jax.shard_map(shards, mesh=mesh, in_specs=ins, out_specs=outs, check_vma=False)
```

```python
import functools
import math

import jax
import jax.numpy as jnp
from jax import lax
from jax.experimental import pallas as pl
from jax.experimental.pallas import tpu as pltpu
from jax.sharding import PartitionSpec as P

HEAD = 72
PATCHES = 256
EPSILON = 1e-06
MIB = 1 << 20
F32 = jnp.float32
BF16 = jnp.bfloat16


def bits_of(size):
    return [1 << k for k in range(size.bit_length() - 1)]


def swap(block, axis, bit):
    count = lax.axis_size(axis)
    return lax.ppermute(block, axis, [(i, i ^ bit) for i in range(count)])


def my_bit(axis, bit):
    return (lax.axis_index(axis) // bit) % 2


def tied(*values):
    return lax.optimization_barrier(values)


def dot(a, b, ca, cb):
    return lax.dot_general(a, b, (((ca,), (cb,)), ((), ())), preferred_element_type=F32)


def row_mean(values):
    return jnp.mean(values, axis=1, keepdims=True)


def normalize(values):
    center = row_mean(values)
    inverse = lax.rsqrt(row_mean(values * values) - center * center + EPSILON)
    return inverse, (values - center) * inverse


def norm_back(incoming, normed, inverse):
    return inverse * (incoming - row_mean(incoming) - normed * row_mean(incoming * normed))


def gelu_both(upper):
    c0 = math.sqrt(2.0 / math.pi)
    square = upper * upper
    tanh = jnp.tanh(upper * (c0 + (c0 * 0.044715) * square))
    half = 0.5 + 0.5 * tanh
    bend = (half * (1.0 - half)) * (2.0 * c0 + (2.0 * c0 * 0.134145) * square)
    return upper * half, half + upper * bend


def params(limit=56):
    return pltpu.CompilerParams(vmem_limit_bytes=limit * MIB)


def cost():
    return pl.CostEstimate(flops=1000000000, bytes_accessed=1, transcendentals=0)


def whole(array):
    return pl.BlockSpec(array.shape, lambda i, *_: (0,) * array.ndim)


def along(array):
    return pl.BlockSpec((1,) + array.shape[1:], lambda i, *_: (i,) + (0,) * (array.ndim - 1))


def shape_of(shape, dtype):
    return jax.ShapeDtypeStruct(shape, dtype)


def attend_kernel(heads, qkv_ref, out_ref):
    part = heads * HEAD
    scale = HEAD ** (-0.5)
    results = []
    for n in range(qkv_ref.shape[0]):
        qs, ks, vs = [
            [qkv_ref[n, :, i * part + h * HEAD : i * part + (h + 1) * HEAD] for h in range(heads)]
            for i in range(3)
        ]
        scores = [dot(k, q, 1, 1) for k, q in zip(ks, qs)]
        probs = []
        for s in scores:
            p = jnp.exp((s - jnp.max(s, axis=0, keepdims=True)) * scale)
            probs.append((p.astype(BF16), 1.0 / jnp.sum(p, axis=0, keepdims=True)))
        for (p, weight), v in zip(probs, vs):
            results.append(dot(v, p, 0, 0) * weight)
    out_ref[...] = jnp.concatenate(results, axis=0).T.astype(BF16)


def attend(qkv, heads):
    groups, rows, cols = qkv.shape
    width = groups * heads * HEAD
    out = shape_of((rows, width), BF16)
    return pl.pallas_call(
        functools.partial(attend_kernel, heads),
        grid=(rows // PATCHES,),
        in_specs=[pl.BlockSpec((groups, PATCHES, cols), lambda f: (0, f, 0))],
        out_specs=pl.BlockSpec((PATCHES, width), lambda f: (f, 0)),
        out_shape=out,
        compiler_params=params(),
        cost_estimate=cost(),
        name="attend",
    )(qkv)


def attend_back_kernel(heads, qkv_ref, grad_ref, *refs):
    out_ref = refs[-1]
    part = heads * HEAD
    scale = HEAD ** (-0.5)
    pad = out_ref.shape[2] - 3 * part
    grad = grad_ref[...]
    if len(refs) > 1:
        grad = dot(grad, refs[0][...], 1, 0).astype(BF16)
    for n in range(qkv_ref.shape[0]):
        qs, ks, vs = [
            [qkv_ref[n, :, i * part + h * HEAD : i * part + (h + 1) * HEAD] for h in range(heads)]
            for i in range(3)
        ]
        gs = [grad[:, n * part + h * HEAD : n * part + (h + 1) * HEAD] for h in range(heads)]
        scores = [dot(k, q, 1, 1) for k, q in zip(ks, qs)]
        slopes = [dot(v, g, 1, 1) for v, g in zip(vs, gs)]
        probs, score_grads = [], []
        for s, dp in zip(scores, slopes):
            p = jnp.exp((s - jnp.max(s, axis=0, keepdims=True)) * scale)
            p = p * (1.0 / jnp.sum(p, axis=0, keepdims=True))
            probs.append(p.astype(BF16))
            score_grads.append((p * (dp - jnp.sum(p * dp, axis=0, keepdims=True))).astype(BF16))
        dvs = [dot(p, g, 1, 0) for p, g in zip(probs, gs)]
        dks = [dot(ds, q, 1, 0) * scale for ds, q in zip(score_grads, qs)]
        dqs = [dot(k, ds, 0, 0) * scale for ds, k in zip(score_grads, ks)]
        dq = jnp.concatenate(dqs, axis=0).T
        zeros = [jnp.zeros((PATCHES, pad), F32)] if pad else []
        out_ref[n] = jnp.concatenate([dq] + dks + dvs + zeros, axis=1).astype(BF16)


def attend_back(qkv, grad, heads, weight=None):
    groups, rows, cols = qkv.shape
    width = groups * heads * HEAD
    out = shape_of((groups, rows, -(-cols // 128) * 128), BF16)
    more = [] if weight is None else [weight]
    return pl.pallas_call(
        functools.partial(attend_back_kernel, heads),
        grid=(rows // PATCHES,),
        in_specs=[
            pl.BlockSpec((groups, PATCHES, cols), lambda f: (0, f, 0)),
            pl.BlockSpec((PATCHES, width), lambda f: (f, 0)),
        ]
        + [whole(a) for a in more],
        out_specs=pl.BlockSpec((groups, PATCHES, out.shape[2]), lambda f: (0, f, 0)),
        out_shape=out,
        compiler_params=params(),
        cost_estimate=cost(),
        name="attend_back",
    )(qkv, grad, *more)


class Sent:
    def __init__(self, *values):
        self.pending = list(values)

    def take(self, got):
        self.got = got
        self.pending = []


def land(sents, *ties):
    sents = [sent for sent in sents if sent.pending]
    pending = [value for sent in sents for value in sent.pending]
    values = list(tied(*pending, *ties))
    for sent in sents:
        count = len(sent.pending)
        sent.take(values[:count])
        values = values[count:]
    return values


class Gather:
    def __init__(self, shard):
        self.depth, self.cols = shard.shape
        self.cut = max(16, self.depth // 2 // 16 * 16)
        wide = [("wide", bit) for bit in reversed(bits_of(lax.axis_size("wide")))]
        narrow = [("narrow", bit) for bit in reversed(bits_of(lax.axis_size("narrow")))]
        self.core = wide[-1]
        self.front = wide[:-1] + narrow[:-2]
        self.last = narrow[-2:]
        self.own = shard[None]
        self.stage = 0
        self.pending = []
        self.crossed = {}

    def in_front(self):
        return self.stage < len(self.front)

    def start(self):
        if self.in_front():
            self.pending = [swap(self.own, *self.front[self.stage])]
        elif self.stage == len(self.front):
            self.pending = [swap(self.own, *key) for key in self.last]
        else:
            self.pending = [
                swap(self.first[:, : self.cut], *self.last[1]),
                swap(self.second[:, self.cut :], *self.last[0]),
            ]
        return self

    def take(self, got):
        self.pending = []
        if self.in_front():
            self.own = jnp.concatenate([self.own, got[0]], axis=0)
        elif self.stage == len(self.front):
            self.first, self.second = got
        else:
            self.third, self.fourth = got
        self.stage += 1

    def cross(self, *names):
        sent = Sent(*[swap(getattr(self, name), *self.core) for name in names])
        for i, name in enumerate(names):
            self.crossed[name] = (sent, i)
        return sent

    def finish(self):
        names = ["own", "first", "second", "third", "fourth"]
        self.arrays = [getattr(self, name) for name in names]
        for name in names:
            sent, i = self.crossed[name]
            self.arrays.append(sent.got[i])
        return self

    def entries(self, n):
        found = []
        (unused, high), (unused, low) = self.last
        whole_rows, cut = (0, self.depth), self.cut
        for w in range(lax.axis_size("wide")):
            index = 0
            for j, (axis, bit) in enumerate(self.front):
                index += bool((n if axis == "narrow" else w) & bit) << j
            side = 5 * bool(w & self.core[1])
            if n & high and n & low:
                parts = [(3, 0, cut), (4, cut, self.depth - cut)]
            else:
                parts = [(1 if n & high else 2 if n & low else 0, 0, self.depth)]
            found += [(side + which, index, w, offset, size) for which, offset, size in parts]
        return found

    def assembled(self):
        sides = []
        for side in (0, 5):
            own, first, second, third, fourth = self.arrays[side : side + 5]
            across = jnp.concatenate([third, fourth], axis=1)
            sides.append(jnp.stack([jnp.stack([own, second]), jnp.stack([first, across])]))
        block = jnp.stack(sides)
        keys = [self.core, *self.last, *self.front[::-1]]
        block = block.reshape([2] * len(keys) + [self.depth, self.cols])
        narrow = [("narrow", bit) for bit in reversed(bits_of(lax.axis_size("narrow")))]
        wide = [("wide", bit) for bit in reversed(bits_of(lax.axis_size("wide")))]
        order = [keys.index(key) for key in narrow + wide]
        block = block.transpose(order + [len(keys), len(keys) + 1])
        for dim, key in enumerate(wide):
            dim += len(narrow)
            block = jnp.where(my_bit(*key) == 1, jnp.flip(block, dim), block)
        return block.reshape(lax.axis_size("narrow"), -1, self.cols)


class Weight:
    def __init__(self, gather):
        groups = lax.axis_size("narrow")
        self.depth, self.cols = gather.depth, gather.cols
        if gather.cut % 16 or gather.depth % 16:
            self.arrays = [gather.assembled()]
            self.plan = [[(0, n, None, 0, 0)] for n in range(groups)]
        else:
            self.arrays = gather.arrays
            self.plan = [gather.entries(n) for n in range(groups)]


class Whole:
    def __init__(self, shard):
        self.depth, self.cols = shard.shape
        groups = lax.axis_size("narrow")
        blocks = lax.all_gather(shard, ("narrow", "wide"), axis=0)
        self.blocks = blocks.reshape(groups, lax.axis_size("wide") * self.depth, self.cols)

    def finish(self):
        self.arrays = [self.blocks]
        self.plan = [[(0, n, None, 0, 0)] for n in range(lax.axis_size("narrow"))]
        return self


def stream(step, weight, me, refs, buffer, sems, before):
    plan = weight.plan

    def issue(n):
        for which, index, w, offset, size in plan[n]:
            if w is None:
                target = buffer.at[n % 2]
                if isinstance(weight, Whole):
                    index = me[1] ^ index
            else:
                row = pl.multiple_of((me[0] ^ w) * weight.depth + offset, 16)
                target = buffer.at[n % 2, pl.ds(row, size)]
            pltpu.make_async_copy(refs[which].at[index], target, sems.at[n % 2]).start()

    @pl.when(step == -before)
    def _():
        issue(0)
        pltpu.make_async_copy(buffer.at[0], buffer.at[0], sems.at[0]).wait()
        issue(1)

    for n in range(1, len(plan)):

        @pl.when(step == n)
        def _():
            pltpu.make_async_copy(buffer.at[n % 2], buffer.at[n % 2], sems.at[n % 2]).wait()
            if n + 1 < len(plan):
                issue(n + 1)

    return buffer.at[jnp.clip(step, 0, len(plan) - 1) % 2]


def group_at(array, before, groups):
    def index(i, *_):
        return (jnp.clip(i - before, 0, groups - 1),) + (0,) * (array.ndim - 1)

    return pl.BlockSpec((1,) + array.shape[1:], index)


def rows_at(array, first, spans):
    def index(i, *_):
        return (jnp.clip(i - first, 0, spans - 1),) + (0,) * (array.ndim - 1)

    return pl.BlockSpec((array.shape[0] // spans,) + array.shape[1:], index)


def weight_call(body, weight, ins, in_specs, outs, out_specs, scratch, name, before=0, after=0):
    count, groups = len(weight.arrays), len(weight.plan)
    width = lax.axis_size("wide") * weight.depth

    def kernel(me_ref, *refs):
        step = pl.program_id(0) - before
        in_refs = refs[: len(ins)]
        weight_refs = refs[len(ins) : len(ins) + count]
        out_refs = refs[len(ins) + count : len(ins) + count + len(outs)]
        buffer, sems = refs[len(ins) + count + len(outs) :][:2]
        scratch_refs = refs[len(ins) + count + len(outs) + 2 :]
        w = stream(step, weight, me_ref, weight_refs, buffer, sems, before)
        body(step, in_refs, w, out_refs, scratch_refs)

    me = jnp.stack([lax.axis_index("wide"), lax.axis_index("narrow")]).astype(jnp.int32)
    return pl.pallas_call(
        kernel,
        grid_spec=pltpu.PrefetchScalarGridSpec(
            num_scalar_prefetch=1,
            grid=(before + groups + after,),
            in_specs=list(in_specs) + [pl.BlockSpec(memory_space=pl.ANY)] * count,
            out_specs=list(out_specs),
            scratch_shapes=[
                pltpu.VMEM((2, width, weight.cols), BF16),
                pltpu.SemaphoreType.DMA((2,)),
            ]
            + list(scratch),
        ),
        out_shape=list(outs),
        compiler_params=params(),
        cost_estimate=cost(),
        name=name,
    )(me, *ins, *weight.arrays)


def project_call(weight, tokens, modes, bias, part):
    rows, width = tokens.shape
    spans, span = modes.shape[0], rows // modes.shape[0]
    groups = len(weight.plan)
    outs = [
        shape_of((rows, width), BF16),
        shape_of((groups, rows, 3 * part), BF16),
        shape_of((width, groups * part), BF16),
    ]

    before = spans - 1

    def body(step, ins, w, out, scratch):
        tokens_ref, modes_ref, bias_ref = ins
        hidden_ref, qkv_ref, merge_ref = out
        held = scratch[0]

        @pl.when(step <= 0)
        def _():
            at = pl.ds(pl.multiple_of((step + before) * span, span), span)
            unused, normed = normalize(tokens_ref[...].astype(F32))
            hidden = (normed * (1.0 + modes_ref[0, 1:2]) + modes_ref[0, 0:1]).astype(BF16)
            hidden_ref[...] = hidden
            held[at, :] = hidden
            qkv_ref[0, at, :] = (dot(hidden, w[:, : 3 * part], 1, 0) + bias_ref[0]).astype(BF16)

        @pl.when(step > 0)
        def _():
            qkv_ref[0] = (dot(held[...], w[:, : 3 * part], 1, 0) + bias_ref[0]).astype(BF16)

        for n in range(groups):

            @pl.when(step == n)
            def _():
                merge_ref[:, n * part : (n + 1) * part] = w[:, 3 * part :]

    return weight_call(
        body,
        weight,
        [tokens, modes, bias],
        [rows_at(tokens, 0, spans), rows_at(modes, 0, spans), group_at(bias, before, groups)],
        outs,
        [rows_at(outs[0], 0, spans), group_at(outs[1], before, groups), whole(outs[2])],
        [pltpu.VMEM((rows, width), BF16)],
        "project",
        before=before,
    )


def merge_kernel(attended_ref, weight_ref, tokens_ref, modes_ref, bias_ref, branch_ref, hidden_ref):
    branch = dot(attended_ref[...], weight_ref[...], 1, 1) + bias_ref[...]
    branch_ref[...] = branch
    middle = tokens_ref[...].astype(F32) + modes_ref[0, 2:3] * branch
    unused, normed = normalize(middle)
    hidden_ref[...] = (normed * (1.0 + modes_ref[0, 4:5]) + modes_ref[0, 3:4]).astype(BF16)


def merge_call(attended, weight, tokens, modes, bias):
    rows, width = tokens.shape
    spans, span = modes.shape[0], rows // modes.shape[0]
    block = pl.BlockSpec((span, width), lambda i: (i, 0))
    outs = [shape_of((rows, width), F32), shape_of((rows, width), BF16)]
    return pl.pallas_call(
        merge_kernel,
        grid=(spans,),
        in_specs=[block, whole(weight), block, along(modes), whole(bias)],
        out_specs=[block, block],
        out_shape=outs,
        compiler_params=params(),
        cost_estimate=cost(),
        name="merge",
    )(attended, weight, tokens, modes, bias)


def up_call(weight, hidden, bias, left):
    rows, width = hidden.shape
    groups, units = len(weight.plan), weight.cols
    zs, depth = left.shape[:2]
    outs = [shape_of((groups, rows, units), BF16)] * 2 + [shape_of((groups, zs, depth, units), BF16)]

    def body(step, ins, w, out, scratch):
        hidden_ref, bias_ref, left_ref = ins
        gelu, slope = gelu_both(dot(hidden_ref[...], w[...], 1, 0) + bias_ref[0])
        gelu = gelu.astype(BF16)
        out[0][0] = gelu
        out[1][0] = slope.astype(BF16)
        part = dot(left_ref[...].reshape(zs * depth, rows), gelu, 1, 0)
        out[2][0] = part.astype(BF16).reshape(zs, depth, units)

    return weight_call(
        body,
        weight,
        [hidden, bias, left],
        [whole(hidden), along(bias), whole(left)],
        outs,
        [along(out) for out in outs],
        [],
        "up",
    )


def down_call(weight, gelu, tokens, branch, modes, bias, grad):
    rows, width = tokens.shape
    spans, span = modes.shape[0], rows // modes.shape[0]
    groups, units = len(weight.plan), weight.cols
    outs = [shape_of((rows, width), BF16), shape_of((spans, 1, width), F32)]

    def body(step, ins, w, out, scratch):
        gelu_ref, tokens_ref, branch_ref, modes_ref, bias_ref, grad_ref = ins
        total = scratch[0]

        @pl.when(step == 0)
        def _():
            total[...] = dot(gelu_ref[0], w[...], 1, 1)

        @pl.when((step > 0) & (step < groups - 1))
        def _():
            total[...] += dot(gelu_ref[0], w[...], 1, 1)

        @pl.when(step >= groups - 1)
        def _():
            at = pl.ds(pl.multiple_of((step - groups + 1) * span, span), span)
            other = total[at, :] + dot(gelu_ref[0, at, :], w[...], 1, 1) + bias_ref[...]
            middle = tokens_ref[...].astype(F32) + modes_ref[0, 2:3] * branch_ref[...]
            out[0][...] = (middle + modes_ref[0, 5:6] * other).astype(BF16)
            out[1][0] = jnp.sum(grad_ref[...].astype(F32) * other, axis=0, keepdims=True)

    def by_span(array):
        return rows_at(array, groups - 1, spans)

    return weight_call(
        body,
        weight,
        [gelu, tokens, branch, modes, bias, grad],
        [group_at(gelu, 0, groups), by_span(tokens), by_span(branch), by_span(modes), whole(bias), by_span(grad)],
        outs,
        [by_span(outs[0]), by_span(outs[1])],
        [pltpu.VMEM((rows, width), F32)],
        "down",
        after=spans - 1,
    )


def gelu_back_call(weight, grad, slope, left):
    rows, width = grad.shape
    groups, units = len(weight.plan), weight.cols
    zs, depth = left.shape[:2]
    outs = [
        shape_of((groups, rows, units), BF16),
        shape_of((groups, 1, units), F32),
        shape_of((groups, zs, depth, units), BF16),
    ]

    def body(step, ins, w, out, scratch):
        grad_ref, slope_ref, left_ref = ins
        upper = (dot(grad_ref[...], w[...], 1, 0) * slope_ref[0].astype(F32)).astype(BF16)
        out[0][0] = upper
        out[1][0] = jnp.sum(upper.astype(F32), axis=0, keepdims=True)
        part = dot(left_ref[...].reshape(zs * depth, rows), upper, 1, 0)
        out[2][0] = part.astype(BF16).reshape(zs, depth, units)

    return weight_call(
        body,
        weight,
        [grad, slope, left],
        [whole(grad), along(slope), whole(left)],
        outs,
        [along(out) for out in outs],
        [],
        "gelu_back",
    )


def up_back_call(weight, upper, tokens, branch, modes, grad):
    rows, width = tokens.shape
    spans, span = modes.shape[0], rows // modes.shape[0]
    groups, units = len(weight.plan), weight.cols
    outs = [
        shape_of((rows, width), F32),
        shape_of((rows, width), BF16),
        shape_of((spans, 3, width), F32),
        shape_of((1, width), F32),
    ]

    def body(step, ins, w, out, scratch):
        upper_ref, tokens_ref, branch_ref, modes_ref, grad_ref = ins
        middle_ref, merged_ref, sums_ref, bias_ref = out
        total = scratch[0]

        @pl.when(step == 0)
        def _():
            total[...] = dot(upper_ref[0], w[...], 1, 1)
            bias_ref[...] = jnp.zeros_like(bias_ref)

        @pl.when((step > 0) & (step < groups - 1))
        def _():
            total[...] += dot(upper_ref[0], w[...], 1, 1)

        @pl.when(step >= groups - 1)
        def _():
            at = pl.ds(pl.multiple_of((step - groups + 1) * span, span), span)
            hidden = total[at, :] + dot(upper_ref[0, at, :], w[...], 1, 1)
            branch = branch_ref[...]
            gate = modes_ref[0, 2:3]
            inverse, normed = normalize(tokens_ref[...].astype(F32) + gate * branch)
            back = norm_back(hidden * (1.0 + modes_ref[0, 4:5]), normed, inverse)
            middle = grad_ref[...].astype(F32) + back
            gated = gate * middle
            middle_ref[...] = middle
            merged_ref[...] = gated.astype(BF16)
            sums_ref[0, 0:1] = jnp.sum(middle * branch, axis=0, keepdims=True)
            sums_ref[0, 1:2] = jnp.sum(hidden, axis=0, keepdims=True)
            sums_ref[0, 2:3] = jnp.sum(hidden * normed, axis=0, keepdims=True)
            bias_ref[...] += jnp.sum(gated, axis=0, keepdims=True)

    def by_span(array):
        return rows_at(array, groups - 1, spans)

    return weight_call(
        body,
        weight,
        [upper, tokens, branch, modes, grad],
        [group_at(upper, 0, groups)] + [by_span(a) for a in (tokens, branch, modes, grad)],
        outs,
        [by_span(a) for a in outs[:3]] + [whole(outs[3])],
        [pltpu.VMEM((rows, width), F32)],
        "up_back",
        after=spans - 1,
    )


def project_back_call(weight, qkv_grad, tokens, middle, modes, cols):
    rows, width = tokens.shape
    spans, span = modes.shape[0], rows // modes.shape[0]
    groups = len(weight.plan)
    outs = [
        shape_of((rows, width), F32),
        shape_of((spans, 2, width), F32),
        shape_of((groups, 1, cols), F32),
    ]

    def body(step, ins, w, out, scratch):
        grad_ref, tokens_ref, middle_ref, modes_ref = ins
        tokens_grad_ref, sums_ref, bias_ref = out
        total = scratch[0]

        @pl.when(step < groups)
        def _():
            bias_ref[0] = jnp.sum(grad_ref[0, :, :cols].astype(F32), axis=0, keepdims=True)

        @pl.when(step == 0)
        def _():
            total[...] = dot(grad_ref[0, :, :cols], w[:, :cols], 1, 1)

        @pl.when((step > 0) & (step < groups - 1))
        def _():
            total[...] += dot(grad_ref[0, :, :cols], w[:, :cols], 1, 1)

        @pl.when(step >= groups - 1)
        def _():
            at = pl.ds(pl.multiple_of((step - groups + 1) * span, span), span)
            inverse, normed = normalize(tokens_ref[...].astype(F32))
            hidden = total[at, :] + dot(grad_ref[0, at, :cols], w[:, :cols], 1, 1)
            back = norm_back(hidden * (1.0 + modes_ref[0, 1:2]), normed, inverse)
            tokens_grad_ref[...] = middle_ref[...] + back
            sums_ref[0, 0:1] = jnp.sum(hidden, axis=0, keepdims=True)
            sums_ref[0, 1:2] = jnp.sum(hidden * normed, axis=0, keepdims=True)

    def by_span(array):
        return rows_at(array, groups - 1, spans)

    return weight_call(
        body,
        weight,
        [qkv_grad, tokens, middle, modes],
        [group_at(qkv_grad, 0, groups)] + [by_span(a) for a in (tokens, middle, modes)],
        outs,
        [by_span(outs[0]), by_span(outs[1]), group_at(outs[2], 0, groups)],
        [pltpu.VMEM((rows, width), F32)],
        "project_back",
        after=spans - 1,
    )


def put_turned(depth, side, block, own_ref, other_ref):
    turned_block = block.T
    for z in range(own_ref.shape[0]):
        even = turned_block[2 * z * depth : (2 * z + 1) * depth]
        odd = turned_block[(2 * z + 1) * depth : (2 * z + 2) * depth]
        own_ref[z] = jnp.where(side == 1, odd, even)
        other_ref[z] = jnp.where(side == 1, even, odd)


def turn_kernel(depth, me_ref, block_ref, own_ref, other_ref):
    put_turned(depth, me_ref[0] & 1, block_ref[...], own_ref, other_ref)


def turn(block):
    rows, width = block.shape
    blocks = lax.axis_size("wide")
    out = shape_of((blocks // 2, width // blocks, rows), BF16)
    me = lax.axis_index("wide").astype(jnp.int32)[None]
    own, other = pl.pallas_call(
        functools.partial(turn_kernel, width // blocks),
        grid_spec=pltpu.PrefetchScalarGridSpec(
            num_scalar_prefetch=1, grid=(1,), in_specs=[whole(block)], out_specs=[whole(out)] * 2
        ),
        out_shape=[out, out],
        compiler_params=params(24),
        cost_estimate=cost(),
        name="turn",
    )(me, block)
    return own, other


def weight_grad_call(lefts, grads, merged, attended, cols, added=None):
    zs, size, rows = lefts[0].shape
    groups = grads[0].shape[0]
    width = 2 * zs * size
    cut = max(16, size // 2 // 16 * 16)
    part = width // groups if merged else 0
    half = groups // 2
    outs = []
    for height in (cut, cut, size - cut, size - cut):
        outs.append(shape_of((half, zs, height, cols + part), BF16))
    more = [] if added is None else [added]
    ins = [*lefts, *grads, *more, *merged, *attended]
    count = len(lefts)

    def product(left_refs, right_refs):
        terms = [
            dot(left[...].reshape(zs * size, rows), right, 1, 0)
            for left, right in zip(left_refs, right_refs)
        ]
        return sum(terms[1:], terms[0])

    def kernel(*refs):
        step = pl.program_id(0)
        left_refs, grad_refs, rest = refs[:count], refs[count : 2 * count], refs[2 * count : len(ins)]
        out_refs, scratch = refs[len(ins) : len(ins) + 4], refs[len(ins) + 4 :]
        result = product(left_refs, [ref[0, :, :cols] for ref in grad_refs])
        if more:
            result = result + rest[0][0].reshape(zs * size, cols).astype(F32)
        result = result.astype(BF16)
        if merged:

            @pl.when(step == 0)
            def _():
                pairs = rest[len(more) :]
                values = [ref[...] for ref in pairs[len(merged) :]]
                scratch[0][...] = product(pairs[: len(merged)], values).astype(BF16)

        for n in range(groups):

            @pl.when(step == n)
            def _():
                value = result
                if merged:
                    value = jnp.concatenate([value, scratch[0][:, n * part : (n + 1) * part]], axis=1)
                first = out_refs[0] if n < half else out_refs[1]
                second = out_refs[2] if n % 2 == 0 else out_refs[3]
                for z in range(zs):
                    first[0, z] = value[z * size : z * size + cut]
                    second[0, z] = value[z * size + cut : (z + 1) * size]

    rest = (0, 0, 0)
    out_specs = [
        pl.BlockSpec((1,) + out.shape[1:], index)
        for out, index in zip(
            outs,
            [
                lambda i: (jnp.minimum(i, half - 1),) + rest,
                lambda i: (jnp.maximum(i - half, 0),) + rest,
                lambda i: (i // 2,) + rest,
                lambda i: (i // 2,) + rest,
            ],
        )
    ]
    return pl.pallas_call(
        kernel,
        grid=(groups,),
        in_specs=[whole(a) for a in lefts]
        + [along(a) for a in (*grads, *more)]
        + [whole(a) for a in (*merged, *attended)],
        out_specs=out_specs,
        scratch_shapes=[pltpu.VMEM((zs * size, width), BF16)] if merged else [],
        out_shape=outs,
        compiler_params=params(),
        cost_estimate=cost(),
        name="weight_grad",
    )(*ins)


def plus(a, b):
    return (a.astype(F32) + b.astype(F32)).astype(BF16)


class Scatter:
    def __init__(self, first_kept, first_sent, second_kept, second_sent):
        narrow = list(reversed(bits_of(lax.axis_size("narrow"))))
        self.orders = [narrow, narrow[::-1]]
        self.left = [list(narrow), list(narrow)]
        self.front = list(bits_of(lax.axis_size("wide")))[1:]
        self.stage = 0
        self.stages = len(narrow) + len(self.front)
        self.kept, self.pending = [], []
        sides = ((first_kept, first_sent), (second_kept, second_sent))
        for part, (kept, sent) in enumerate(sides):
            bit = self.orders[part][0]
            self.left[part].remove(bit)
            self.kept.append(kept.reshape([2] * (len(narrow) - 1) + list(kept.shape[1:])))
            self.pending.append(swap(sent.reshape(self.kept[-1].shape), "narrow", bit))

    def take(self, got):
        self.got = list(got)
        self.go()

    def wait(self):
        sent = Sent(*self.pending)
        sent.take = lambda got: setattr(self, "got", list(got))
        self.pending = []
        return sent

    def go(self):
        kept, got, narrow = self.kept, self.got, len(self.orders[0])
        self.stage += 1
        if self.stage < narrow:
            self.kept, self.pending = [], []
            for part, order in enumerate(self.orders):
                bit = order[self.stage]
                dim = self.left[part].index(bit)
                self.left[part].remove(bit)
                stay, go = [
                    plus(
                        lax.index_in_dim(kept[part], side, dim, False),
                        lax.index_in_dim(got[part], side, dim, False),
                    )
                    for side in (0, 1)
                ]
                self.kept.append(stay)
                self.pending.append(swap(go, "narrow", bit))
        elif self.stage < self.stages:
            bit = self.front[self.stage - narrow]
            mine = my_bit("wide", bit)
            dim = len(self.front) - 1 - (self.stage - narrow)
            sides = []
            for side in (mine, 1 - mine):
                blocks = []
                for a, b in zip(kept, got):
                    if self.stage == narrow:
                        shape = [2] * len(self.front) + list(a.shape[1:])
                        a, b = a.reshape(shape), b.reshape(shape)
                    blocks.append(
                        plus(
                            lax.dynamic_index_in_dim(a, side, dim, False),
                            lax.dynamic_index_in_dim(b, side, dim, False),
                        )
                    )
                sides.append(jnp.concatenate(blocks, axis=-2) if len(blocks) > 1 else blocks[0])
            self.kept = [sides[0]]
            self.pending = [swap(sides[1], "wide", bit)]
        else:
            self.result = kept[0].astype(F32) + got[0].astype(F32)
            self.pending = []


def spread(block, axis, bits):
    blocks = [block]
    for index in range(1, 1 << len(bits)):
        mask = sum(bit for j, bit in enumerate(bits) if index >> j & 1)
        blocks.append(swap(block, axis, mask))
    return blocks


def tree_sum(blocks):
    while len(blocks) > 1:
        blocks = [blocks[i] + blocks[i + 1] for i in range(0, len(blocks), 2)]
    return blocks[0]


def unpack_call(span_clip, narrow_me, clips, blocks, grad):
    spans = span_clip.shape[0]
    rows, width = grad.shape
    span = rows // spans
    groups = len(blocks)
    height, part = blocks[0].shape
    at = 6 * clips
    units = (height - at - 4) * part
    wide = lax.axis_size("wide")
    outs = [
        shape_of((spans, 6, width), F32),
        shape_of((2, 1, width), F32),
        shape_of((groups, 1, 3 * part), F32),
        shape_of((groups, 1, units), F32),
        shape_of((rows, width), BF16),
        shape_of((1, width), F32),
        shape_of((wide // 2, width // wide, rows), BF16),
        shape_of((wide // 2, width // wide, rows), BF16),
    ]

    def kernel(clip_ref, me_ref, *refs):
        block_refs, grad_ref = refs[: len(blocks)], refs[len(blocks)]
        modes_ref, bias_ref, qkv_ref, up_ref, core_ref, sum_ref, own_ref, other_ref = refs[len(blocks) + 1 :]
        for rel, ref in enumerate(block_refs):
            owner = me_ref[0] ^ rel
            found = []
            for s in range(spans):
                for k in range(6):
                    found.append(ref[pl.ds(k * clips + clip_ref[s], 1), :])
            for n in range(groups):

                @pl.when(owner == n)
                def _():
                    lanes = slice(n * part, (n + 1) * part)
                    for s in range(spans):
                        for k in range(6):
                            modes_ref[s, k : k + 1, lanes] = found[6 * s + k]
                    for k in range(2):
                        bias_ref[k, :, lanes] = ref[at + 2 + k : at + 3 + k, :]

            qkv_ref[rel] = jnp.concatenate(
                [ref[at : at + 1, :], jnp.zeros((1, part), F32), ref[at + 1 : at + 2, :]], axis=1
            )
            for j in range(units // part):
                up_ref[rel, :, j * part : (j + 1) * part] = ref[at + 4 + j : at + 5 + j, :]
        for s in range(spans):
            lines = slice(s * span, (s + 1) * span)
            gated = modes_ref[s, 5:6] * grad_ref[lines, :].astype(F32)
            core_ref[lines, :] = gated.astype(BF16)
            here = jnp.sum(gated, axis=0, keepdims=True)
            sum_ref[...] = here if s == 0 else sum_ref[...] + here
        put_turned(width // wide, me_ref[1] & 1, core_ref[...], own_ref, other_ref)

    me = jnp.stack([narrow_me, lax.axis_index("wide")]).astype(jnp.int32)
    return pl.pallas_call(
        kernel,
        grid_spec=pltpu.PrefetchScalarGridSpec(
            num_scalar_prefetch=2,
            grid=(1,),
            in_specs=[whole(a) for a in (*blocks, grad)],
            out_specs=[whole(a) for a in outs],
        ),
        out_shape=outs,
        compiler_params=params(32),
        cost_estimate=cost(),
        name="unpack",
    )(span_clip, me, *blocks, grad)


def pack_call(span_clip, narrow_me, clips, sums_a, sums_b, sums_g, merge_bias, down_bias, qkv_sums, up_bias):
    spans, unused, width = sums_a.shape
    groups = qkv_sums.shape[0]
    part, units = width // groups, up_bias.shape[2]
    at = 6 * clips
    height = at + 4 + units // part
    outs = [shape_of((groups // 2, height, part), F32)] * 2
    ins = [sums_a, sums_b, sums_g, merge_bias, down_bias, qkv_sums, up_bias]

    def kernel(clip_ref, me_ref, a_ref, b_ref, g_ref, merge_ref, down_ref, qkv_ref, up_ref, *refs):
        total = refs[2]
        out_refs = [refs[rel // (groups // 2)].at[rel % (groups // 2)] for rel in range(groups)]
        total[...] = jnp.zeros_like(total)
        for s in range(spans):
            rows = [a_ref[s, 0:1], a_ref[s, 1:2]] + [b_ref[s, i : i + 1] for i in range(3)]
            rows.append(g_ref[s, 0:1])
            for k in range(6):
                row = pl.ds(k * clips + clip_ref[s], 1)
                total[row, :] += rows[k]
        total[at : at + 1, :] = merge_ref[...]
        total[at + 1 : at + 2, :] = down_ref[...]
        for rel in range(groups):
            owner = me_ref[0] ^ rel
            for n in range(groups):

                @pl.when(owner == n)
                def _():
                    own = total[:, n * part : (n + 1) * part]
                    out_refs[rel][:at, :] = own[:at]
                    out_refs[rel][at + 2 : at + 4, :] = own[at : at + 2]

            out_refs[rel][at : at + 1, :] = qkv_ref[rel, :, :part]
            out_refs[rel][at + 1 : at + 2, :] = qkv_ref[rel, :, 2 * part :]
            for j in range(units // part):
                out_refs[rel][at + 4 + j : at + 5 + j, :] = up_ref[rel, :, j * part : (j + 1) * part]

    return pl.pallas_call(
        kernel,
        grid_spec=pltpu.PrefetchScalarGridSpec(
            num_scalar_prefetch=2,
            grid=(1,),
            in_specs=[whole(a) for a in ins],
            out_specs=[whole(a) for a in outs],
            scratch_shapes=[pltpu.VMEM((at + 8, width), F32)],
        ),
        out_shape=outs,
        compiler_params=params(16),
        name="pack",
    )(span_clip, narrow_me.astype(jnp.int32)[None], *ins)


def sum_over(block, axis):
    for bit in bits_of(lax.axis_size(axis)):
        block = block + swap(block, axis, bit)
    return block


def collect(block, axis):
    block = block[None]
    for bit in bits_of(lax.axis_size(axis)):
        block = jnp.concatenate([block, swap(block, axis, bit)], axis=0)
    return block


def turned(block, axis):
    count = lax.axis_size(axis)
    bits = bits_of(count)
    rest = block.shape[1:]
    block = block.reshape([2] * len(bits) + list(rest))
    for dim, bit in enumerate(reversed(bits)):
        block = jnp.where(my_bit(axis, bit) == 1, jnp.flip(block, dim), block)
    return block.reshape((count,) + rest)


def share(block, count):
    for bit in bits_of(count):
        groups, rows, cols = block.shape
        pair = block.reshape(groups // 2, 2, rows, cols)
        kept, got = pair[:, 0], swap(pair[:, 1], "narrow", bit)
        mine = my_bit("narrow", bit) == 1
        block = jnp.concatenate([jnp.where(mine, got, kept), jnp.where(mine, kept, got)], axis=1)
    return block


def unshare(block, count):
    for bit in reversed(bits_of(count)):
        groups, rows, cols = block.shape
        pair = block.reshape(groups, 2, rows // 2, cols)
        mine = my_bit("narrow", bit)
        kept = lax.dynamic_index_in_dim(pair, mine, 1, True)
        got = swap(lax.dynamic_index_in_dim(pair, 1 - mine, 1, True), "narrow", bit)
        block = jnp.concatenate([kept, got], axis=1).reshape(2 * groups, rows // 2, cols)
    return block


def shards(
    tokens,
    condition,
    frame_clip,
    mod_weight,
    mod_bias,
    project_weight,
    project_bias,
    merge_weight,
    merge_bias,
    up_weight,
    up_bias,
    down_weight,
    down_bias,
    out_cotangent,
):
    rows, width = tokens.shape
    wide_count, narrow_count = lax.axis_size("wide"), lax.axis_size("narrow")
    wide_me, narrow_me = lax.axis_index("wide"), lax.axis_index("narrow")
    depth = width // wide_count
    part = width // narrow_count
    units = up_weight.shape[1]
    heads = part // HEAD
    clips = condition.shape[0]
    span = math.gcd(rows, PATCHES)
    spans = rows // span
    sharing = PATCHES // span

    def twin(*blocks):
        return Sent(*[swap(block, "wide", 1) for block in blocks])

    def hop(block, axis, bit):
        return Sent(swap(block, axis, bit))

    attn = Gather(
        jnp.concatenate([project_weight.reshape(depth, 3 * part), merge_weight.T], axis=1)
    )
    up, down_shard = Gather(up_weight), down_weight.T
    attn.start()
    z_bits = bits_of(wide_count)[1:]
    narrow_bits = bits_of(narrow_count)
    active = jax.nn.silu(condition).astype(BF16)
    active_mine = lax.dynamic_slice_in_dim(active, wide_me * depth, depth, 1)
    mode_part = jnp.einsum("cd,dki->kci", active_mine, mod_weight, preferred_element_type=F32)
    unit_rows = units // part
    at = 6 * clips
    mode_part = mode_part + swap(mode_part, "wide", 1)
    for bit in z_bits:
        sent = hop(mode_part, "wide", bit)
        if bit == z_bits[0]:
            (mode_part,) = land([sent, attn], mode_part)
        else:
            mode_part, attn.own = land([sent], mode_part, attn.own)
        mode_part = mode_part + sent.got[0]
    small = jnp.concatenate(
        [
            (mode_part + mod_bias.astype(F32)[:, None]).reshape(at, part),
            project_bias.astype(F32),
            merge_bias.astype(F32)[None],
            down_bias.astype(F32)[None],
            up_bias.astype(F32).reshape(unit_rows, part),
        ],
        axis=0,
    )
    span_frame = (narrow_me * rows + jnp.arange(spans, dtype=jnp.int32) * span) // PATCHES
    span_clip = jnp.sum(
        jnp.where(
            span_frame[:, None] == jnp.arange(frame_clip.shape[0], dtype=jnp.int32)[None],
            frame_clip[None],
            0,
        ),
        axis=1,
    )
    attn.start()
    sent = Sent(*spread(small, "narrow", narrow_bits)[1:])
    small, span_clip, up.own = land([sent, attn], small, span_clip, up.own)
    while attn.in_front():
        attn.start()
        land([attn])
    attn.start()
    up.start()
    modes, out_bias, qkv_bias, up_bias_all, core_grad, down_bias_grad, core_own, core_other = unpack_call(
        span_clip, narrow_me, clips, [small, *sent.got], out_cotangent
    )
    (modes,) = land([attn, up, attn.cross("own")], modes)
    while len(up.front) - up.stage > 1:
        up.start()
        land([up])
    attn.start()
    up.start()
    modes, down_shard = land([attn, up, attn.cross("first")], modes, down_shard)
    down = Whole(down_shard)
    attn_far = attn.cross("second", "third", "fourth")
    up.start()
    modes, up.own = land([attn_far], modes, up.own)
    attn.finish()

    attn_w = Weight(attn)
    up_own = up.cross("own")
    hidden_a, qkv, merge_w = project_call(attn_w, tokens, modes, qkv_bias, part)
    qkv, hidden_a = land([up, up_own], qkv, hidden_a)
    up.start()
    up_near = up.cross("first")
    qkv_frames = share(qkv, sharing)
    attended = attend(qkv_frames, heads)
    if sharing > 1:
        attended = attended.reshape(rows * sharing, narrow_count // sharing, part)
        attended = unshare(attended.transpose(1, 0, 2), sharing)
        attended = attended.transpose(1, 0, 2).reshape(rows, width)
    attended, hidden_a = land([up, up_near], attended, hidden_a)
    up_far = up.cross("second", "third", "fourth")
    branch_a, hidden_b = merge_call(attended, merge_w, tokens, modes, out_bias[0])
    hidden_b, attended, hidden_a = land([up_far], hidden_b, attended, hidden_a)
    up.finish()
    hidden_own, hidden_other = turn(hidden_a)
    hidden_twin = twin(hidden_other)
    up_w = Weight(up)
    gelu, slope, sent_part = up_call(up_w, hidden_b, up_bias_all, core_other)

    gelu, slope, hidden_b, sent_part = land([hidden_twin], gelu, slope, hidden_b, sent_part)
    down_cross = twin(sent_part)
    hidden_b_own, hidden_b_other = turn(hidden_b)
    down_w = down.finish()
    upper_grad, up_bias_grad, sent_part = gelu_back_call(down_w, core_grad, slope, hidden_b_other)
    upper_grad, sent_part, attended, gelu, core_own = land(
        [down_cross], upper_grad, sent_part, attended, gelu, core_own
    )
    up_cross = twin(sent_part)
    down_parts = weight_grad_call([core_own], [gelu], [], [], units, down_cross.got[0])
    upper_grad, attended, *down_parts = land([up_cross], upper_grad, attended, *down_parts)
    down_scatter = Scatter(*down_parts)
    attended_twin = twin(attended)
    middle_grad, merged_grad, sums_b, merge_bias_grad = up_back_call(
        up_w, upper_grad, tokens, branch_a, modes, out_cotangent
    )
    merged_grad, upper_grad = land([attended_twin], merged_grad, upper_grad)
    merged_own, merged_other = turn(merged_grad)
    merged_twin = twin(merged_other)
    (merged_grad,) = land([], merged_grad)

    if sharing > 1:
        attended_grad = jnp.dot(merged_grad, merge_w, preferred_element_type=F32).astype(BF16)
        attended_grad = attended_grad.reshape(rows, narrow_count, part).transpose(1, 0, 2)
        attended_grad = share(attended_grad, sharing).transpose(1, 0, 2)
        attended_grad = attended_grad.reshape(rows * sharing, width // sharing)
        qkv_grad = unshare(attend_back(qkv_frames, attended_grad, heads), sharing)
    else:
        qkv_grad = attend_back(qkv_frames, merged_grad, heads, merge_w)
    qkv_grad, upper_grad = land([down_scatter, merged_twin], qkv_grad, upper_grad)
    qkv_twin = twin(qkv_grad)
    up_parts = weight_grad_call(
        [hidden_b_own],
        [upper_grad],
        [merged_own, merged_twin.got[0]],
        [attended, attended_twin.got[0]],
        units,
        up_cross.got[0],
    )
    qkv_grad, *up_parts = land([down_scatter, qkv_twin], qkv_grad, *up_parts)
    up_scatter = Scatter(*up_parts)
    tokens_grad, sums_a, qkv_sums = project_back_call(
        attn_w, qkv_grad, tokens, middle_grad, modes, 3 * part
    )
    sums_a, qkv_grad = land([down_scatter], sums_a, qkv_grad)
    attn_parts = weight_grad_call(
        [hidden_own, hidden_twin.got[0]],
        [qkv_grad, qkv_twin.got[0]],
        [],
        [],
        3 * part,
    )
    gelu, *attn_parts = land([up_scatter, down_scatter], gelu, *attn_parts)
    attn_scatter = Scatter(*attn_parts)
    output, sums_g = down_call(
        down_w, gelu, tokens, branch_a, modes, out_bias[1], out_cotangent
    )
    (sums_g,) = land([up_scatter], sums_g)

    lower, upper = pack_call(
        span_clip, narrow_me, clips, sums_a, sums_b, sums_g, merge_bias_grad, down_bias_grad,
        qkv_sums, up_bias_grad,
    )
    sent = hop(upper, "narrow", narrow_bits[-1])
    (lower,) = land([sent, attn_scatter, up_scatter], lower)
    packed = lower + sent.got[0]
    for bit in reversed(narrow_bits[:-1]):
        sent = hop(packed[bit:], "narrow", bit)
        (packed,) = land([sent], packed)
        packed = packed[:bit] + sent.got[0]
    packed = packed[0]
    sent = hop(packed, "wide", 1)
    (packed,) = land([sent], packed)
    packed = packed + sent.got[0]
    for bit in z_bits:
        sent = hop(packed, "wide", bit)
        scatters = {z_bits[0]: [attn_scatter], z_bits[-1]: [up_scatter]}
        (packed,) = land([sent, *scatters.get(bit, [])], packed)
        packed = packed + sent.got[0]
    clip_slice = packed[:at].reshape(6, clips, part)
    active_grad = jnp.einsum(
        "kci,dki->cd", clip_slice, mod_weight.astype(F32), precision=lax.Precision.HIGHEST
    )
    for bit in narrow_bits:
        sent = hop(active_grad, "narrow", bit)
        (active_grad,) = land(
            [sent, attn_scatter] if bit == narrow_bits[-1] else [sent], active_grad
        )
        active_grad = active_grad + sent.got[0]
    active_grad = active_grad[None]
    for bit in bits_of(wide_count):
        sent = hop(active_grad, "wide", bit)
        (active_grad,) = land([sent], active_grad)
        active_grad = jnp.concatenate([active_grad, sent.got[0]], axis=0)
    active_grad = turned(active_grad, "wide").transpose(1, 0, 2).reshape(clips, width)
    unused, silu_pullback = jax.vjp(jax.nn.silu, condition)
    condition_grad = silu_pullback(active_grad)[0]
    mod_bias_grad = jnp.sum(clip_slice, axis=1)
    mod_weight_grad = jnp.einsum(
        "cd,kci->dki", active_mine.astype(F32), clip_slice, precision=lax.Precision.HIGHEST
    )

    for scatter in (down_scatter, up_scatter, attn_scatter):
        while scatter.stage < scatter.stages:
            land([scatter])
    return (
        output,
        tokens_grad,
        condition_grad,
        mod_weight_grad,
        mod_bias_grad,
        attn_scatter.result.reshape(depth, 3, part),
        packed[at : at + 2],
        up_scatter.result[:, units:].T,
        packed[at + 2],
        up_scatter.result[:, :units],
        packed[at + 4 :].reshape(units),
        down_scatter.result.T,
        packed[at + 3],
    )


def solution(mesh):
    both = P(("wide", "narrow"), None)
    ins = (
        both,
        P(),
        P("wide"),
        P("wide", None, "narrow"),
        P(None, "narrow"),
        P("wide", None, "narrow"),
        P(None, "narrow"),
        P("narrow", "wide"),
        P("narrow"),
        P("wide", "narrow"),
        P("narrow"),
        P("narrow", "wide"),
        P("narrow"),
        both,
    )
    outs = (
        both,
        both,
        P(),
        P("wide", None, "narrow"),
        P(None, "narrow"),
        P("wide", None, "narrow"),
        P(None, "narrow"),
        P("narrow", "wide"),
        P("narrow"),
        P("wide", "narrow"),
        P("narrow"),
        P("narrow", "wide"),
        P("narrow"),
    )
    return jax.shard_map(shards, mesh=mesh, in_specs=ins, out_specs=outs, check_vma=False)
```

```python
import functools
import math

import jax
import jax.numpy as jnp
from jax import lax
from jax.experimental import pallas as pl
from jax.experimental.pallas import tpu as pltpu
from jax.sharding import PartitionSpec as P

HEAD = 72
PATCHES = 256
EPSILON = 1e-06
MIB = 1 << 20
F32 = jnp.float32
BF16 = jnp.bfloat16


def bits_of(size):
    return [1 << k for k in range(size.bit_length() - 1)]


def swap(block, axis, bit):
    count = lax.axis_size(axis)
    return lax.ppermute(block, axis, [(i, i ^ bit) for i in range(count)])


def my_bit(axis, bit):
    return (lax.axis_index(axis) // bit) % 2


def tied(*values):
    return lax.optimization_barrier(values)


def dot(a, b, ca, cb):
    return lax.dot_general(a, b, (((ca,), (cb,)), ((), ())), preferred_element_type=F32)


def row_mean(values):
    return jnp.mean(values, axis=1, keepdims=True)


def normalize(values):
    center = row_mean(values)
    inverse = lax.rsqrt(row_mean(values * values) - center * center + EPSILON)
    return inverse, (values - center) * inverse


def norm_back(incoming, normed, inverse):
    return inverse * (incoming - row_mean(incoming) - normed * row_mean(incoming * normed))


def gelu_both(upper):
    c0 = math.sqrt(2.0 / math.pi)
    square = upper * upper
    tanh = jnp.tanh(upper * (c0 + (c0 * 0.044715) * square))
    half = 0.5 + 0.5 * tanh
    bend = (half * (1.0 - half)) * (2.0 * c0 + (2.0 * c0 * 0.134145) * square)
    return upper * half, half + upper * bend


def params(limit=56):
    return pltpu.CompilerParams(vmem_limit_bytes=limit * MIB)


def cost():
    return pl.CostEstimate(flops=100000000, bytes_accessed=1, transcendentals=0)


def whole(array):
    return pl.BlockSpec(array.shape, lambda i, *_: (0,) * array.ndim)


def along(array):
    return pl.BlockSpec((1,) + array.shape[1:], lambda i, *_: (i,) + (0,) * (array.ndim - 1))


def shape_of(shape, dtype):
    return jax.ShapeDtypeStruct(shape, dtype)


def attend_kernel(heads, qkv_ref, out_ref):
    part = heads * HEAD
    scale = HEAD ** (-0.5)
    results = []
    for n in range(qkv_ref.shape[0]):
        qs, ks, vs = [
            [qkv_ref[n, :, i * part + h * HEAD : i * part + (h + 1) * HEAD] for h in range(heads)]
            for i in range(3)
        ]
        scores = [dot(k, q, 1, 1) for k, q in zip(ks, qs)]
        probs = []
        for s in scores:
            p = jnp.exp((s - jnp.max(s, axis=0, keepdims=True)) * scale)
            probs.append((p.astype(BF16), 1.0 / jnp.sum(p, axis=0, keepdims=True)))
        for (p, weight), v in zip(probs, vs):
            results.append(dot(v, p, 0, 0) * weight)
    out_ref[...] = jnp.concatenate(results, axis=0).T.astype(BF16)


def attend(qkv, heads):
    groups, rows, cols = qkv.shape
    width = groups * heads * HEAD
    out = shape_of((rows, width), BF16)
    return pl.pallas_call(
        functools.partial(attend_kernel, heads),
        grid=(rows // PATCHES,),
        in_specs=[pl.BlockSpec((groups, PATCHES, cols), lambda f: (0, f, 0))],
        out_specs=pl.BlockSpec((PATCHES, width), lambda f: (f, 0)),
        out_shape=out,
        compiler_params=params(),
        cost_estimate=cost(),
        name="attend",
    )(qkv)


def attend_back_kernel(heads, qkv_ref, grad_ref, *refs):
    out_ref = refs[-1]
    part = heads * HEAD
    scale = HEAD ** (-0.5)
    pad = out_ref.shape[2] - 3 * part
    grad = grad_ref[...]
    if len(refs) > 1:
        grad = dot(grad, refs[0][...], 1, 0).astype(BF16)
    for n in range(qkv_ref.shape[0]):
        qs, ks, vs = [
            [qkv_ref[n, :, i * part + h * HEAD : i * part + (h + 1) * HEAD] for h in range(heads)]
            for i in range(3)
        ]
        gs = [grad[:, n * part + h * HEAD : n * part + (h + 1) * HEAD] for h in range(heads)]
        scores = [dot(k, q, 1, 1) for k, q in zip(ks, qs)]
        slopes = [dot(v, g, 1, 1) for v, g in zip(vs, gs)]
        probs, score_grads = [], []
        for s, dp in zip(scores, slopes):
            p = jnp.exp((s - jnp.max(s, axis=0, keepdims=True)) * scale)
            p = p * (1.0 / jnp.sum(p, axis=0, keepdims=True))
            probs.append(p.astype(BF16))
            score_grads.append((p * (dp - jnp.sum(p * dp, axis=0, keepdims=True))).astype(BF16))
        dvs = [dot(p, g, 1, 0) for p, g in zip(probs, gs)]
        dks = [dot(ds, q, 1, 0) * scale for ds, q in zip(score_grads, qs)]
        dqs = [dot(k, ds, 0, 0) * scale for ds, k in zip(score_grads, ks)]
        dq = jnp.concatenate(dqs, axis=0).T
        zeros = [jnp.zeros((PATCHES, pad), F32)] if pad else []
        out_ref[n] = jnp.concatenate([dq] + dks + dvs + zeros, axis=1).astype(BF16)


def attend_back(qkv, grad, heads, weight=None):
    groups, rows, cols = qkv.shape
    width = groups * heads * HEAD
    out = shape_of((groups, rows, -(-cols // 128) * 128), BF16)
    more = [] if weight is None else [weight]
    return pl.pallas_call(
        functools.partial(attend_back_kernel, heads),
        grid=(rows // PATCHES,),
        in_specs=[
            pl.BlockSpec((groups, PATCHES, cols), lambda f: (0, f, 0)),
            pl.BlockSpec((PATCHES, width), lambda f: (f, 0)),
        ]
        + [whole(a) for a in more],
        out_specs=pl.BlockSpec((groups, PATCHES, out.shape[2]), lambda f: (0, f, 0)),
        out_shape=out,
        compiler_params=params(),
        cost_estimate=cost(),
        name="attend_back",
    )(qkv, grad, *more)


class Sent:
    def __init__(self, *values):
        self.pending = list(values)

    def take(self, got):
        self.got = got
        self.pending = []


def land(sents, *ties):
    sents = [sent for sent in sents if sent.pending]
    pending = [value for sent in sents for value in sent.pending]
    values = list(tied(*pending, *ties))
    for sent in sents:
        count = len(sent.pending)
        sent.take(values[:count])
        values = values[count:]
    return values


class Gather:
    def __init__(self, shard):
        self.depth, self.cols = shard.shape
        self.cut = max(16, self.depth // 2 // 16 * 16)
        wide = [("wide", bit) for bit in reversed(bits_of(lax.axis_size("wide")))]
        narrow = [("narrow", bit) for bit in reversed(bits_of(lax.axis_size("narrow")))]
        self.core = wide[-1]
        self.front = wide[:-1] + narrow[:-2]
        self.last = narrow[-2:]
        self.own = shard[None]
        self.stage = 0
        self.pending = []
        self.crossed = {}

    def in_front(self):
        return self.stage < len(self.front)

    def start(self):
        if self.in_front():
            self.pending = [swap(self.own, *self.front[self.stage])]
        elif self.stage == len(self.front):
            self.pending = [swap(self.own, *key) for key in self.last]
        else:
            self.pending = [
                swap(self.first[:, : self.cut], *self.last[1]),
                swap(self.second[:, self.cut :], *self.last[0]),
            ]
        return self

    def take(self, got):
        self.pending = []
        if self.in_front():
            self.own = jnp.concatenate([self.own, got[0]], axis=0)
        elif self.stage == len(self.front):
            self.first, self.second = got
        else:
            self.third, self.fourth = got
        self.stage += 1

    def cross(self, *names):
        sent = Sent(*[swap(getattr(self, name), *self.core) for name in names])
        for i, name in enumerate(names):
            self.crossed[name] = (sent, i)
        return sent

    def finish(self):
        names = ["own", "first", "second", "third", "fourth"]
        self.arrays = [getattr(self, name) for name in names]
        for name in names:
            sent, i = self.crossed[name]
            self.arrays.append(sent.got[i])
        return self

    def entries(self, n):
        found = []
        (unused, high), (unused, low) = self.last
        whole_rows, cut = (0, self.depth), self.cut
        for w in range(lax.axis_size("wide")):
            index = 0
            for j, (axis, bit) in enumerate(self.front):
                index += bool((n if axis == "narrow" else w) & bit) << j
            side = 5 * bool(w & self.core[1])
            if n & high and n & low:
                parts = [(3, 0, cut), (4, cut, self.depth - cut)]
            else:
                parts = [(1 if n & high else 2 if n & low else 0, 0, self.depth)]
            found += [(side + which, index, w, offset, size) for which, offset, size in parts]
        return found

    def assembled(self):
        sides = []
        for side in (0, 5):
            own, first, second, third, fourth = self.arrays[side : side + 5]
            across = jnp.concatenate([third, fourth], axis=1)
            sides.append(jnp.stack([jnp.stack([own, second]), jnp.stack([first, across])]))
        block = jnp.stack(sides)
        keys = [self.core, *self.last, *self.front[::-1]]
        block = block.reshape([2] * len(keys) + [self.depth, self.cols])
        narrow = [("narrow", bit) for bit in reversed(bits_of(lax.axis_size("narrow")))]
        wide = [("wide", bit) for bit in reversed(bits_of(lax.axis_size("wide")))]
        order = [keys.index(key) for key in narrow + wide]
        block = block.transpose(order + [len(keys), len(keys) + 1])
        for dim, key in enumerate(wide):
            dim += len(narrow)
            block = jnp.where(my_bit(*key) == 1, jnp.flip(block, dim), block)
        return block.reshape(lax.axis_size("narrow"), -1, self.cols)


class Weight:
    def __init__(self, gather):
        groups = lax.axis_size("narrow")
        self.depth, self.cols = gather.depth, gather.cols
        if gather.cut % 16 or gather.depth % 16:
            self.arrays = [gather.assembled()]
            self.plan = [[(0, n, None, 0, 0)] for n in range(groups)]
        else:
            self.arrays = gather.arrays
            self.plan = [gather.entries(n) for n in range(groups)]


class Whole:
    def __init__(self, shard):
        self.depth, self.cols = shard.shape
        groups = lax.axis_size("narrow")
        blocks = lax.all_gather(shard, ("narrow", "wide"), axis=0)
        self.blocks = blocks.reshape(groups, lax.axis_size("wide") * self.depth, self.cols)

    def finish(self):
        self.arrays = [self.blocks]
        self.plan = [[(0, n, None, 0, 0)] for n in range(lax.axis_size("narrow"))]
        return self


def stream(step, weight, me, refs, buffer, sems, before):
    plan = weight.plan

    def issue(n):
        for which, index, w, offset, size in plan[n]:
            if w is None:
                target = buffer.at[n % 2]
                if isinstance(weight, Whole):
                    index = me[1] ^ index
            else:
                row = pl.multiple_of((me[0] ^ w) * weight.depth + offset, 16)
                target = buffer.at[n % 2, pl.ds(row, size)]
            pltpu.make_async_copy(refs[which].at[index], target, sems.at[n % 2]).start()

    @pl.when(step == -before)
    def _():
        issue(0)
        pltpu.make_async_copy(buffer.at[0], buffer.at[0], sems.at[0]).wait()
        issue(1)

    for n in range(1, len(plan)):

        @pl.when(step == n)
        def _():
            pltpu.make_async_copy(buffer.at[n % 2], buffer.at[n % 2], sems.at[n % 2]).wait()
            if n + 1 < len(plan):
                issue(n + 1)

    return buffer.at[jnp.clip(step, 0, len(plan) - 1) % 2]


def group_at(array, before, groups):
    def index(i, *_):
        return (jnp.clip(i - before, 0, groups - 1),) + (0,) * (array.ndim - 1)

    return pl.BlockSpec((1,) + array.shape[1:], index)


def rows_at(array, first, spans):
    def index(i, *_):
        return (jnp.clip(i - first, 0, spans - 1),) + (0,) * (array.ndim - 1)

    return pl.BlockSpec((array.shape[0] // spans,) + array.shape[1:], index)


def weight_call(body, weight, ins, in_specs, outs, out_specs, scratch, name, before=0, after=0):
    count, groups = len(weight.arrays), len(weight.plan)
    width = lax.axis_size("wide") * weight.depth

    def kernel(me_ref, *refs):
        step = pl.program_id(0) - before
        in_refs = refs[: len(ins)]
        weight_refs = refs[len(ins) : len(ins) + count]
        out_refs = refs[len(ins) + count : len(ins) + count + len(outs)]
        buffer, sems = refs[len(ins) + count + len(outs) :][:2]
        scratch_refs = refs[len(ins) + count + len(outs) + 2 :]
        w = stream(step, weight, me_ref, weight_refs, buffer, sems, before)
        body(step, in_refs, w, out_refs, scratch_refs)

    me = jnp.stack([lax.axis_index("wide"), lax.axis_index("narrow")]).astype(jnp.int32)
    return pl.pallas_call(
        kernel,
        grid_spec=pltpu.PrefetchScalarGridSpec(
            num_scalar_prefetch=1,
            grid=(before + groups + after,),
            in_specs=list(in_specs) + [pl.BlockSpec(memory_space=pl.ANY)] * count,
            out_specs=list(out_specs),
            scratch_shapes=[
                pltpu.VMEM((2, width, weight.cols), BF16),
                pltpu.SemaphoreType.DMA((2,)),
            ]
            + list(scratch),
        ),
        out_shape=list(outs),
        compiler_params=params(),
        cost_estimate=cost(),
        name=name,
    )(me, *ins, *weight.arrays)


def project_call(weight, tokens, modes, bias, part):
    rows, width = tokens.shape
    spans, span = modes.shape[0], rows // modes.shape[0]
    groups = len(weight.plan)
    outs = [
        shape_of((rows, width), BF16),
        shape_of((groups, rows, 3 * part), BF16),
        shape_of((width, groups * part), BF16),
    ]

    before = spans - 1

    def body(step, ins, w, out, scratch):
        tokens_ref, modes_ref, bias_ref = ins
        hidden_ref, qkv_ref, merge_ref = out
        held = scratch[0]

        @pl.when(step <= 0)
        def _():
            at = pl.ds(pl.multiple_of((step + before) * span, span), span)
            unused, normed = normalize(tokens_ref[...].astype(F32))
            hidden = (normed * (1.0 + modes_ref[0, 1:2]) + modes_ref[0, 0:1]).astype(BF16)
            hidden_ref[...] = hidden
            held[at, :] = hidden
            qkv_ref[0, at, :] = (dot(hidden, w[:, : 3 * part], 1, 0) + bias_ref[0]).astype(BF16)

        @pl.when(step > 0)
        def _():
            qkv_ref[0] = (dot(held[...], w[:, : 3 * part], 1, 0) + bias_ref[0]).astype(BF16)

        for n in range(groups):

            @pl.when(step == n)
            def _():
                merge_ref[:, n * part : (n + 1) * part] = w[:, 3 * part :]

    return weight_call(
        body,
        weight,
        [tokens, modes, bias],
        [rows_at(tokens, 0, spans), rows_at(modes, 0, spans), group_at(bias, before, groups)],
        outs,
        [rows_at(outs[0], 0, spans), group_at(outs[1], before, groups), whole(outs[2])],
        [pltpu.VMEM((rows, width), BF16)],
        "project",
        before=before,
    )


def merge_kernel(attended_ref, weight_ref, tokens_ref, modes_ref, bias_ref, branch_ref, hidden_ref):
    branch = dot(attended_ref[...], weight_ref[...], 1, 1) + bias_ref[...]
    branch_ref[...] = branch
    middle = tokens_ref[...].astype(F32) + modes_ref[0, 2:3] * branch
    unused, normed = normalize(middle)
    hidden_ref[...] = (normed * (1.0 + modes_ref[0, 4:5]) + modes_ref[0, 3:4]).astype(BF16)


def merge_call(attended, weight, tokens, modes, bias):
    rows, width = tokens.shape
    spans, span = modes.shape[0], rows // modes.shape[0]
    block = pl.BlockSpec((span, width), lambda i: (i, 0))
    outs = [shape_of((rows, width), F32), shape_of((rows, width), BF16)]
    return pl.pallas_call(
        merge_kernel,
        grid=(spans,),
        in_specs=[block, whole(weight), block, along(modes), whole(bias)],
        out_specs=[block, block],
        out_shape=outs,
        compiler_params=params(),
        cost_estimate=cost(),
        name="merge",
    )(attended, weight, tokens, modes, bias)


def up_call(weight, hidden, bias, left):
    rows, width = hidden.shape
    groups, units = len(weight.plan), weight.cols
    zs, depth = left.shape[:2]
    outs = [shape_of((groups, rows, units), BF16)] * 2 + [shape_of((groups, zs, depth, units), BF16)]

    def body(step, ins, w, out, scratch):
        hidden_ref, bias_ref, left_ref = ins
        gelu, slope = gelu_both(dot(hidden_ref[...], w[...], 1, 0) + bias_ref[0])
        gelu = gelu.astype(BF16)
        out[0][0] = gelu
        out[1][0] = slope.astype(BF16)
        part = dot(left_ref[...].reshape(zs * depth, rows), gelu, 1, 0)
        out[2][0] = part.astype(BF16).reshape(zs, depth, units)

    return weight_call(
        body,
        weight,
        [hidden, bias, left],
        [whole(hidden), along(bias), whole(left)],
        outs,
        [along(out) for out in outs],
        [],
        "up",
    )


def down_call(weight, gelu, tokens, branch, modes, bias, grad):
    rows, width = tokens.shape
    spans, span = modes.shape[0], rows // modes.shape[0]
    groups, units = len(weight.plan), weight.cols
    outs = [shape_of((rows, width), BF16), shape_of((spans, 1, width), F32)]

    def body(step, ins, w, out, scratch):
        gelu_ref, tokens_ref, branch_ref, modes_ref, bias_ref, grad_ref = ins
        total = scratch[0]

        @pl.when(step == 0)
        def _():
            total[...] = dot(gelu_ref[0], w[...], 1, 1)

        @pl.when((step > 0) & (step < groups - 1))
        def _():
            total[...] += dot(gelu_ref[0], w[...], 1, 1)

        @pl.when(step >= groups - 1)
        def _():
            at = pl.ds(pl.multiple_of((step - groups + 1) * span, span), span)
            other = total[at, :] + dot(gelu_ref[0, at, :], w[...], 1, 1) + bias_ref[...]
            middle = tokens_ref[...].astype(F32) + modes_ref[0, 2:3] * branch_ref[...]
            out[0][...] = (middle + modes_ref[0, 5:6] * other).astype(BF16)
            out[1][0] = jnp.sum(grad_ref[...].astype(F32) * other, axis=0, keepdims=True)

    def by_span(array):
        return rows_at(array, groups - 1, spans)

    return weight_call(
        body,
        weight,
        [gelu, tokens, branch, modes, bias, grad],
        [group_at(gelu, 0, groups), by_span(tokens), by_span(branch), by_span(modes), whole(bias), by_span(grad)],
        outs,
        [by_span(outs[0]), by_span(outs[1])],
        [pltpu.VMEM((rows, width), F32)],
        "down",
        after=spans - 1,
    )


def gelu_back_call(weight, grad, slope, left):
    rows, width = grad.shape
    groups, units = len(weight.plan), weight.cols
    zs, depth = left.shape[:2]
    outs = [
        shape_of((groups, rows, units), BF16),
        shape_of((groups, 1, units), F32),
        shape_of((groups, zs, depth, units), BF16),
    ]

    def body(step, ins, w, out, scratch):
        grad_ref, slope_ref, left_ref = ins
        upper = (dot(grad_ref[...], w[...], 1, 0) * slope_ref[0].astype(F32)).astype(BF16)
        out[0][0] = upper
        out[1][0] = jnp.sum(upper.astype(F32), axis=0, keepdims=True)
        part = dot(left_ref[...].reshape(zs * depth, rows), upper, 1, 0)
        out[2][0] = part.astype(BF16).reshape(zs, depth, units)

    return weight_call(
        body,
        weight,
        [grad, slope, left],
        [whole(grad), along(slope), whole(left)],
        outs,
        [along(out) for out in outs],
        [],
        "gelu_back",
    )


def up_back_call(weight, upper, tokens, branch, modes, grad):
    rows, width = tokens.shape
    spans, span = modes.shape[0], rows // modes.shape[0]
    groups, units = len(weight.plan), weight.cols
    outs = [
        shape_of((rows, width), F32),
        shape_of((rows, width), BF16),
        shape_of((spans, 3, width), F32),
        shape_of((1, width), F32),
    ]

    def body(step, ins, w, out, scratch):
        upper_ref, tokens_ref, branch_ref, modes_ref, grad_ref = ins
        middle_ref, merged_ref, sums_ref, bias_ref = out
        total = scratch[0]

        @pl.when(step == 0)
        def _():
            total[...] = dot(upper_ref[0], w[...], 1, 1)
            bias_ref[...] = jnp.zeros_like(bias_ref)

        @pl.when((step > 0) & (step < groups - 1))
        def _():
            total[...] += dot(upper_ref[0], w[...], 1, 1)

        @pl.when(step >= groups - 1)
        def _():
            at = pl.ds(pl.multiple_of((step - groups + 1) * span, span), span)
            hidden = total[at, :] + dot(upper_ref[0, at, :], w[...], 1, 1)
            branch = branch_ref[...]
            gate = modes_ref[0, 2:3]
            inverse, normed = normalize(tokens_ref[...].astype(F32) + gate * branch)
            back = norm_back(hidden * (1.0 + modes_ref[0, 4:5]), normed, inverse)
            middle = grad_ref[...].astype(F32) + back
            gated = gate * middle
            middle_ref[...] = middle
            merged_ref[...] = gated.astype(BF16)
            sums_ref[0, 0:1] = jnp.sum(middle * branch, axis=0, keepdims=True)
            sums_ref[0, 1:2] = jnp.sum(hidden, axis=0, keepdims=True)
            sums_ref[0, 2:3] = jnp.sum(hidden * normed, axis=0, keepdims=True)
            bias_ref[...] += jnp.sum(gated, axis=0, keepdims=True)

    def by_span(array):
        return rows_at(array, groups - 1, spans)

    return weight_call(
        body,
        weight,
        [upper, tokens, branch, modes, grad],
        [group_at(upper, 0, groups)] + [by_span(a) for a in (tokens, branch, modes, grad)],
        outs,
        [by_span(a) for a in outs[:3]] + [whole(outs[3])],
        [pltpu.VMEM((rows, width), F32)],
        "up_back",
        after=spans - 1,
    )


def project_back_call(weight, qkv_grad, tokens, middle, modes, cols):
    rows, width = tokens.shape
    spans, span = modes.shape[0], rows // modes.shape[0]
    groups = len(weight.plan)
    outs = [
        shape_of((rows, width), F32),
        shape_of((spans, 2, width), F32),
        shape_of((groups, 1, cols), F32),
    ]

    def body(step, ins, w, out, scratch):
        grad_ref, tokens_ref, middle_ref, modes_ref = ins
        tokens_grad_ref, sums_ref, bias_ref = out
        total = scratch[0]

        @pl.when(step < groups)
        def _():
            bias_ref[0] = jnp.sum(grad_ref[0, :, :cols].astype(F32), axis=0, keepdims=True)

        @pl.when(step == 0)
        def _():
            total[...] = dot(grad_ref[0, :, :cols], w[:, :cols], 1, 1)

        @pl.when((step > 0) & (step < groups - 1))
        def _():
            total[...] += dot(grad_ref[0, :, :cols], w[:, :cols], 1, 1)

        @pl.when(step >= groups - 1)
        def _():
            at = pl.ds(pl.multiple_of((step - groups + 1) * span, span), span)
            inverse, normed = normalize(tokens_ref[...].astype(F32))
            hidden = total[at, :] + dot(grad_ref[0, at, :cols], w[:, :cols], 1, 1)
            back = norm_back(hidden * (1.0 + modes_ref[0, 1:2]), normed, inverse)
            tokens_grad_ref[...] = middle_ref[...] + back
            sums_ref[0, 0:1] = jnp.sum(hidden, axis=0, keepdims=True)
            sums_ref[0, 1:2] = jnp.sum(hidden * normed, axis=0, keepdims=True)

    def by_span(array):
        return rows_at(array, groups - 1, spans)

    return weight_call(
        body,
        weight,
        [qkv_grad, tokens, middle, modes],
        [group_at(qkv_grad, 0, groups)] + [by_span(a) for a in (tokens, middle, modes)],
        outs,
        [by_span(outs[0]), by_span(outs[1]), group_at(outs[2], 0, groups)],
        [pltpu.VMEM((rows, width), F32)],
        "project_back",
        after=spans - 1,
    )


def put_turned(depth, side, block, own_ref, other_ref):
    turned_block = block.T
    for z in range(own_ref.shape[0]):
        even = turned_block[2 * z * depth : (2 * z + 1) * depth]
        odd = turned_block[(2 * z + 1) * depth : (2 * z + 2) * depth]
        own_ref[z] = jnp.where(side == 1, odd, even)
        other_ref[z] = jnp.where(side == 1, even, odd)


def turn_kernel(depth, me_ref, block_ref, own_ref, other_ref):
    put_turned(depth, me_ref[0] & 1, block_ref[...], own_ref, other_ref)


def turn(block):
    rows, width = block.shape
    blocks = lax.axis_size("wide")
    out = shape_of((blocks // 2, width // blocks, rows), BF16)
    me = lax.axis_index("wide").astype(jnp.int32)[None]
    own, other = pl.pallas_call(
        functools.partial(turn_kernel, width // blocks),
        grid_spec=pltpu.PrefetchScalarGridSpec(
            num_scalar_prefetch=1, grid=(1,), in_specs=[whole(block)], out_specs=[whole(out)] * 2
        ),
        out_shape=[out, out],
        compiler_params=params(24),
        cost_estimate=cost(),
        name="turn",
    )(me, block)
    return own, other


def weight_grad_call(lefts, grads, merged, attended, cols, added=None):
    zs, size, rows = lefts[0].shape
    groups = grads[0].shape[0]
    width = 2 * zs * size
    cut = max(16, size // 2 // 16 * 16)
    part = width // groups if merged else 0
    half = groups // 2
    outs = []
    for height in (cut, cut, size - cut, size - cut):
        outs.append(shape_of((half, zs, height, cols + part), BF16))
    more = [] if added is None else [added]
    ins = [*lefts, *grads, *more, *merged, *attended]
    count = len(lefts)

    def product(left_refs, right_refs):
        terms = [
            dot(left[...].reshape(zs * size, rows), right, 1, 0)
            for left, right in zip(left_refs, right_refs)
        ]
        return sum(terms[1:], terms[0])

    def kernel(*refs):
        step = pl.program_id(0)
        left_refs, grad_refs, rest = refs[:count], refs[count : 2 * count], refs[2 * count : len(ins)]
        out_refs, scratch = refs[len(ins) : len(ins) + 4], refs[len(ins) + 4 :]
        result = product(left_refs, [ref[0, :, :cols] for ref in grad_refs])
        if more:
            result = result + rest[0][0].reshape(zs * size, cols).astype(F32)
        result = result.astype(BF16)
        if merged:

            @pl.when(step == 0)
            def _():
                pairs = rest[len(more) :]
                values = [ref[...] for ref in pairs[len(merged) :]]
                scratch[0][...] = product(pairs[: len(merged)], values).astype(BF16)

        for n in range(groups):

            @pl.when(step == n)
            def _():
                value = result
                if merged:
                    value = jnp.concatenate([value, scratch[0][:, n * part : (n + 1) * part]], axis=1)
                first = out_refs[0] if n < half else out_refs[1]
                second = out_refs[2] if n % 2 == 0 else out_refs[3]
                for z in range(zs):
                    first[0, z] = value[z * size : z * size + cut]
                    second[0, z] = value[z * size + cut : (z + 1) * size]

    rest = (0, 0, 0)
    out_specs = [
        pl.BlockSpec((1,) + out.shape[1:], index)
        for out, index in zip(
            outs,
            [
                lambda i: (jnp.minimum(i, half - 1),) + rest,
                lambda i: (jnp.maximum(i - half, 0),) + rest,
                lambda i: (i // 2,) + rest,
                lambda i: (i // 2,) + rest,
            ],
        )
    ]
    return pl.pallas_call(
        kernel,
        grid=(groups,),
        in_specs=[whole(a) for a in lefts]
        + [along(a) for a in (*grads, *more)]
        + [whole(a) for a in (*merged, *attended)],
        out_specs=out_specs,
        scratch_shapes=[pltpu.VMEM((zs * size, width), BF16)] if merged else [],
        out_shape=outs,
        compiler_params=params(),
        cost_estimate=cost(),
        name="weight_grad",
    )(*ins)


def plus(a, b):
    return (a.astype(F32) + b.astype(F32)).astype(BF16)


class Scatter:
    def __init__(self, first_kept, first_sent, second_kept, second_sent):
        narrow = list(reversed(bits_of(lax.axis_size("narrow"))))
        self.orders = [narrow, narrow[::-1]]
        self.left = [list(narrow), list(narrow)]
        self.front = list(bits_of(lax.axis_size("wide")))[1:]
        self.stage = 0
        self.stages = len(narrow) + len(self.front)
        self.kept, self.pending = [], []
        sides = ((first_kept, first_sent), (second_kept, second_sent))
        for part, (kept, sent) in enumerate(sides):
            bit = self.orders[part][0]
            self.left[part].remove(bit)
            self.kept.append(kept.reshape([2] * (len(narrow) - 1) + list(kept.shape[1:])))
            self.pending.append(swap(sent.reshape(self.kept[-1].shape), "narrow", bit))

    def take(self, got):
        self.got = list(got)
        self.go()

    def wait(self):
        sent = Sent(*self.pending)
        sent.take = lambda got: setattr(self, "got", list(got))
        self.pending = []
        return sent

    def go(self):
        kept, got, narrow = self.kept, self.got, len(self.orders[0])
        self.stage += 1
        if self.stage < narrow:
            self.kept, self.pending = [], []
            for part, order in enumerate(self.orders):
                bit = order[self.stage]
                dim = self.left[part].index(bit)
                self.left[part].remove(bit)
                stay, go = [
                    plus(
                        lax.index_in_dim(kept[part], side, dim, False),
                        lax.index_in_dim(got[part], side, dim, False),
                    )
                    for side in (0, 1)
                ]
                self.kept.append(stay)
                self.pending.append(swap(go, "narrow", bit))
        elif self.stage < self.stages:
            bit = self.front[self.stage - narrow]
            mine = my_bit("wide", bit)
            dim = len(self.front) - 1 - (self.stage - narrow)
            sides = []
            for side in (mine, 1 - mine):
                blocks = []
                for a, b in zip(kept, got):
                    if self.stage == narrow:
                        shape = [2] * len(self.front) + list(a.shape[1:])
                        a, b = a.reshape(shape), b.reshape(shape)
                    blocks.append(
                        plus(
                            lax.dynamic_index_in_dim(a, side, dim, False),
                            lax.dynamic_index_in_dim(b, side, dim, False),
                        )
                    )
                sides.append(jnp.concatenate(blocks, axis=-2) if len(blocks) > 1 else blocks[0])
            self.kept = [sides[0]]
            self.pending = [swap(sides[1], "wide", bit)]
        else:
            self.result = kept[0].astype(F32) + got[0].astype(F32)
            self.pending = []


def spread(block, axis, bits):
    blocks = [block]
    for index in range(1, 1 << len(bits)):
        mask = sum(bit for j, bit in enumerate(bits) if index >> j & 1)
        blocks.append(swap(block, axis, mask))
    return blocks


def tree_sum(blocks):
    while len(blocks) > 1:
        blocks = [blocks[i] + blocks[i + 1] for i in range(0, len(blocks), 2)]
    return blocks[0]


def unpack_call(span_clip, narrow_me, clips, blocks, grad):
    spans = span_clip.shape[0]
    rows, width = grad.shape
    span = rows // spans
    groups = len(blocks)
    height, part = blocks[0].shape
    at = 6 * clips
    units = (height - at - 4) * part
    wide = lax.axis_size("wide")
    outs = [
        shape_of((spans, 6, width), F32),
        shape_of((2, 1, width), F32),
        shape_of((groups, 1, 3 * part), F32),
        shape_of((groups, 1, units), F32),
        shape_of((rows, width), BF16),
        shape_of((1, width), F32),
        shape_of((wide // 2, width // wide, rows), BF16),
        shape_of((wide // 2, width // wide, rows), BF16),
    ]

    def kernel(clip_ref, me_ref, *refs):
        block_refs, grad_ref = refs[: len(blocks)], refs[len(blocks)]
        modes_ref, bias_ref, qkv_ref, up_ref, core_ref, sum_ref, own_ref, other_ref = refs[len(blocks) + 1 :]
        for rel, ref in enumerate(block_refs):
            owner = me_ref[0] ^ rel
            found = []
            for s in range(spans):
                for k in range(6):
                    found.append(ref[pl.ds(k * clips + clip_ref[s], 1), :])
            for n in range(groups):

                @pl.when(owner == n)
                def _():
                    lanes = slice(n * part, (n + 1) * part)
                    for s in range(spans):
                        for k in range(6):
                            modes_ref[s, k : k + 1, lanes] = found[6 * s + k]
                    for k in range(2):
                        bias_ref[k, :, lanes] = ref[at + 2 + k : at + 3 + k, :]

            qkv_ref[rel] = jnp.concatenate(
                [ref[at : at + 1, :], jnp.zeros((1, part), F32), ref[at + 1 : at + 2, :]], axis=1
            )
            for j in range(units // part):
                up_ref[rel, :, j * part : (j + 1) * part] = ref[at + 4 + j : at + 5 + j, :]
        for s in range(spans):
            lines = slice(s * span, (s + 1) * span)
            gated = modes_ref[s, 5:6] * grad_ref[lines, :].astype(F32)
            core_ref[lines, :] = gated.astype(BF16)
            here = jnp.sum(gated, axis=0, keepdims=True)
            sum_ref[...] = here if s == 0 else sum_ref[...] + here
        put_turned(width // wide, me_ref[1] & 1, core_ref[...], own_ref, other_ref)

    me = jnp.stack([narrow_me, lax.axis_index("wide")]).astype(jnp.int32)
    return pl.pallas_call(
        kernel,
        grid_spec=pltpu.PrefetchScalarGridSpec(
            num_scalar_prefetch=2,
            grid=(1,),
            in_specs=[whole(a) for a in (*blocks, grad)],
            out_specs=[whole(a) for a in outs],
        ),
        out_shape=outs,
        compiler_params=params(32),
        cost_estimate=cost(),
        name="unpack",
    )(span_clip, me, *blocks, grad)


def pack_call(span_clip, narrow_me, clips, sums_a, sums_b, sums_g, merge_bias, down_bias, qkv_sums, up_bias):
    spans, unused, width = sums_a.shape
    groups = qkv_sums.shape[0]
    part, units = width // groups, up_bias.shape[2]
    at = 6 * clips
    height = at + 4 + units // part
    outs = [shape_of((groups // 2, height, part), F32)] * 2
    ins = [sums_a, sums_b, sums_g, merge_bias, down_bias, qkv_sums, up_bias]

    def kernel(clip_ref, me_ref, a_ref, b_ref, g_ref, merge_ref, down_ref, qkv_ref, up_ref, *refs):
        total = refs[2]
        out_refs = [refs[rel // (groups // 2)].at[rel % (groups // 2)] for rel in range(groups)]
        total[...] = jnp.zeros_like(total)
        for s in range(spans):
            rows = [a_ref[s, 0:1], a_ref[s, 1:2]] + [b_ref[s, i : i + 1] for i in range(3)]
            rows.append(g_ref[s, 0:1])
            for k in range(6):
                row = pl.ds(k * clips + clip_ref[s], 1)
                total[row, :] += rows[k]
        total[at : at + 1, :] = merge_ref[...]
        total[at + 1 : at + 2, :] = down_ref[...]
        for rel in range(groups):
            owner = me_ref[0] ^ rel
            for n in range(groups):

                @pl.when(owner == n)
                def _():
                    own = total[:, n * part : (n + 1) * part]
                    out_refs[rel][:at, :] = own[:at]
                    out_refs[rel][at + 2 : at + 4, :] = own[at : at + 2]

            out_refs[rel][at : at + 1, :] = qkv_ref[rel, :, :part]
            out_refs[rel][at + 1 : at + 2, :] = qkv_ref[rel, :, 2 * part :]
            for j in range(units // part):
                out_refs[rel][at + 4 + j : at + 5 + j, :] = up_ref[rel, :, j * part : (j + 1) * part]

    return pl.pallas_call(
        kernel,
        grid_spec=pltpu.PrefetchScalarGridSpec(
            num_scalar_prefetch=2,
            grid=(1,),
            in_specs=[whole(a) for a in ins],
            out_specs=[whole(a) for a in outs],
            scratch_shapes=[pltpu.VMEM((at + 8, width), F32)],
        ),
        out_shape=outs,
        compiler_params=params(16),
        name="pack",
    )(span_clip, narrow_me.astype(jnp.int32)[None], *ins)


def sum_over(block, axis):
    for bit in bits_of(lax.axis_size(axis)):
        block = block + swap(block, axis, bit)
    return block


def collect(block, axis):
    block = block[None]
    for bit in bits_of(lax.axis_size(axis)):
        block = jnp.concatenate([block, swap(block, axis, bit)], axis=0)
    return block


def turned(block, axis):
    count = lax.axis_size(axis)
    bits = bits_of(count)
    rest = block.shape[1:]
    block = block.reshape([2] * len(bits) + list(rest))
    for dim, bit in enumerate(reversed(bits)):
        block = jnp.where(my_bit(axis, bit) == 1, jnp.flip(block, dim), block)
    return block.reshape((count,) + rest)


def share(block, count):
    for bit in bits_of(count):
        groups, rows, cols = block.shape
        pair = block.reshape(groups // 2, 2, rows, cols)
        kept, got = pair[:, 0], swap(pair[:, 1], "narrow", bit)
        mine = my_bit("narrow", bit) == 1
        block = jnp.concatenate([jnp.where(mine, got, kept), jnp.where(mine, kept, got)], axis=1)
    return block


def unshare(block, count):
    for bit in reversed(bits_of(count)):
        groups, rows, cols = block.shape
        pair = block.reshape(groups, 2, rows // 2, cols)
        mine = my_bit("narrow", bit)
        kept = lax.dynamic_index_in_dim(pair, mine, 1, True)
        got = swap(lax.dynamic_index_in_dim(pair, 1 - mine, 1, True), "narrow", bit)
        block = jnp.concatenate([kept, got], axis=1).reshape(2 * groups, rows // 2, cols)
    return block


def shards(
    tokens,
    condition,
    frame_clip,
    mod_weight,
    mod_bias,
    project_weight,
    project_bias,
    merge_weight,
    merge_bias,
    up_weight,
    up_bias,
    down_weight,
    down_bias,
    out_cotangent,
):
    rows, width = tokens.shape
    wide_count, narrow_count = lax.axis_size("wide"), lax.axis_size("narrow")
    wide_me, narrow_me = lax.axis_index("wide"), lax.axis_index("narrow")
    depth = width // wide_count
    part = width // narrow_count
    units = up_weight.shape[1]
    heads = part // HEAD
    clips = condition.shape[0]
    span = math.gcd(rows, PATCHES)
    spans = rows // span
    sharing = PATCHES // span

    def twin(*blocks):
        return Sent(*[swap(block, "wide", 1) for block in blocks])

    def hop(block, axis, bit):
        return Sent(swap(block, axis, bit))

    attn = Gather(
        jnp.concatenate([project_weight.reshape(depth, 3 * part), merge_weight.T], axis=1)
    )
    up, down_shard = Gather(up_weight), down_weight.T
    attn.start()
    z_bits = bits_of(wide_count)[1:]
    narrow_bits = bits_of(narrow_count)
    active = jax.nn.silu(condition).astype(BF16)
    active_mine = lax.dynamic_slice_in_dim(active, wide_me * depth, depth, 1)
    mode_part = jnp.einsum("cd,dki->kci", active_mine, mod_weight, preferred_element_type=F32)
    unit_rows = units // part
    at = 6 * clips
    mode_part = mode_part + swap(mode_part, "wide", 1)
    for bit in z_bits:
        sent = hop(mode_part, "wide", bit)
        if bit == z_bits[0]:
            (mode_part,) = land([sent, attn], mode_part)
        else:
            mode_part, attn.own = land([sent], mode_part, attn.own)
        mode_part = mode_part + sent.got[0]
    small = jnp.concatenate(
        [
            (mode_part + mod_bias.astype(F32)[:, None]).reshape(at, part),
            project_bias.astype(F32),
            merge_bias.astype(F32)[None],
            down_bias.astype(F32)[None],
            up_bias.astype(F32).reshape(unit_rows, part),
        ],
        axis=0,
    )
    span_frame = (narrow_me * rows + jnp.arange(spans, dtype=jnp.int32) * span) // PATCHES
    span_clip = jnp.sum(
        jnp.where(
            span_frame[:, None] == jnp.arange(frame_clip.shape[0], dtype=jnp.int32)[None],
            frame_clip[None],
            0,
        ),
        axis=1,
    )
    attn.start()
    sent = Sent(*spread(small, "narrow", narrow_bits)[1:])
    small, span_clip, up.own = land([sent, attn], small, span_clip, up.own)
    while attn.in_front():
        attn.start()
        land([attn])
    attn.start()
    up.start()
    modes, out_bias, qkv_bias, up_bias_all, core_grad, down_bias_grad, core_own, core_other = unpack_call(
        span_clip, narrow_me, clips, [small, *sent.got], out_cotangent
    )
    (modes,) = land([attn, up, attn.cross("own")], modes)
    while len(up.front) - up.stage > 1:
        up.start()
        land([up])
    attn.start()
    up.start()
    modes, down_shard = land([attn, up, attn.cross("first")], modes, down_shard)
    down = Whole(down_shard)
    attn_far = attn.cross("second", "third", "fourth")
    up.start()
    modes, up.own = land([attn_far], modes, up.own)
    attn.finish()

    attn_w = Weight(attn)
    up_own = up.cross("own")
    hidden_a, qkv, merge_w = project_call(attn_w, tokens, modes, qkv_bias, part)
    qkv, hidden_a = land([up, up_own], qkv, hidden_a)
    up.start()
    up_near = up.cross("first")
    qkv_frames = share(qkv, sharing)
    attended = attend(qkv_frames, heads)
    if sharing > 1:
        attended = attended.reshape(rows * sharing, narrow_count // sharing, part)
        attended = unshare(attended.transpose(1, 0, 2), sharing)
        attended = attended.transpose(1, 0, 2).reshape(rows, width)
    attended, hidden_a = land([up, up_near], attended, hidden_a)
    up_far = up.cross("second", "third", "fourth")
    branch_a, hidden_b = merge_call(attended, merge_w, tokens, modes, out_bias[0])
    hidden_b, attended, hidden_a = land([up_far], hidden_b, attended, hidden_a)
    up.finish()
    hidden_own, hidden_other = turn(hidden_a)
    hidden_twin = twin(hidden_other)
    up_w = Weight(up)
    gelu, slope, sent_part = up_call(up_w, hidden_b, up_bias_all, core_other)

    gelu, slope, hidden_b, sent_part = land([hidden_twin], gelu, slope, hidden_b, sent_part)
    down_cross = twin(sent_part)
    hidden_b_own, hidden_b_other = turn(hidden_b)
    down_w = down.finish()
    upper_grad, up_bias_grad, sent_part = gelu_back_call(down_w, core_grad, slope, hidden_b_other)
    upper_grad, sent_part, attended, gelu, core_own = land(
        [down_cross], upper_grad, sent_part, attended, gelu, core_own
    )
    up_cross = twin(sent_part)
    down_parts = weight_grad_call([core_own], [gelu], [], [], units, down_cross.got[0])
    upper_grad, attended, *down_parts = land([up_cross], upper_grad, attended, *down_parts)
    down_scatter = Scatter(*down_parts)
    attended_twin = twin(attended)
    middle_grad, merged_grad, sums_b, merge_bias_grad = up_back_call(
        up_w, upper_grad, tokens, branch_a, modes, out_cotangent
    )
    merged_grad, upper_grad = land([attended_twin], merged_grad, upper_grad)
    merged_own, merged_other = turn(merged_grad)
    merged_twin = twin(merged_other)
    (merged_grad,) = land([], merged_grad)

    if sharing > 1:
        attended_grad = jnp.dot(merged_grad, merge_w, preferred_element_type=F32).astype(BF16)
        attended_grad = attended_grad.reshape(rows, narrow_count, part).transpose(1, 0, 2)
        attended_grad = share(attended_grad, sharing).transpose(1, 0, 2)
        attended_grad = attended_grad.reshape(rows * sharing, width // sharing)
        qkv_grad = unshare(attend_back(qkv_frames, attended_grad, heads), sharing)
    else:
        qkv_grad = attend_back(qkv_frames, merged_grad, heads, merge_w)
    qkv_grad, upper_grad = land([down_scatter, merged_twin], qkv_grad, upper_grad)
    qkv_twin = twin(qkv_grad)
    up_parts = weight_grad_call(
        [hidden_b_own],
        [upper_grad],
        [merged_own, merged_twin.got[0]],
        [attended, attended_twin.got[0]],
        units,
        up_cross.got[0],
    )
    qkv_grad, *up_parts = land([down_scatter, qkv_twin], qkv_grad, *up_parts)
    up_scatter = Scatter(*up_parts)
    tokens_grad, sums_a, qkv_sums = project_back_call(
        attn_w, qkv_grad, tokens, middle_grad, modes, 3 * part
    )
    sums_a, qkv_grad = land([down_scatter], sums_a, qkv_grad)
    attn_parts = weight_grad_call(
        [hidden_own, hidden_twin.got[0]],
        [qkv_grad, qkv_twin.got[0]],
        [],
        [],
        3 * part,
    )
    gelu, *attn_parts = land([up_scatter, down_scatter], gelu, *attn_parts)
    attn_scatter = Scatter(*attn_parts)
    output, sums_g = down_call(
        down_w, gelu, tokens, branch_a, modes, out_bias[1], out_cotangent
    )
    (sums_g,) = land([up_scatter], sums_g)

    lower, upper = pack_call(
        span_clip, narrow_me, clips, sums_a, sums_b, sums_g, merge_bias_grad, down_bias_grad,
        qkv_sums, up_bias_grad,
    )
    sent = hop(upper, "narrow", narrow_bits[-1])
    (lower,) = land([sent, attn_scatter, up_scatter], lower)
    packed = lower + sent.got[0]
    for bit in reversed(narrow_bits[:-1]):
        sent = hop(packed[bit:], "narrow", bit)
        (packed,) = land([sent], packed)
        packed = packed[:bit] + sent.got[0]
    packed = packed[0]
    sent = hop(packed, "wide", 1)
    (packed,) = land([sent], packed)
    packed = packed + sent.got[0]
    for bit in z_bits:
        sent = hop(packed, "wide", bit)
        scatters = {z_bits[0]: [attn_scatter], z_bits[-1]: [up_scatter]}
        (packed,) = land([sent, *scatters.get(bit, [])], packed)
        packed = packed + sent.got[0]
    clip_slice = packed[:at].reshape(6, clips, part)
    active_grad = jnp.einsum(
        "kci,dki->cd", clip_slice, mod_weight.astype(F32), precision=lax.Precision.HIGHEST
    )
    for bit in narrow_bits:
        sent = hop(active_grad, "narrow", bit)
        (active_grad,) = land(
            [sent, attn_scatter] if bit == narrow_bits[-1] else [sent], active_grad
        )
        active_grad = active_grad + sent.got[0]
    active_grad = active_grad[None]
    for bit in bits_of(wide_count):
        sent = hop(active_grad, "wide", bit)
        (active_grad,) = land([sent, attn_scatter] if bit == z_bits[0] else [sent], active_grad)
        active_grad = jnp.concatenate([active_grad, sent.got[0]], axis=0)
    active_grad = turned(active_grad, "wide").transpose(1, 0, 2).reshape(clips, width)
    unused, silu_pullback = jax.vjp(jax.nn.silu, condition)
    condition_grad = silu_pullback(active_grad)[0]
    mod_bias_grad = jnp.sum(clip_slice, axis=1)
    mod_weight_grad = jnp.einsum(
        "cd,kci->dki", active_mine.astype(F32), clip_slice, precision=lax.Precision.HIGHEST
    )

    for scatter in (down_scatter, up_scatter, attn_scatter):
        while scatter.stage < scatter.stages:
            land([scatter])
    return (
        output,
        tokens_grad,
        condition_grad,
        mod_weight_grad,
        mod_bias_grad,
        attn_scatter.result.reshape(depth, 3, part),
        packed[at : at + 2],
        up_scatter.result[:, units:].T,
        packed[at + 2],
        up_scatter.result[:, :units],
        packed[at + 4 :].reshape(units),
        down_scatter.result.T,
        packed[at + 3],
    )


def solution(mesh):
    both = P(("wide", "narrow"), None)
    ins = (
        both,
        P(),
        P("wide"),
        P("wide", None, "narrow"),
        P(None, "narrow"),
        P("wide", None, "narrow"),
        P(None, "narrow"),
        P("narrow", "wide"),
        P("narrow"),
        P("wide", "narrow"),
        P("narrow"),
        P("narrow", "wide"),
        P("narrow"),
        both,
    )
    outs = (
        both,
        both,
        P(),
        P("wide", None, "narrow"),
        P(None, "narrow"),
        P("wide", None, "narrow"),
        P(None, "narrow"),
        P("narrow", "wide"),
        P("narrow"),
        P("wide", "narrow"),
        P("narrow"),
        P("narrow", "wide"),
        P("narrow"),
    )
    return jax.shard_map(shards, mesh=mesh, in_specs=ins, out_specs=outs, check_vma=False)
```
